512 devices in a mesh: pp: 16 (over z), ep: 32 (over y, x, core).
Axes of the slice: x: 4, y: 4, z: 16, core: 2. Of those that a mesh axis runs over, the one named last changes fastest.
Arguments:
- state_fwd: bfloat16 [16, 768, 3584], P('pp', 'ep'), may hold values from -6 to 6
- state_bwd: bfloat16 [16, 768, 3584], P('pp', 'ep'), may hold values from -6 to 6
- enter_fwd: bfloat16 [1, 768, 3584], P(None, 'ep', 'pp'), may hold values from -6 to 6
- enter_bwd: bfloat16 [1, 768, 3584], P(None, 'ep', 'pp'), may hold values from -6 to 6
- norm_gain: float32 [16, 3584], P('pp'), may hold values from 0.1 to 1.9
- w_gate: bfloat16 [16, 3584, 4096], P('pp', None, 'ep'), may hold values from -0.09375 to 0.09375
- w_up: bfloat16 [16, 3584, 4096], P('pp', None, 'ep'), may hold values from -0.09375 to 0.09375
- w_down: bfloat16 [16, 4096, 3584], P('pp', 'ep'), may hold values from -0.1875 to 0.1875
- route_ids: int32 [16, 1, 2, 768, 2], P('pp', None, None, 'ep'), may hold values from 0 to 3, all different within a row; in each aligned block of 24 rows (0 to 23, 24 to 47, ..., all dimensions but the last counted through in order) at most 15 rows name the same one
- route_gates: float32 [16, 1, 2, 768, 2], P('pp', None, None, 'ep'), may hold values from 0.2 to 1
Outputs:
- out_fwd: bfloat16 [16, 768, 3584], P('pp', 'ep')
- out_bwd: bfloat16 [16, 768, 3584], P('pp', 'ep')
- leave_fwd: bfloat16 [1, 768, 3584], P(None, 'ep', 'pp')
- leave_bwd: bfloat16 [1, 768, 3584], P(None, 'ep', 'pp')
The draws below stay inside these ranges and needn't reach their ends.
Inputs may be any that keep to these rules, and one draw needn't show every extreme that they name: `route_ids`: each row names 2 different experts. In the rows of one device at each section, step and direction (aligned blocks of 24 rows), no expert is named by more than 15 rows, and in some blocks one expert is named by exactly 15.
All inputs are finite; a program needn't handle non-finite values.
Results may differ from the reference program's by a relative error of at most 0.009.
Values may be sent and summed in bfloat16 or wider, within the bound.
No kernel may reach another device: no remote copies, remote signals or barrier semaphores. Data moves between devices by JAX's collectives and lax.ppermute only.
A program may use at most 128 MiB of HBM per device.

```python
import math
from functools import partial
import jax
import jax.numpy as jnp
import numpy as np
from jax import lax

D = 3584
FFW = 1024
TOPK = 2
TICKS = 1
TOK_DEV = 24
EXPERTS = 4
SPLIT = 8
CAP = 15
TOKENS = 768
N_PP = 16
N_EP = 32


def block_scale(rng, shape, shards, low, largest):
    loudness, own = 1.0, jax.random.fold_in(rng, 6)
    for dim, blocks in shards:
        draws = jnp.exp(jax.random.uniform(jax.random.fold_in(own, dim), (blocks,), jnp.float32, low / len(shards), largest / len(shards)))
        loudness = loudness * jnp.repeat(draws, shape[dim] // blocks).reshape([-1 if axis == dim else 1 for axis in range(len(shape))])
    return loudness


def shared_out(own_key, own, number, rows, count, top, limit, skew):
    sequence = jax.random.permutation(own_key, count)
    heavy_load, common = portions_of(count, rows * top, limit, skew, True), portions_of(count, rows * top, limit, skew, False)
    places = jnp.arange(count)

    def named(sizes, offset_by):
        used = int((sizes > 0).sum())
        fixed = max(1, used // 4)
        shifted = fixed + (places - fixed + offset_by * (used - fixed)) % max(1, count - fixed)
        return jnp.zeros((count,), jnp.int32).at[sequence[jnp.where(places < fixed, places, shifted)]].set(jnp.asarray(sizes, jnp.int32))

    sizes = jnp.where(number % 4 == 0, named(heavy_load, number // 4), named(common, number - number // 4 - 1))
    mixed = jax.random.permutation(jax.random.fold_in(own, 3), count)
    source_of, sink = mixed[0:count // 2 * 2:2], mixed[1:count // 2 * 2:2]
    margin = jnp.minimum(sizes[source_of] - 1, limit - sizes[sink]) // 2
    margin = jnp.where((source_of == sequence[0]) | (sink == sequence[0]) | (sizes[sink] == 0), 0, jnp.maximum(margin, 0))
    shifted = jax.random.randint(jax.random.fold_in(own, 4), (count // 2,), 0, 1 << 20) % (margin + 1)
    sizes = sizes.at[source_of].add(-shifted).at[sink].add(shifted)
    labels = jnp.searchsorted(jnp.cumsum(sizes), jnp.arange(rows * top), side="right").astype(jnp.int32)
    grid = labels.reshape(top, rows).T
    grid = grid[jax.random.permutation(jax.random.fold_in(own, 1), rows)]
    offset_by = jax.random.randint(jax.random.fold_in(own, 2), (rows, 1), 0, top)
    return jnp.take_along_axis(grid, (jnp.arange(top)[None, :] + offset_by) % top, axis=1)


def portions_of(count, total, bound, slope, full):
    loads = [(1 << 20) // math.isqrt(rank ** slope) + 1 for rank in range(1, count + 1)]
    largest = bound if full else min(bound, max(-(-total // count), total * loads[0] // sum(loads)))
    least = 1 if total - largest >= count - 1 else 0
    counts, rest = [largest] + [least] * (count - 1), total - largest - least * (count - 1)
    while rest > 0:
        free = [i for i in range(1, count) if counts[i] < largest] or [i for i in range(1, count) if counts[i] < bound]
        pool, remaining = sum([loads[i] for i in free]), rest
        for i in free:
            extra = min(bound - counts[i], max(1, remaining * loads[i] // pool), rest)
            counts[i] = counts[i] + extra
            rest = rest - extra
    return np.array(counts)


def scatter_about(key, extent, scale, reach, cuts=(), held_as=jnp.bfloat16):
    result = scale * jax.random.normal(key, extent, jnp.float32)
    if cuts:
        result = result * block_scale(key, extent, cuts, -0.22, 0.18)
    return jnp.clip(result, -reach, reach).astype(held_as)


def setup_inputs(seed: int = 0) -> dict:
    key_list = jax.random.split(jax.random.key(seed), 11)
    state_fwd = scatter_about(key_list[0], (N_PP, TOKENS, D), 1.0, 6.0, ((0, 16), (1, 32)))
    state_bwd = scatter_about(key_list[1], (N_PP, TOKENS, D), 1.0, 6.0, ((0, 16), (1, 32)))
    enter_fwd = scatter_about(key_list[2], (TICKS, TOKENS, D), 1.0, 6.0, ((1, 32), (2, 16)))
    enter_bwd = scatter_about(key_list[3], (TICKS, TOKENS, D), 1.0, 6.0, ((1, 32), (2, 16)))
    norm_gain = jnp.clip(1.0 + 0.18 * jax.random.normal(key_list[4], (N_PP, D), jnp.float32), 0.1, 1.9)
    w_gate = scatter_about(key_list[5], (N_PP, D, EXPERTS * FFW), D ** -0.5, 0.09375, ((0, 16), (2, 32)))
    w_up = scatter_about(key_list[6], (N_PP, D, EXPERTS * FFW), D ** -0.5, 0.09375, ((0, 16), (2, 32)))
    w_down = scatter_about(key_list[7], (N_PP, EXPERTS * FFW, D), FFW ** -0.5, 0.1875, ((0, 16), (1, 32)))
    route_ids_keys = jax.random.split(jax.random.fold_in(key_list[8], 1), N_PP * TICKS * 2 * TOKENS // TOK_DEV)
    route_ids_turns = jax.random.permutation(jax.random.fold_in(key_list[8], 3), N_PP * TICKS * 2 * TOKENS // TOK_DEV)
    route_ids = jax.vmap(lambda own, number: shared_out(jax.random.fold_in(key_list[8], 2), own, number, TOK_DEV, EXPERTS, TOPK, CAP, 2))(route_ids_keys, route_ids_turns).reshape((N_PP, TICKS, 2, TOKENS, TOPK))
    route_gates = jnp.clip(0.2 + 0.8 * jax.random.uniform(key_list[9], (N_PP, TICKS, 2, TOKENS, TOPK), jnp.float32) ** block_scale(key_list[9], (N_PP, TICKS, 2, TOKENS, TOPK), ((0, 16), (3, 32)), -0.2, 0.2), 0.2, 1.0)
    return dict(state_fwd=state_fwd, state_bwd=state_bwd, enter_fwd=enter_fwd, enter_bwd=enter_bwd, norm_gain=norm_gain, w_gate=w_gate, w_up=w_up, w_down=w_down, route_ids=route_ids, route_gates=route_gates)


eps = 1e-06

def rms_normed(values, norm_scale):
    widened = values.astype(jnp.float32)
    inverse = lax.rsqrt(lax.optimization_barrier(jnp.mean(widened * widened, axis=-1, keepdims=True)) + eps)
    return (widened * inverse * norm_scale[None, :].astype(jnp.float32)).astype(jnp.bfloat16)

def slot_tables(expert_ids, weights, experts, capacity):
    row_count, pick_count = expert_ids.shape
    flat_ids = expert_ids.reshape(row_count * pick_count).astype(jnp.int32)
    columns = lax.broadcasted_iota(jnp.int32, (row_count * pick_count, experts), 1)
    onehot = (flat_ids[:, None] == columns).astype(jnp.int32)
    before = jnp.cumsum(onehot, axis=0) - onehot
    slot_index = lax.optimization_barrier(jnp.sum(before * onehot, axis=1))
    target = (flat_ids * capacity + slot_index).reshape(row_count, pick_count)
    places = lax.broadcasted_iota(jnp.int32, (experts * capacity, row_count, pick_count), 0)
    matched = target[None, :, :] == places
    dispatch = lax.optimization_barrier(jnp.sum(matched.astype(jnp.float32), axis=2)).astype(jnp.bfloat16)
    combine = lax.optimization_barrier(jnp.sum(jnp.where(matched, weights[None, :, :], jnp.zeros_like(weights)[None, :, :]), axis=2)).T
    return (dispatch, combine)

def section_layer(values, norm_scale, gate_stack, up_stack, down_stack, expert_ids, weights):
    normed = rms_normed(values, norm_scale)
    block_rows = normed.reshape(N_EP, TOK_DEV, D)
    block_ids = expert_ids.reshape(N_EP, TOK_DEV, TOPK)
    block_weights = weights.reshape(N_EP, TOK_DEV, TOPK)
    dispatch, combine = jax.vmap(partial(slot_tables, experts=EXPERTS, capacity=CAP))(block_ids, block_weights)
    outgoing = jnp.einsum('bst,btd->bsd', dispatch.astype(jnp.float32), block_rows.astype(jnp.float32)).astype(jnp.bfloat16)
    by_expert = outgoing.reshape(N_EP, EXPERTS, CAP, D).transpose(1, 0, 2, 3).reshape(EXPERTS, N_EP * CAP, D)
    gate_all = gate_stack.reshape(D, EXPERTS, FFW).transpose(1, 0, 2)
    up_all = up_stack.reshape(D, EXPERTS, FFW).transpose(1, 0, 2)
    gate_act = jnp.einsum('erd,edf->erf', by_expert.astype(jnp.float32), gate_all.astype(jnp.float32))
    up_act = jnp.einsum('erd,edf->erf', by_expert.astype(jnp.float32), up_all.astype(jnp.float32))
    hidden = (jax.nn.silu(gate_act) * up_act).astype(jnp.bfloat16)
    hidden_parts = hidden.reshape(EXPERTS, N_EP * CAP, SPLIT, FFW // SPLIT)
    down_parts = down_stack.reshape(EXPERTS, SPLIT, FFW // SPLIT, D)
    partial_out = jnp.einsum('erpf,epfd->perd', hidden_parts.astype(jnp.float32), down_parts.astype(jnp.float32)).astype(jnp.bfloat16)
    produced = lax.optimization_barrier(jnp.sum(partial_out.astype(jnp.float32), axis=0))
    returned = produced.reshape(EXPERTS, N_EP, CAP, D).transpose(1, 0, 2, 3).reshape(N_EP, EXPERTS * CAP, D)
    mixture = jnp.einsum('bts,bsd->btd', combine, returned, precision=lax.Precision.HIGHEST)
    return (values.astype(jnp.float32) + mixture.reshape(N_EP * TOK_DEV, D)).astype(jnp.bfloat16)

def reference(state_fwd, state_bwd, enter_fwd, enter_bwd, norm_gain, w_gate, w_up, w_down, route_ids, route_gates):
    fwd_states = [state_fwd[section_index] for section_index in range(N_PP)]
    bwd_states = [state_bwd[section_index] for section_index in range(N_PP)]
    leaving_fwd = []
    leaving_bwd = []
    for tick_index in range(TICKS):
        fwd_done = [section_layer(fwd_states[section_index], norm_gain[section_index], w_gate[section_index], w_up[section_index], w_down[section_index], route_ids[section_index, tick_index, 0], route_gates[section_index, tick_index, 0]) for section_index in range(N_PP)]
        bwd_done = [section_layer(bwd_states[section_index], norm_gain[section_index], w_gate[section_index], w_up[section_index], w_down[section_index], route_ids[section_index, tick_index, 1], route_gates[section_index, tick_index, 1]) for section_index in range(N_PP)]
        leaving_fwd.append(fwd_done[N_PP - 1])
        leaving_bwd.append(bwd_done[0])
        fwd_states = [enter_fwd[tick_index]] + fwd_done[:N_PP - 1]
        bwd_states = bwd_done[1:] + [enter_bwd[tick_index]]
    return (jnp.stack(fwd_states), jnp.stack(bwd_states), jnp.stack(leaving_fwd), jnp.stack(leaving_bwd))
```

```python
import jax
import jax.numpy as jnp
from jax import lax
from jax.experimental import pallas as pl
from jax.experimental.pallas import tpu as pltpu
from jax.sharding import PartitionSpec as P

EPS = 1e-06
BF = jnp.bfloat16
F32 = jnp.float32
EXPERTS = 4
COLS = 4
CAP = 15
ROWS = 24
BOTH = 2 * ROWS
SLOTS = 2 * CAP
EXTRA = 128
WIDE = 512


def device(y, x, core):
    return (y * COLS + x) * 2 + core


Y_FIRST = [[device(y, x, 0) for y in range(EXPERTS)] for x in range(COLS)] + [
    [device(y, x, 1) for x in range(COLS)] for y in range(EXPERTS)
]
X_FIRST = [[device(y, x, 0) for x in range(COLS)] for y in range(EXPERTS)] + [
    [device(y, x, 1) for y in range(EXPERTS)] for x in range(COLS)
]


def exchange(rows, groups):
    return lax.all_to_all(
        rows, "ep", split_axis=0, concat_axis=0, axis_index_groups=groups, tiled=True
    )


def iota(shape, dim):
    return lax.broadcasted_iota(jnp.int32, shape, dim)


def dot(a, b):
    return jnp.dot(a, b, preferred_element_type=F32)


def split_gate(gate):
    high = gate.astype(BF).astype(F32)
    return high, (gate - high).astype(BF).astype(F32)


def send_kernel(core_ref, fwd_ref, bwd_ref, gain_ref, ids_ref, gates_ref, out_ref, meta_ref):
    ids = ids_ref[...]
    gates = gates_ref[...]
    lanes = iota((BOTH, EXTRA), 1)
    row = iota((BOTH, EXTRA), 0)
    first, second = ids[:, 0:1], ids[:, 1:2]
    named = jnp.where((lanes == first) | (lanes == second), 1.0, 0.0)
    r0, r1 = iota((BOTH, BOTH), 0), iota((BOTH, BOTH), 1)
    earlier = jnp.where((r1 < r0) & ((r1 < ROWS) == (r0 < ROWS)), 1.0, 0.0)
    rank = dot(earlier.astype(BF), named.astype(BF))
    offset = jnp.where(row[:, 0:1] < ROWS, 0, CAP)
    slots = []
    for chosen in (first, second):
        taken = jnp.sum(jnp.where(lanes == chosen, rank, 0.0), axis=1, keepdims=True)
        slots.append(taken.astype(jnp.int32) + offset)
    fields = [first.astype(F32), slots[0].astype(F32), second.astype(F32), slots[1].astype(F32)]
    fields += split_gate(gates[:, 0:1])
    fields += split_gate(gates[:, 1:2])
    meta = jnp.zeros((BOTH, EXTRA), F32)
    for place, field in enumerate(fields):
        meta = jnp.where(lanes == place, field, meta)
    meta_ref[...] = meta

    def as_row(column):
        return jnp.sum(jnp.where(r0 == r1, column, 0), axis=0, keepdims=True)

    target = iota((EXPERTS * BOTH, BOTH), 0)
    source = iota((EXPERTS * BOTH, BOTH), 1)
    routed = (target == as_row(first * BOTH + slots[0])) | (
        target == as_row(second * BOTH + slots[1])
    )
    copied = target == source
    for part in range(1, COLS):
        copied = copied | (target == source + part * BOTH)
    routed_f = jnp.where(routed, 1.0, 0.0)
    copied_f = jnp.where(copied, 1.0, 0.0)
    pick = jnp.where(core_ref[0] == 0, routed_f, copied_f).astype(BF)
    values = jnp.concatenate([fwd_ref[...].astype(F32), bwd_ref[...].astype(F32)], axis=0)
    features = values.shape[1]
    inverse = lax.rsqrt(jnp.mean(values * values, axis=-1, keepdims=True) + EPS)
    normed = (values * inverse * gain_ref[...]).astype(BF)
    for start in range(0, features, WIDE):
        out_ref[:, start : start + WIDE] = dot(pick, normed[:, start : start + WIDE]).astype(BF)
    out_ref[:, features:] = dot(pick, meta.astype(BF)).astype(BF)


def spread_kernel(core_ref, rows_ref, extra_ref, out_ref, high_ref, low_ref, pick_ref):
    total = EXPERTS * BOTH
    slots = EXPERTS * COLS * SLOTS

    @pl.when(pl.program_id(0) == 0)
    def _():
        extra = extra_ref[...].astype(F32)
        row = iota((total, 1), 0)
        part = (
            (row >= BOTH).astype(jnp.int32)
            + (row >= 2 * BOTH).astype(jnp.int32)
            + (row >= 3 * BOTH).astype(jnp.int32)
        )
        place = row - part * BOTH
        on_first = core_ref[0] == 0
        none = jnp.full((total, 1), -1, jnp.int32)
        packed = jnp.where(place < SLOTS, part * SLOTS + place, -slots)
        block = COLS * SLOTS
        targets, highs, lows = [], [], []
        for k in range(COLS):
            if k < 2:
                expert = extra[:, 2 * k : 2 * k + 1].astype(jnp.int32)
                slot = extra[:, 2 * k + 1 : 2 * k + 2].astype(jnp.int32)
                there = expert * block + part * SLOTS + slot
                high = extra[:, 4 + 2 * k : 5 + 2 * k]
                low = extra[:, 5 + 2 * k : 6 + 2 * k]
            else:
                there, high, low = none, jnp.zeros((total, 1), F32), jnp.zeros((total, 1), F32)
            targets.append(jnp.where(on_first, packed + k * block, there))
            highs.append(jnp.where(on_first, 1.0, high))
            lows.append(jnp.where(on_first, 0.0, low))
        column = iota((total, slots), 1)
        pick = jnp.zeros((total, slots), F32)
        high_m = jnp.zeros((total, slots), F32)
        low_m = jnp.zeros((total, slots), F32)
        for target, high, low in zip(targets, highs, lows):
            here = column == target
            pick = jnp.where(here, 1.0, pick)
            high_m = jnp.where(here, high, high_m)
            low_m = jnp.where(here, low, low_m)
        high_ref[...] = high_m.astype(BF)
        low_ref[...] = low_m.astype(BF)
        pick_ref[...] = pick.T.astype(BF)

    out_ref[...] = dot(pick_ref[...], rows_ref[...]).astype(BF)


def expert_kernel(
    steps, rows_ref, g0_ref, g1_ref, u0_ref, u1_ref, d0_ref, d1_ref, out_ref, gate_acc, up_acc, hid_ref
):
    step = pl.program_id(0)
    half = g0_ref.shape[1]

    @pl.when(step == 0)
    def _():
        gate_acc[...] = jnp.zeros_like(gate_acc)
        up_acc[...] = jnp.zeros_like(up_acc)

    @pl.when(step < steps)
    def _():
        rows = rows_ref[...]
        gate_acc[...] += dot(rows, jnp.concatenate([g0_ref[...], g1_ref[...]], axis=1))
        up_acc[...] += dot(rows, jnp.concatenate([u0_ref[...], u1_ref[...]], axis=1))

    @pl.when(step == steps - 1)
    def _():
        gate = gate_acc[...]
        hid_ref[...] = (gate / (1.0 + jnp.exp(-gate)) * up_acc[...]).astype(BF)

    @pl.when(step >= steps)
    def _():
        hidden = hid_ref[...]
        down = jnp.concatenate([d0_ref[...], d1_ref[...]], axis=0)
        out_ref[...] = dot(hidden, down).astype(BF)


def gather_kernel(high_ref, low_ref, rows_ref, out_ref):
    rows = rows_ref[...]
    out_ref[...] = (dot(high_ref[...], rows) + dot(low_ref[...], rows)).astype(BF)


def finish_kernel(core_ref, meta_ref, rows_ref, fwd_ref, bwd_ref, of_ref, ob_ref, high_ref, low_ref):
    @pl.when(pl.program_id(0) == 0)
    def _():
        meta = meta_ref[...]
        total = EXPERTS * BOTH
        column = iota((BOTH, total), 1)
        row = iota((BOTH, total), 0)
        high = jnp.zeros((BOTH, total), F32)
        low = jnp.zeros((BOTH, total), F32)
        for k in range(2):
            there = (meta[:, 2 * k : 2 * k + 1] * BOTH + meta[:, 2 * k + 1 : 2 * k + 2]).astype(
                jnp.int32
            )
            high = jnp.where(column == there, meta[:, 4 + 2 * k : 5 + 2 * k], high)
            low = jnp.where(column == there, meta[:, 5 + 2 * k : 6 + 2 * k], low)
        same = column == row
        for part in range(1, COLS):
            same = same | (column == row + part * BOTH)
        ones = jnp.where(same, 1.0, 0.0)
        on_first = core_ref[0] == 0
        high_ref[...] = jnp.where(on_first, high, ones).astype(BF)
        low_ref[...] = jnp.where(on_first, low, 0.0).astype(BF)

    rows = rows_ref[...]
    mixture = dot(high_ref[...], rows) + dot(low_ref[...], rows)
    of_ref[...] = (fwd_ref[...].astype(F32) + mixture[:ROWS]).astype(BF)
    ob_ref[...] = (bwd_ref[...].astype(F32) + mixture[ROWS:]).astype(BF)


SMEM = pl.BlockSpec(memory_space=pltpu.SMEM)
PARAMS = pltpu.CompilerParams(vmem_limit_bytes=48 * 1024 * 1024)


def whole(shape):
    return pl.BlockSpec(shape, lambda i: (0,) * len(shape))


def tile(rows, width=WIDE):
    return pl.BlockSpec((rows, width), lambda i: (0, i))


def shape(rows, columns, dtype=BF):
    return jax.ShapeDtypeStruct((rows, columns), dtype)


def make_send(core, fwd, bwd, gain, ids, gates):
    features = fwd.shape[1]
    vmem = pl.BlockSpec(memory_space=pltpu.VMEM)
    return pl.pallas_call(
        send_kernel,
        out_shape=(shape(EXPERTS * BOTH, features + EXTRA), shape(BOTH, EXTRA, F32)),
        in_specs=[SMEM] + [vmem] * 5,
        out_specs=(vmem, vmem),
        compiler_params=PARAMS,
        name="normed",
    )(core, fwd, bwd, gain, ids, gates)


def make_spread(core, rows):
    total = rows.shape[0]
    features = rows.shape[1] - EXTRA
    slots = EXPERTS * COLS * SLOTS
    return pl.pallas_call(
        spread_kernel,
        grid=(features // WIDE,),
        out_shape=(shape(slots, features), shape(total, slots), shape(total, slots)),
        in_specs=[
            SMEM,
            tile(total),
            pl.BlockSpec((total, EXTRA), lambda i: (0, features // EXTRA)),
        ],
        out_specs=(tile(slots), whole((total, slots)), whole((total, slots))),
        scratch_shapes=[pltpu.VMEM((slots, total), BF)],
        compiler_params=PARAMS,
        name="spread",
    )(core, rows, rows)


def run_experts(rows, gates, ups, downs):
    count, features = rows.shape
    width = gates[0].shape[1]
    steps = features // WIDE
    first = lambda i: jnp.minimum(i, steps - 1)
    later = lambda i: jnp.maximum(i - steps, 0)
    tall = pl.BlockSpec((WIDE, width), lambda i: (first(i), 0))
    flat = pl.BlockSpec((width, WIDE), lambda i: (0, later(i)))

    def body(*refs):
        expert_kernel(steps, *refs)

    return pl.pallas_call(
        body,
        grid=(2 * steps,),
        out_shape=shape(count, features),
        in_specs=[pl.BlockSpec((count, WIDE), lambda i: (0, first(i)))] + [tall] * 4 + [flat] * 2,
        out_specs=pl.BlockSpec((count, WIDE), lambda i: (0, later(i))),
        scratch_shapes=[
            pltpu.VMEM((count, 2 * width), F32),
            pltpu.VMEM((count, 2 * width), F32),
            pltpu.VMEM((count, 2 * width), BF),
        ],
        compiler_params=PARAMS,
        name="experts",
    )(rows, gates[0], gates[1], ups[0], ups[1], downs[0], downs[1])


def make_gather(high, low, rows):
    slots, features = rows.shape
    total = high.shape[0]
    return pl.pallas_call(
        gather_kernel,
        grid=(features // WIDE,),
        out_shape=shape(total, features),
        in_specs=[whole((total, slots)), whole((total, slots)), tile(slots)],
        out_specs=tile(total),
        compiler_params=PARAMS,
        name="gather",
    )(high, low, rows)


def make_finish(core, meta, rows, fwd, bwd):
    total, features = rows.shape
    return pl.pallas_call(
        finish_kernel,
        grid=(features // WIDE,),
        out_shape=(shape(ROWS, features), shape(ROWS, features)),
        in_specs=[SMEM, whole((BOTH, EXTRA)), tile(total), tile(ROWS), tile(ROWS)],
        out_specs=(tile(ROWS), tile(ROWS)),
        scratch_shapes=[pltpu.VMEM((BOTH, total), BF), pltpu.VMEM((BOTH, total), BF)],
        compiler_params=PARAMS,
        name="finish",
    )(core, meta, rows, fwd, bwd)


def shifted(block, distance, count):
    route = [(i, i + distance) for i in range(count) if 0 <= i + distance < count]
    return lax.ppermute(block, "pp", route)


def from_other_core(block):
    return lax.ppermute(block, "ep", [(i, i ^ 1) for i in range(lax.axis_size("ep"))])


def across_sections(blocks):
    return lax.all_to_all(blocks, "pp", split_axis=0, concat_axis=0, tiled=True)


def body(
    state_fwd,
    state_bwd,
    enter_fwd,
    enter_bwd,
    norm_gain,
    w_gate,
    w_up,
    w_down,
    route_ids,
    route_gates,
):
    sections = lax.axis_size("pp")
    section = lax.axis_index("pp")
    core = (lax.axis_index("ep") % 2).astype(jnp.int32).reshape(1)
    fwd, bwd = state_fwd[0], state_bwd[0]
    features = fwd.shape[1]
    part = features // sections
    ids = route_ids[0, 0].reshape(BOTH, 2)
    gates = route_gates[0, 0].reshape(BOTH, 2)

    own = (w_gate[0], w_up[0], w_down[0])
    others = tuple(from_other_core(w) for w in own)

    target = lax.broadcasted_iota(jnp.int32, (sections, 1, 1), 0)
    entering = jnp.where(target == sections - 1, enter_bwd, enter_fwd)
    entered = across_sections(entering).transpose(1, 0, 2).reshape(ROWS, features)

    send, meta = make_send(core, fwd, bwd, norm_gain, ids, gates)
    spread, high, low = make_spread(core, exchange(send, Y_FIRST))
    done = run_experts(exchange(spread, X_FIRST), *zip(own, others))
    gathered = make_gather(high, low, exchange(done, X_FIRST))
    fwd_out, bwd_out = make_finish(core, meta, exchange(gathered, Y_FIRST), fwd, bwd)

    fwd_next = jnp.where(section == 0, entered, shifted(fwd_out, 1, sections))
    bwd_next = jnp.where(section == sections - 1, entered, shifted(bwd_out, -1, sections))
    leaving = jnp.where(section == 0, bwd_out, fwd_out)
    left = across_sections(leaving.reshape(ROWS, sections, part).transpose(1, 0, 2))
    return (fwd_next[None], bwd_next[None], left[sections - 1 :], left[:1])


def solution(mesh):
    placed = (
        P("pp", "ep", None),
        P("pp", "ep", None),
        P(None, "ep", "pp"),
        P(None, "ep", "pp"),
        P("pp", None),
        P("pp", None, "ep"),
        P("pp", None, "ep"),
        P("pp", "ep", None),
        P("pp", None, None, "ep", None),
        P("pp", None, None, "ep", None),
    )
    return jax.shard_map(
        body,
        mesh=mesh,
        in_specs=placed,
        out_specs=(
            P("pp", "ep", None),
            P("pp", "ep", None),
            P(None, "ep", "pp"),
            P(None, "ep", "pp"),
        ),
        check_vma=False,
    )
```

```python
import jax
import jax.numpy as jnp
from jax import lax
from jax.experimental import pallas as pl
from jax.experimental.pallas import tpu as pltpu
from jax.sharding import PartitionSpec as P

EPS = 1e-06
BF = jnp.bfloat16
F32 = jnp.float32
EXPERTS = 4
COLS = 4
CAP = 15
ROWS = 24
BOTH = 2 * ROWS
SLOTS = 2 * CAP
EXTRA = 128
WIDE = 1792
CARRIED = 1536
CHUNK = 512
LANES = 128


def device(y, x, core):
    return (y * COLS + x) * 2 + core


def hop(block, distance, y_first):
    route = []
    for y in range(EXPERTS):
        for x in range(COLS):
            for core in range(2):
                along_y = (core == 0) == y_first
                there = ((y + distance) % EXPERTS, x) if along_y else (y, (x + distance) % COLS)
                route.append((device(y, x, core), device(*there, core)))
    return lax.ppermute(block, "ep", route)


def iota(shape, dim):
    return lax.broadcasted_iota(jnp.int32, shape, dim)


def dot(a, b):
    return jnp.dot(a, b, preferred_element_type=F32)


def split_gate(gate):
    high = gate.astype(BF).astype(F32)
    return high, (gate - high).astype(BF).astype(F32)


def send_kernel(place_ref, fwd_ref, bwd_ref, gain_ref, ids_ref, gates_ref, *outs):
    meta_ref = outs[-1]
    lanes = iota((BOTH, EXTRA), 1)
    row = iota((BOTH, EXTRA), 0)
    in_fwd = row < ROWS
    own = lanes[:, :ROWS] == row[:, :ROWS] - jnp.where(in_fwd[:, :ROWS], 0, ROWS)

    def column(ref, k):
        both = jnp.where(in_fwd[:, :ROWS], ref[0, k : k + 1, :], ref[1, k : k + 1, :])
        return jnp.sum(jnp.where(own, both, jnp.zeros_like(both)), axis=1, keepdims=True)

    first, second = [
        jnp.bitwise_and(column(ids_ref, k) - place_ref[1] + EXPERTS, EXPERTS - 1) for k in range(2)
    ]
    named = jnp.where((lanes == first) | (lanes == second), 1.0, 0.0)
    r0, r1 = iota((BOTH, BOTH), 0), iota((BOTH, BOTH), 1)
    earlier = jnp.where((r1 < r0) & ((r1 < ROWS) == (r0 < ROWS)), 1.0, 0.0)
    rank = dot(earlier.astype(BF), named.astype(BF))
    offset = jnp.where(in_fwd[:, 0:1], 0, CAP)
    slots = []
    for chosen in (first, second):
        taken = jnp.sum(jnp.where(lanes == chosen, rank, 0.0), axis=1, keepdims=True)
        slots.append(taken.astype(jnp.int32) + offset)
    fields = [first.astype(F32), slots[0].astype(F32), second.astype(F32), slots[1].astype(F32)]
    fields += split_gate(column(gates_ref, 0))
    fields += split_gate(column(gates_ref, 1))
    meta = jnp.zeros((BOTH, EXTRA), F32)
    for place, field in enumerate(fields):
        meta = jnp.where(lanes == place, field, meta)
    meta_ref[...] = meta

    def as_row(column):
        return jnp.sum(jnp.where(r0 == r1, column, 0), axis=0, keepdims=True)

    target = iota((EXPERTS * BOTH, BOTH), 0)
    source = iota((EXPERTS * BOTH, BOTH), 1)
    routed = (target == as_row(first * BOTH + slots[0])) | (
        target == as_row(second * BOTH + slots[1])
    )
    copied = target == source
    for part in range(1, COLS):
        copied = copied | (target == source + part * BOTH)
    routed_f = jnp.where(routed, 1.0, 0.0)
    copied_f = jnp.where(copied, 1.0, 0.0)
    pick = jnp.where(place_ref[0] == 0, routed_f, copied_f).astype(BF)
    values = jnp.concatenate([fwd_ref[...].astype(F32), bwd_ref[...].astype(F32)], axis=0)
    features = values.shape[1]
    inverse = lax.rsqrt(jnp.mean(values * values, axis=-1, keepdims=True) + EPS)
    normed = (values * inverse * gain_ref[...]).astype(BF)
    for start in range(0, features, CHUNK):
        picked = dot(pick, normed[:, start : start + CHUNK]).astype(BF)
        for part in range(EXPERTS):
            outs[part][:, start : start + CHUNK] = picked[part * BOTH : (part + 1) * BOTH]
    extra = dot(pick, meta.astype(BF)).astype(BF)
    for part in range(EXPERTS):
        outs[part][:, features:] = extra[part * BOTH : (part + 1) * BOTH]


def spread_kernel(place_ref, *refs):
    rows_refs, extra_refs, out_refs = refs[:4], refs[4:8], refs[8:12]
    high_ref, low_ref, pick_ref = refs[12:]
    total = EXPERTS * BOTH
    lanes = EXPERTS * LANES

    @pl.when(pl.program_id(0) == 0)
    def _():
        extra = jnp.concatenate([ref[...].astype(F32) for ref in extra_refs], axis=0)
        row = iota((total, 1), 0)
        part = (
            (row >= BOTH).astype(jnp.int32)
            + (row >= 2 * BOTH).astype(jnp.int32)
            + (row >= 3 * BOTH).astype(jnp.int32)
        )
        place = row - part * BOTH
        on_first = place_ref[0] == 0
        packed = jnp.where(place < SLOTS, part * SLOTS + place, -lanes)
        column = iota((total, lanes), 1)
        pick = jnp.zeros((total, lanes), F32)
        high_m = jnp.zeros((total, lanes), F32)
        low_m = jnp.zeros((total, lanes), F32)
        for k in range(COLS):
            there, high, low = -1, 0.0, 0.0
            if k < 2:
                expert = extra[:, 2 * k : 2 * k + 1].astype(jnp.int32)
                slot = extra[:, 2 * k + 1 : 2 * k + 2].astype(jnp.int32)
                there = expert * LANES + part * SLOTS + slot
                high = extra[:, 4 + 2 * k : 5 + 2 * k]
                low = extra[:, 5 + 2 * k : 6 + 2 * k]
            here = column == jnp.where(on_first, packed + k * LANES, there)
            pick = jnp.where(here, 1.0, pick)
            high_m = jnp.where(here, jnp.where(on_first, 1.0, high), high_m)
            low_m = jnp.where(here, jnp.where(on_first, 0.0, low), low_m)
        high_ref[...] = high_m.astype(BF)
        low_ref[...] = low_m.astype(BF)
        pick_ref[...] = pick.T.astype(BF)

    width = rows_refs[0].shape[1]
    for start in range(0, width, CHUNK):
        cut = slice(start, min(start + CHUNK, width))
        rows = jnp.concatenate([ref[:, cut] for ref in rows_refs], axis=0)
        for part, out_ref in enumerate(out_refs):
            moved = dot(pick_ref[part * LANES : (part + 1) * LANES, :], rows)
            out_ref[:, cut] = moved[: COLS * SLOTS].astype(BF)


def expert_kernel(steps, count, *refs):
    rows_refs = refs[:count]
    g0_ref, g1_ref, u0_ref, u1_ref, d0_ref, d1_ref = refs[count : count + 6]
    out_refs = refs[count + 6 : 2 * count + 6]
    gate_acc, up_acc, hid_ref = refs[2 * count + 6 :]
    step = pl.program_id(0)

    @pl.when(step < steps)
    def _():
        gate_w = jnp.concatenate([g0_ref[...], g1_ref[...]], axis=1)
        up_w = jnp.concatenate([u0_ref[...], u1_ref[...]], axis=1)
        for i, rows_ref in enumerate(rows_refs):
            gate = dot(rows_ref[...], gate_w)
            up = dot(rows_ref[...], up_w)

            @pl.when(step == 0)
            def _():
                gate_acc[i] = gate
                up_acc[i] = up

            @pl.when(step > 0)
            def _():
                gate_acc[i] += gate
                up_acc[i] += up

    @pl.when(step == steps - 1)
    def _():
        gate = gate_acc[...]
        hid_ref[...] = (gate / (1.0 + jnp.exp(-gate)) * up_acc[...]).astype(BF)

    @pl.when(step >= steps)
    def _():
        down = jnp.concatenate([d0_ref[...], d1_ref[...]], axis=0)
        for i, out_ref in enumerate(out_refs):
            out_ref[...] = dot(hid_ref[i], down).astype(BF)


def gather_kernel(high_ref, low_ref, *refs):
    rows_refs, out_refs = refs[:4], refs[4:]
    width = rows_refs[0].shape[1]
    used = COLS * SLOTS
    for start in range(0, width, CHUNK):
        cut = slice(start, min(start + CHUNK, width))
        total = 0.0
        for part, ref in enumerate(rows_refs):
            lanes = slice(part * LANES, part * LANES + used)
            rows = ref[:, cut]
            total += dot(high_ref[:, lanes], rows) + dot(low_ref[:, lanes], rows)
        total = total.astype(BF)
        for part, out_ref in enumerate(out_refs):
            out_ref[:, cut] = total[part * BOTH : (part + 1) * BOTH]


def finish_kernel(place_ref, meta_ref, *refs):
    rows_refs = refs[:4]
    fwd_ref, bwd_ref, of_ref, ob_ref, high_ref, low_ref = refs[4:]

    @pl.when(pl.program_id(0) == 0)
    def _():
        meta = meta_ref[...]
        total = EXPERTS * BOTH
        column = iota((BOTH, total), 1)
        row = iota((BOTH, total), 0)
        high = jnp.zeros((BOTH, total), F32)
        low = jnp.zeros((BOTH, total), F32)
        for k in range(2):
            there = (meta[:, 2 * k : 2 * k + 1] * BOTH + meta[:, 2 * k + 1 : 2 * k + 2]).astype(
                jnp.int32
            )
            high = jnp.where(column == there, meta[:, 4 + 2 * k : 5 + 2 * k], high)
            low = jnp.where(column == there, meta[:, 5 + 2 * k : 6 + 2 * k], low)
        same = column == row
        for part in range(1, COLS):
            same = same | (column == row + part * BOTH)
        ones = jnp.where(same, 1.0, 0.0)
        on_first = place_ref[0] == 0
        high_ref[...] = jnp.where(on_first, high, ones).astype(BF)
        low_ref[...] = jnp.where(on_first, low, 0.0).astype(BF)

    width = fwd_ref.shape[1]
    for start in range(0, width, CHUNK):
        cut = slice(start, min(start + CHUNK, width))
        rows = jnp.concatenate([ref[:, cut] for ref in rows_refs], axis=0)
        mixture = dot(high_ref[...], rows) + dot(low_ref[...], rows)
        of_ref[:, cut] = (fwd_ref[:, cut].astype(F32) + mixture[:ROWS]).astype(BF)
        ob_ref[:, cut] = (bwd_ref[:, cut].astype(F32) + mixture[ROWS:]).astype(BF)


SMEM = pl.BlockSpec(memory_space=pltpu.SMEM)
PARAMS = pltpu.CompilerParams(vmem_limit_bytes=24 * 1024 * 1024)


def whole(shape):
    return pl.BlockSpec(shape, lambda i: (0,) * len(shape))


def tile(rows, width=WIDE):
    return pl.BlockSpec((rows, width), lambda i: (0, i))


def shape(rows, columns, dtype=BF):
    return jax.ShapeDtypeStruct((rows, columns), dtype)


def make_send(place, fwd, bwd, gain, ids, gates):
    features = fwd.shape[1]
    vmem = pl.BlockSpec(memory_space=pltpu.VMEM)
    *blocks, meta = pl.pallas_call(
        send_kernel,
        out_shape=(shape(BOTH, features + EXTRA),) * 4 + (shape(BOTH, EXTRA, F32),),
        in_specs=[SMEM] + [vmem] * 5,
        out_specs=(vmem,) * 5,
        compiler_params=PARAMS,
        name="normed",
    )(place, fwd, bwd, gain, ids, gates)
    return blocks, meta


def make_spread(place, blocks):
    features = blocks[0].shape[1] - EXTRA
    total = EXPERTS * BOTH
    lanes = EXPERTS * LANES
    extra = pl.BlockSpec((BOTH, EXTRA), lambda i: (0, features // EXTRA))
    *blocks, high, low = pl.pallas_call(
        spread_kernel,
        grid=(features // WIDE,),
        out_shape=(shape(COLS * SLOTS, features),) * 4 + (shape(total, lanes),) * 2,
        in_specs=[SMEM] + [tile(BOTH)] * 4 + [extra] * 4,
        out_specs=(tile(COLS * SLOTS),) * 4 + (whole((total, lanes)),) * 2,
        scratch_shapes=[pltpu.VMEM((lanes, total), BF)],
        compiler_params=PARAMS,
        name="spread",
    )(place, *blocks, *blocks)
    return blocks, high, low


def run_experts(blocks, gates, ups, downs):
    count = len(blocks)
    rows, features = blocks[0].shape
    width = gates[0].shape[1]
    steps = features // WIDE
    first = lambda i: jnp.minimum(i, steps - 1)
    later = lambda i: jnp.maximum(i - steps, 0)
    tall = pl.BlockSpec((WIDE, width), lambda i: (first(i), 0))
    flat = pl.BlockSpec((width, WIDE), lambda i: (0, later(i)))

    def body(*refs):
        expert_kernel(steps, count, *refs)

    return pl.pallas_call(
        body,
        grid=(2 * steps,),
        out_shape=(shape(rows, features),) * count,
        in_specs=[pl.BlockSpec((rows, WIDE), lambda i: (0, first(i)))] * count
        + [tall] * 4
        + [flat] * 2,
        out_specs=(pl.BlockSpec((rows, WIDE), lambda i: (0, later(i))),) * count,
        scratch_shapes=[
            pltpu.VMEM((count, rows, 2 * width), F32),
            pltpu.VMEM((count, rows, 2 * width), F32),
            pltpu.VMEM((count, rows, 2 * width), BF),
        ],
        compiler_params=PARAMS,
        name="experts",
    )(*blocks, gates[0], gates[1], ups[0], ups[1], downs[0], downs[1])


def make_gather(high, low, blocks):
    rows, features = blocks[0].shape
    return pl.pallas_call(
        gather_kernel,
        grid=(features // WIDE,),
        out_shape=(shape(BOTH, features),) * 4,
        in_specs=[whole(high.shape), whole(low.shape)] + [tile(rows)] * 4,
        out_specs=(tile(BOTH),) * 4,
        compiler_params=PARAMS,
        name="gather",
    )(high, low, *blocks)


def make_finish(place, meta, blocks, fwd, bwd):
    features = fwd.shape[1]
    total = EXPERTS * BOTH
    return pl.pallas_call(
        finish_kernel,
        grid=(features // WIDE,),
        out_shape=(shape(ROWS, features), shape(ROWS, features)),
        in_specs=[SMEM, whole((BOTH, EXTRA))] + [tile(BOTH)] * 4 + [tile(ROWS), tile(ROWS)],
        out_specs=(tile(ROWS), tile(ROWS)),
        scratch_shapes=[pltpu.VMEM((BOTH, total), BF), pltpu.VMEM((BOTH, total), BF)],
        compiler_params=PARAMS,
        name="finish",
    )(place, meta, *blocks, fwd, bwd)


def shifted(block, distance, count):
    route = [(i, i + distance) for i in range(count) if 0 <= i + distance < count]
    return lax.ppermute(block, "pp", route)


def from_other_core(block):
    return lax.ppermute(block, "ep", [(i, i ^ 1) for i in range(lax.axis_size("ep"))])


def across_sections(blocks):
    return lax.all_to_all(blocks, "pp", split_axis=0, concat_axis=0, tiled=True)


def body(
    state_fwd,
    state_bwd,
    enter_fwd,
    enter_bwd,
    norm_gain,
    w_gate,
    w_up,
    w_down,
    route_ids,
    route_gates,
):
    sections = lax.axis_size("pp")
    section = lax.axis_index("pp")
    position = lax.axis_index("ep")
    place = jnp.stack([position % 2, position // (2 * COLS)]).astype(jnp.int32)
    fwd, bwd = state_fwd[0], state_bwd[0]
    features = fwd.shape[1]
    part = features // sections
    ids = route_ids[0, 0].transpose(0, 2, 1)
    gates = route_gates[0, 0].transpose(0, 2, 1)

    sent, meta = make_send(place, fwd, bwd, norm_gain, ids, gates)
    around = [hop(sent[d], d, True) for d in (1, 3, 2)]

    own = (w_gate[0], w_up[0], w_down[0])
    passed, entering, _ = lax.optimization_barrier((own, (enter_fwd[0], enter_bwd[0]), meta))
    weights = tuple(zip(own, (from_other_core(w) for w in passed)))
    both = jnp.concatenate(entering, axis=1)
    entered = lax.all_gather(
        jnp.pad(both, ((0, 0), (0, CARRIED - both.shape[1]))), "pp", axis=0, tiled=True
    )

    def joined(start):
        blocks = entered[:, start : start + part].reshape(sections, ROWS, part)
        return blocks.transpose(1, 0, 2).reshape(ROWS, features)

    spread, high, low = make_spread(place, [sent[0], around[0], around[2], around[1]])
    near, far, last = [hop(spread[d], d, False) for d in (1, 3, 2)]
    (done0,) = run_experts([spread[0]], *weights)
    near, far, done0 = lax.optimization_barrier((near, far, done0))
    done1, done3 = run_experts([near, far], *weights)
    last, done1, done3 = lax.optimization_barrier((last, done1, done3))
    back1, back3 = hop(done1, -1, False), hop(done3, -3, False)
    (done2,) = run_experts([last], *weights)
    back2 = hop(done2, -2, False)
    gathered = make_gather(high, low, [done0, back1, back2, back3])
    home = [gathered[0]] + [hop(gathered[d], -d, True) for d in (1, 2, 3)]
    fwd_out, bwd_out = make_finish(place, meta, home, fwd, bwd)

    arrived = jnp.where(section == 0, joined(0), joined(part))
    leaving = jnp.where(section == 0, bwd_out, fwd_out)
    left = across_sections(leaving.reshape(ROWS, sections, part).transpose(1, 0, 2))
    fwd_next = jnp.where(section == 0, arrived, shifted(fwd_out, 1, sections))
    bwd_next = jnp.where(section == sections - 1, arrived, shifted(bwd_out, -1, sections))
    return (fwd_next[None], bwd_next[None], left[sections - 1 :], left[:1])


def solution(mesh):
    placed = (
        P("pp", "ep", None),
        P("pp", "ep", None),
        P(None, "ep", "pp"),
        P(None, "ep", "pp"),
        P("pp", None),
        P("pp", None, "ep"),
        P("pp", None, "ep"),
        P("pp", "ep", None),
        P("pp", None, None, "ep", None),
        P("pp", None, None, "ep", None),
    )
    return jax.shard_map(
        body,
        mesh=mesh,
        in_specs=placed,
        out_specs=(
            P("pp", "ep", None),
            P("pp", "ep", None),
            P(None, "ep", "pp"),
            P(None, "ep", "pp"),
        ),
        check_vma=False,
    )
```

```python
import jax
import jax.numpy as jnp
from jax import lax
from jax.experimental import pallas as pl
from jax.experimental.pallas import tpu as pltpu
from jax.sharding import PartitionSpec as P

EPS = 1e-06
BF = jnp.bfloat16
F32 = jnp.float32
EXPERTS = 4
COLS = 4
CAP = 15
ROWS = 24
BOTH = 2 * ROWS
SLOTS = 2 * CAP
EXTRA = 128
WIDE = 1792
CHUNK = 512
RADIX = 4
LANES = 128


def device(y, x, core):
    return (y * COLS + x) * 2 + core


def hop(block, distance):
    route = []
    for y in range(EXPERTS):
        for x in range(COLS):
            for core in range(2):
                along_y = core == 1
                there = ((y + distance) % EXPERTS, x) if along_y else (y, (x + distance) % COLS)
                route.append((device(y, x, core), device(*there, core)))
    return lax.ppermute(block, "ep", route)


def rings(along_y):
    groups = []
    for core in range(2):
        if (core == 0) == along_y:
            groups += [[device(y, x, core) for y in range(EXPERTS)] for x in range(COLS)]
        else:
            groups += [[device(y, x, core) for x in range(COLS)] for y in range(EXPERTS)]
    return groups


def exchange(rows):
    return lax.all_to_all(
        rows, "ep", split_axis=0, concat_axis=0, axis_index_groups=rings(True), tiled=True
    )


def iota(shape, dim):
    return lax.broadcasted_iota(jnp.int32, shape, dim)


def dot(a, b):
    return jnp.dot(a, b, preferred_element_type=F32)


def split_gate(gate):
    high = gate.astype(BF).astype(F32)
    return high, (gate - high).astype(BF).astype(F32)


def send_kernel(place_ref, fwd_ref, bwd_ref, gain_ref, ids_ref, gates_ref, out_ref, meta_ref):
    lanes = iota((BOTH, EXTRA), 1)
    row = iota((BOTH, EXTRA), 0)
    in_fwd = row < ROWS
    own = lanes[:, :ROWS] == row[:, :ROWS] - jnp.where(in_fwd[:, :ROWS], 0, ROWS)

    def column(ref, k):
        both = jnp.where(in_fwd[:, :ROWS], ref[0, k : k + 1, :], ref[1, k : k + 1, :])
        return jnp.sum(jnp.where(own, both, jnp.zeros_like(both)), axis=1, keepdims=True)

    first, second = column(ids_ref, 0), column(ids_ref, 1)
    named = jnp.where((lanes == first) | (lanes == second), 1.0, 0.0)
    r0, r1 = iota((BOTH, BOTH), 0), iota((BOTH, BOTH), 1)
    earlier = jnp.where((r1 < r0) & ((r1 < ROWS) == (r0 < ROWS)), 1.0, 0.0)
    rank = dot(earlier.astype(BF), named.astype(BF))
    offset = jnp.where(in_fwd[:, 0:1], 0, CAP)
    slots = []
    for chosen in (first, second):
        taken = jnp.sum(jnp.where(lanes == chosen, rank, 0.0), axis=1, keepdims=True)
        slots.append(taken.astype(jnp.int32) + offset)
    ahead = [
        jnp.bitwise_and(chosen - place_ref[1] + EXPERTS, EXPERTS - 1) for chosen in (first, second)
    ]
    fields = [ahead[0].astype(F32), slots[0].astype(F32), ahead[1].astype(F32), slots[1].astype(F32)]
    fields += split_gate(column(gates_ref, 0))
    fields += split_gate(column(gates_ref, 1))
    fields += [first.astype(F32), second.astype(F32)]
    meta = jnp.zeros((BOTH, EXTRA), F32)
    for place, field in enumerate(fields):
        meta = jnp.where(lanes == place, field, meta)
    meta_ref[...] = meta

    def as_row(column):
        return jnp.sum(jnp.where(r0 == r1, column, 0), axis=0, keepdims=True)

    target = iota((EXPERTS * BOTH, BOTH), 0)
    source = iota((EXPERTS * BOTH, BOTH), 1)
    routed = (target == as_row(first * BOTH + slots[0])) | (
        target == as_row(second * BOTH + slots[1])
    )
    copied = target == source
    for part in range(1, COLS):
        copied = copied | (target == source + part * BOTH)
    routed_f = jnp.where(routed, 1.0, 0.0)
    copied_f = jnp.where(copied, 1.0, 0.0)
    pick = jnp.where(place_ref[0] == 0, routed_f, copied_f).astype(BF)
    values = jnp.concatenate([fwd_ref[...].astype(F32), bwd_ref[...].astype(F32)], axis=0)
    features = values.shape[1]
    inverse = lax.rsqrt(jnp.mean(values * values, axis=-1, keepdims=True) + EPS)
    normed = (values * inverse * gain_ref[...]).astype(BF)
    for start in range(0, features, CHUNK):
        out_ref[:, start : start + CHUNK] = dot(pick, normed[:, start : start + CHUNK]).astype(BF)
    out_ref[:, features:] = dot(pick, meta.astype(BF)).astype(BF)


def slot_targets(place_ref, extra):
    total = EXPERTS * BOTH
    row = iota((total, 1), 0)
    part = (
        (row >= BOTH).astype(jnp.int32)
        + (row >= 2 * BOTH).astype(jnp.int32)
        + (row >= 3 * BOTH).astype(jnp.int32)
    )
    place = row - part * BOTH
    on_first = place_ref[0] == 0
    packed = jnp.where(place < SLOTS, part * SLOTS + place, -EXPERTS * LANES)
    found = []
    for k in range(COLS):
        there, high, low = -1, 0.0, 0.0
        if k < 2:
            expert = extra[:, 2 * k : 2 * k + 1].astype(jnp.int32)
            slot = extra[:, 2 * k + 1 : 2 * k + 2].astype(jnp.int32)
            there = expert * LANES + part * SLOTS + slot
            high = extra[:, 4 + 2 * k : 5 + 2 * k]
            low = extra[:, 5 + 2 * k : 6 + 2 * k]
        target = jnp.where(on_first, packed + k * LANES, there)
        found.append((target, jnp.where(on_first, 1.0, high), jnp.where(on_first, 0.0, low)))
    return found


def move(pick_ref, rows_ref, parts, out_refs):
    width = rows_ref.shape[1]
    for start in range(0, width, CHUNK):
        cut = slice(start, min(start + CHUNK, width))
        rows = rows_ref[:, cut]
        for part, out_ref in zip(parts, out_refs):
            moved = dot(pick_ref[part * LANES : (part + 1) * LANES, :], rows)
            out_ref[:, cut] = moved[: COLS * SLOTS].astype(BF)


def near_kernel(place_ref, rows_ref, extra_ref, first_ref, third_ref, pick_ref):
    @pl.when(pl.program_id(0) == 0)
    def _():
        column = iota((EXPERTS * BOTH, EXPERTS * LANES), 1)
        pick = jnp.zeros(column.shape, F32)
        for target, _, _ in slot_targets(place_ref, extra_ref[...].astype(F32)):
            pick = jnp.where(column == target, 1.0, pick)
        pick_ref[...] = pick.T.astype(BF)

    move(pick_ref, rows_ref, (1, 3), (first_ref, third_ref))


def rest_kernel(
    place_ref, rows_ref, extra_ref, pick_ref, own_ref, second_ref, high_ref, low_ref
):
    @pl.when(pl.program_id(0) == 0)
    def _():
        column = iota((EXPERTS * BOTH, EXPERTS * LANES), 1)
        high_m = jnp.zeros(column.shape, F32)
        low_m = jnp.zeros(column.shape, F32)
        for target, high, low in slot_targets(place_ref, extra_ref[...].astype(F32)):
            here = column == target
            high_m = jnp.where(here, high, high_m)
            low_m = jnp.where(here, low, low_m)
        high_ref[...] = high_m.astype(BF)
        low_ref[...] = low_m.astype(BF)

    move(pick_ref, rows_ref, (0, 2), (own_ref, second_ref))


def expert_kernel(steps, count, *refs):
    rows_refs = refs[:count]
    g0_ref, g1_ref, u0_ref, u1_ref, d0_ref, d1_ref = refs[count : count + 6]
    token_ref, gate_acc, up_acc, hid_ref = refs[-4:]
    out_refs = refs[-4 - count : -4]
    step = pl.program_id(0)
    token_ref[...] = jnp.zeros_like(token_ref)

    @pl.when(step < steps)
    def _():
        gate_w = jnp.concatenate([g0_ref[...], g1_ref[...]], axis=1)
        up_w = jnp.concatenate([u0_ref[...], u1_ref[...]], axis=1)
        for i, rows_ref in enumerate(rows_refs):
            gate = dot(rows_ref[...], gate_w)
            up = dot(rows_ref[...], up_w)

            @pl.when(step == 0)
            def _():
                gate_acc[i] = gate
                up_acc[i] = up

            @pl.when(step > 0)
            def _():
                gate_acc[i] += gate
                up_acc[i] += up

    @pl.when(step == steps - 1)
    def _():
        gate = gate_acc[...]
        hid_ref[...] = (gate / (1.0 + jnp.exp(-gate)) * up_acc[...]).astype(BF)

    @pl.when(step >= steps)
    def _():
        down = jnp.concatenate([d0_ref[...], d1_ref[...]], axis=0)
        for i, out_ref in enumerate(out_refs):
            out_ref[...] = dot(hid_ref[i], down).astype(BF)


def gather_kernel(parts, last, high_ref, low_ref, *refs):
    rows_refs, so_far_ref, out_ref = refs[: len(parts)], refs[len(parts)], refs[-1]
    width = rows_refs[0].shape[1]
    used = COLS * SLOTS
    for start in range(0, width, CHUNK):
        cut = slice(start, min(start + CHUNK, width))
        total = so_far_ref[:, cut] if last else 0.0
        for part, ref in zip(parts, rows_refs):
            lanes = slice(part * LANES, part * LANES + used)
            rows = ref[:, cut]
            total += dot(high_ref[:, lanes], rows) + dot(low_ref[:, lanes], rows)
        out_ref[:, cut] = total.astype(out_ref.dtype)


def finish_kernel(place_ref, meta_ref, rows_ref, fwd_ref, bwd_ref, of_ref, ob_ref, *leave_refs):
    meta = meta_ref[...]
    total = EXPERTS * BOTH
    column = iota((BOTH, total), 1)
    row = iota((BOTH, total), 0)
    high = jnp.zeros((BOTH, total), F32)
    low = jnp.zeros((BOTH, total), F32)
    for k in range(2):
        there = (meta[:, 8 + k : 9 + k] * BOTH + meta[:, 2 * k + 1 : 2 * k + 2]).astype(jnp.int32)
        high = jnp.where(column == there, meta[:, 4 + 2 * k : 5 + 2 * k], high)
        low = jnp.where(column == there, meta[:, 5 + 2 * k : 6 + 2 * k], low)
    same = column == row
    for part in range(1, COLS):
        same = same | (column == row + part * BOTH)
    ones = jnp.where(same, 1.0, 0.0)
    on_first = place_ref[0] == 0
    high = jnp.where(on_first, high, ones).astype(BF)
    low = jnp.where(on_first, low, 0.0).astype(BF)
    width = fwd_ref.shape[1] // RADIX
    for part in range(RADIX):
        cut = slice(part * width, (part + 1) * width)
        rows = rows_ref[:, cut]
        mixture = dot(high, rows) + dot(low, rows)
        of_ref[:, cut] = (fwd_ref[:, cut].astype(F32) + mixture[:ROWS]).astype(BF)
        ob_ref[:, cut] = (bwd_ref[:, cut].astype(F32) + mixture[ROWS:]).astype(BF)
    for part in range(RADIX):
        up = slice(part * width, (part + 1) * width)
        down = slice((RADIX - 1 - part) * width, (RADIX - part) * width)

        @pl.when(place_ref[2] == 0)
        def _():
            leave_refs[part][...] = ob_ref[:, up]

        @pl.when(place_ref[2] != 0)
        def _():
            leave_refs[part][...] = of_ref[:, down]


SMEM = pl.BlockSpec(memory_space=pltpu.SMEM)


def params(mib=20):
    return pltpu.CompilerParams(vmem_limit_bytes=mib * 1024 * 1024)


def whole(shape):
    return pl.BlockSpec(shape, lambda i: (0,) * len(shape))


def tile(rows, width=WIDE):
    return pl.BlockSpec((rows, width), lambda i: (0, i))


def shape(rows, columns, dtype=BF):
    return jax.ShapeDtypeStruct((rows, columns), dtype)


def make_send(place, fwd, bwd, gain, ids, gates):
    features = fwd.shape[1]
    vmem = pl.BlockSpec(memory_space=pltpu.VMEM)
    return pl.pallas_call(
        send_kernel,
        out_shape=(shape(EXPERTS * BOTH, features + EXTRA), shape(BOTH, EXTRA, F32)),
        in_specs=[SMEM] + [vmem] * 5,
        out_specs=(vmem, vmem),
        compiler_params=params(),
        name="normed",
    )(place, fwd, bwd, gain, ids, gates)


def make_near(place, rows):
    features = rows.shape[1] - EXTRA
    total = EXPERTS * BOTH
    lanes = EXPERTS * LANES
    return pl.pallas_call(
        near_kernel,
        grid=(features // WIDE,),
        out_shape=(shape(COLS * SLOTS, features),) * 2 + (shape(lanes, total),),
        in_specs=[SMEM, tile(total), whole_extra(total, features)],
        out_specs=(tile(COLS * SLOTS),) * 2 + (whole((lanes, total)),),
        compiler_params=params(),
        name="near",
    )(place, rows, rows)


def make_rest(place, rows, pick):
    features = rows.shape[1] - EXTRA
    total = EXPERTS * BOTH
    lanes = EXPERTS * LANES
    return pl.pallas_call(
        rest_kernel,
        grid=(features // WIDE,),
        out_shape=(shape(COLS * SLOTS, features),) * 2 + (shape(total, lanes),) * 2,
        in_specs=[SMEM, tile(total), whole_extra(total, features), whole((lanes, total))],
        out_specs=(tile(COLS * SLOTS),) * 2 + (whole((total, lanes)),) * 2,
        compiler_params=params(),
        name="rest",
    )(place, rows, rows, pick)


def whole_extra(total, features):
    return pl.BlockSpec((total, EXTRA), lambda i: (0, features // EXTRA))


def run_experts(blocks, gates, ups, downs, *before):
    count = len(blocks)
    rows, features = blocks[0].shape
    width = gates[0].shape[1]
    steps = features // WIDE
    first = lambda i: jnp.minimum(i, steps - 1)
    later = lambda i: jnp.maximum(i - steps, 0)
    tall = pl.BlockSpec((WIDE, width), lambda i: (first(i), 0))
    flat = pl.BlockSpec((width, WIDE), lambda i: (0, later(i)))
    token = (8, LANES)

    def body(*refs):
        expert_kernel(steps, count, *refs)

    return pl.pallas_call(
        body,
        grid=(2 * steps,),
        out_shape=(shape(rows, features),) * count + (shape(*token, jnp.int32),),
        in_specs=[pl.BlockSpec((rows, WIDE), lambda i: (0, first(i)))] * count
        + [tall] * 4
        + [flat] * 2
        + [pl.BlockSpec(memory_space=pl.ANY)] * len(before),
        out_specs=(pl.BlockSpec((rows, WIDE), lambda i: (0, later(i))),) * count + (whole(token),),
        scratch_shapes=[
            pltpu.VMEM((count, rows, 2 * width), F32),
            pltpu.VMEM((count, rows, 2 * width), F32),
            pltpu.VMEM((count, rows, 2 * width), BF),
        ],
        compiler_params=params(),
        name="experts",
    )(*blocks, gates[0], gates[1], ups[0], ups[1], downs[0], downs[1], *before)


def make_gather(high, low, blocks, parts, so_far=None, before=()):
    rows, features = blocks[0].shape
    total = high.shape[0]
    last = so_far is not None

    def body(*refs):
        gather_kernel(parts, last, *refs)

    return pl.pallas_call(
        body,
        grid=(features // WIDE,),
        out_shape=shape(total, features, BF if last else F32),
        in_specs=[whole(high.shape), whole(low.shape)]
        + [tile(rows)] * len(blocks)
        + [tile(total)] * last
        + [pl.BlockSpec(memory_space=pl.ANY)] * len(before),
        out_specs=tile(total),
        compiler_params=params(),
        name="gather",
    )(high, low, *blocks, *([so_far] if last else []), *before)


def make_finish(place, meta, rows, fwd, bwd):
    features = fwd.shape[1]
    vmem = pl.BlockSpec(memory_space=pltpu.VMEM)
    return pl.pallas_call(
        finish_kernel,
        out_shape=(shape(ROWS, features),) * 2 + (shape(ROWS, features // RADIX),) * RADIX,
        in_specs=[SMEM] + [vmem] * 4,
        out_specs=(vmem,) * (2 + RADIX),
        compiler_params=params(),
        name="finish",
    )(place, meta, rows, fwd, bwd)


def shifted(block, distance, count):
    route = [(i, i + distance) for i in range(count) if 0 <= i + distance < count]
    return lax.ppermute(block, "pp", route)


def from_other_core(block):
    return lax.ppermute(block, "ep", [(i, i ^ 1) for i in range(lax.axis_size("ep"))])


def tree_start(fwd, bwd, section):
    odd = (section & 1) == 1
    return jnp.where(odd, bwd, fwd), jnp.where(odd, fwd, bwd)


def tree_send(block, step, sections):
    bit = 1 << step
    route = [(s, s - bit) for s in range(bit, sections, 2 * bit)]
    route += [(s, s + bit) for s in range(bit - 1, sections, 2 * bit)]
    return lax.ppermute(block, "pp", route)


def tree_join(held, got, step, section):
    upper = (section & (1 << step)) != 0
    return jnp.where(
        upper, jnp.concatenate([got, held], axis=0), jnp.concatenate([held, got], axis=0)
    )


def scatter_far(parts, section, sections):
    final = sections - 1
    held = parts[0]
    for k in range(1, RADIX):
        got = lax.ppermute(parts[k], "pp", [(final, final - RADIX * k), (0, RADIX * k)])
        here = (section == final - RADIX * k) | (section == RADIX * k)
        held = jnp.where(here, got, held)
    return held


def scatter_near(held, section, sections):
    place = section & (RADIX - 1)
    width = held.shape[1] // RADIX
    blocks = [held[:, m * width : (m + 1) * width] for m in range(RADIX)]
    to_fwd, to_bwd = blocks[RADIX - 1], blocks[0]
    for m in range(1, RADIX):
        sent = jnp.where(place == 0, blocks[m], blocks[RADIX - 1 - m])
        route = [(s, s - m) for s in range(RADIX - 1, sections, RADIX)]
        route += [(s, s + m) for s in range(0, sections, RADIX)]
        got = lax.ppermute(sent, "pp", route)
        to_fwd = jnp.where(place == RADIX - 1 - m, got, to_fwd)
        to_bwd = jnp.where(place == m, got, to_bwd)
    return to_fwd, to_bwd


def body(
    state_fwd,
    state_bwd,
    enter_fwd,
    enter_bwd,
    norm_gain,
    w_gate,
    w_up,
    w_down,
    route_ids,
    route_gates,
):
    sections = lax.axis_size("pp")
    section = lax.axis_index("pp")
    position = lax.axis_index("ep")
    place = jnp.stack([position % 2, position // (2 * COLS), section]).astype(jnp.int32)
    fwd, bwd = state_fwd[0], state_bwd[0]
    features = fwd.shape[1]
    part = features // sections
    ids = route_ids[0, 0].transpose(0, 2, 1)
    gates = route_gates[0, 0].transpose(0, 2, 1)

    own = (w_gate[0], w_up[0], w_down[0])
    sent, meta = make_send(place, fwd, bwd, norm_gain, ids, gates)
    after = lax.optimization_barrier
    passed, meta = after((own, meta))
    weights = tuple(zip(own, (from_other_core(w) for w in passed)))

    rows = exchange(sent)
    send1, send3, pick = make_near(place, rows)
    near, far = hop(send1, 1), hop(send3, 3)
    send0, send2, high, low = make_rest(place, rows, pick)
    last = hop(send2, 2)
    done0, token = run_experts([send0], *weights)
    held, sent = tree_start(enter_fwd[0], enter_bwd[0], section + token[0, 0])
    got = tree_send(sent, 0, sections)
    held = tree_join(held, got, 0, section)
    got = tree_send(held, 1, sections)
    done1, done3, token = run_experts([near, far], *weights, token, got)
    back1, back3 = hop(done1, -1), hop(done3, -3)
    done2, token = run_experts([last], *weights, token)
    back2 = hop(done2, -2)
    held = tree_join(held, got, 1, section + token[0, 0])
    got = tree_send(held, 2, sections)
    held = tree_join(held, got, 2, section)
    begun = make_gather(high, low, [done0, back1, back3], (0, 1, 3))
    gathered = make_gather(high, low, [back2], (2,), begun, (got,))
    got = tree_send(held, 3, sections)
    held = tree_join(held, got, 3, section)
    entered = held.reshape(sections, ROWS, part).transpose(1, 0, 2).reshape(ROWS, features)
    fwd_out, bwd_out, *leaving = make_finish(place, meta, exchange(gathered), fwd, bwd)
    fwd_out, bwd_out, entered = after((fwd_out, bwd_out, entered))

    from_left, from_right = shifted(fwd_out, 1, sections), shifted(bwd_out, -1, sections)
    held = scatter_far(leaving, section, sections)
    held, from_left, from_right = after((held, from_left, from_right))
    leave_fwd, leave_bwd = scatter_near(held, section, sections)
    fwd_next = jnp.where(section == 0, entered, from_left)
    bwd_next = jnp.where(section == sections - 1, entered, from_right)
    return (fwd_next[None], bwd_next[None], leave_fwd[None], leave_bwd[None])


def solution(mesh):
    placed = (
        P("pp", "ep", None),
        P("pp", "ep", None),
        P(None, "ep", "pp"),
        P(None, "ep", "pp"),
        P("pp", None),
        P("pp", None, "ep"),
        P("pp", None, "ep"),
        P("pp", "ep", None),
        P("pp", None, None, "ep", None),
        P("pp", None, None, "ep", None),
    )
    return jax.shard_map(
        body,
        mesh=mesh,
        in_specs=placed,
        out_specs=(
            P("pp", "ep", None),
            P("pp", "ep", None),
            P(None, "ep", "pp"),
            P(None, "ep", "pp"),
        ),
        check_vma=False,
    )
```

```python
import jax
import jax.numpy as jnp
from jax import lax
from jax.experimental import pallas as pl
from jax.experimental.pallas import tpu as pltpu
from jax.sharding import PartitionSpec as P

EPS = 1e-06
BF = jnp.bfloat16
F32 = jnp.float32
EXPERTS = 4
COLS = 4
CAP = 15
ROWS = 24
BOTH = 2 * ROWS
SLOTS = 2 * CAP
EXTRA = 128
WIDE = 1792
CHUNK = 512
LANES = 128


def device(y, x, core):
    return (y * COLS + x) * 2 + core


def hop(block, distance):
    route = []
    for y in range(EXPERTS):
        for x in range(COLS):
            for core in range(2):
                along_y = core == 1
                there = ((y + distance) % EXPERTS, x) if along_y else (y, (x + distance) % COLS)
                route.append((device(y, x, core), device(*there, core)))
    return lax.ppermute(block, "ep", route)


def rings(along_y):
    groups = []
    for core in range(2):
        if (core == 0) == along_y:
            groups += [[device(y, x, core) for y in range(EXPERTS)] for x in range(COLS)]
        else:
            groups += [[device(y, x, core) for x in range(COLS)] for y in range(EXPERTS)]
    return groups


def exchange(rows):
    return lax.all_to_all(
        rows, "ep", split_axis=0, concat_axis=0, axis_index_groups=rings(True), tiled=True
    )


def iota(shape, dim):
    return lax.broadcasted_iota(jnp.int32, shape, dim)


def dot(a, b):
    return jnp.dot(a, b, preferred_element_type=F32)


def split_gate(gate):
    high = gate.astype(BF).astype(F32)
    return high, (gate - high).astype(BF).astype(F32)


def send_kernel(place_ref, fwd_ref, bwd_ref, gain_ref, ids_ref, gates_ref, out_ref, meta_ref):
    lanes = iota((BOTH, EXTRA), 1)
    row = iota((BOTH, EXTRA), 0)
    in_fwd = row < ROWS
    own = lanes[:, :ROWS] == row[:, :ROWS] - jnp.where(in_fwd[:, :ROWS], 0, ROWS)

    def column(ref, k):
        both = jnp.where(in_fwd[:, :ROWS], ref[0, k : k + 1, :], ref[1, k : k + 1, :])
        return jnp.sum(jnp.where(own, both, jnp.zeros_like(both)), axis=1, keepdims=True)

    first, second = column(ids_ref, 0), column(ids_ref, 1)
    named = jnp.where((lanes == first) | (lanes == second), 1.0, 0.0)
    r0, r1 = iota((BOTH, BOTH), 0), iota((BOTH, BOTH), 1)
    earlier = jnp.where((r1 < r0) & ((r1 < ROWS) == (r0 < ROWS)), 1.0, 0.0)
    rank = dot(earlier.astype(BF), named.astype(BF))
    offset = jnp.where(in_fwd[:, 0:1], 0, CAP)
    slots = []
    for chosen in (first, second):
        taken = jnp.sum(jnp.where(lanes == chosen, rank, 0.0), axis=1, keepdims=True)
        slots.append(taken.astype(jnp.int32) + offset)
    ahead = [
        jnp.bitwise_and(chosen - place_ref[1] + EXPERTS, EXPERTS - 1) for chosen in (first, second)
    ]
    fields = [ahead[0].astype(F32), slots[0].astype(F32), ahead[1].astype(F32), slots[1].astype(F32)]
    fields += split_gate(column(gates_ref, 0))
    fields += split_gate(column(gates_ref, 1))
    fields += [first.astype(F32), second.astype(F32)]
    meta = jnp.zeros((BOTH, EXTRA), F32)
    for place, field in enumerate(fields):
        meta = jnp.where(lanes == place, field, meta)
    meta_ref[...] = meta

    def as_row(column):
        return jnp.sum(jnp.where(r0 == r1, column, 0), axis=0, keepdims=True)

    target = iota((EXPERTS * BOTH, BOTH), 0)
    source = iota((EXPERTS * BOTH, BOTH), 1)
    routed = (target == as_row(first * BOTH + slots[0])) | (
        target == as_row(second * BOTH + slots[1])
    )
    copied = target == source
    for part in range(1, COLS):
        copied = copied | (target == source + part * BOTH)
    routed_f = jnp.where(routed, 1.0, 0.0)
    copied_f = jnp.where(copied, 1.0, 0.0)
    pick = jnp.where(place_ref[0] == 0, routed_f, copied_f).astype(BF)
    values = jnp.concatenate([fwd_ref[...].astype(F32), bwd_ref[...].astype(F32)], axis=0)
    features = values.shape[1]
    inverse = lax.rsqrt(jnp.mean(values * values, axis=-1, keepdims=True) + EPS)
    normed = (values * inverse * gain_ref[...]).astype(BF)
    for start in range(0, features, CHUNK):
        out_ref[:, start : start + CHUNK] = dot(pick, normed[:, start : start + CHUNK]).astype(BF)
    out_ref[:, features:] = dot(pick, meta.astype(BF)).astype(BF)


def slot_targets(place_ref, extra):
    total = EXPERTS * BOTH
    row = iota((total, 1), 0)
    part = (
        (row >= BOTH).astype(jnp.int32)
        + (row >= 2 * BOTH).astype(jnp.int32)
        + (row >= 3 * BOTH).astype(jnp.int32)
    )
    place = row - part * BOTH
    on_first = place_ref[0] == 0
    packed = jnp.where(place < SLOTS, part * SLOTS + place, -EXPERTS * LANES)
    found = []
    for k in range(COLS):
        there, high, low = -1, 0.0, 0.0
        if k < 2:
            expert = extra[:, 2 * k : 2 * k + 1].astype(jnp.int32)
            slot = extra[:, 2 * k + 1 : 2 * k + 2].astype(jnp.int32)
            there = expert * LANES + part * SLOTS + slot
            high = extra[:, 4 + 2 * k : 5 + 2 * k]
            low = extra[:, 5 + 2 * k : 6 + 2 * k]
        target = jnp.where(on_first, packed + k * LANES, there)
        found.append((target, jnp.where(on_first, 1.0, high), jnp.where(on_first, 0.0, low)))
    return found


def move(pick_ref, rows_ref, parts, out_refs):
    width = rows_ref.shape[1]
    for start in range(0, width, CHUNK):
        cut = slice(start, min(start + CHUNK, width))
        rows = rows_ref[:, cut]
        for part, out_ref in zip(parts, out_refs):
            moved = dot(pick_ref[part * LANES : (part + 1) * LANES, :], rows)
            out_ref[:, cut] = moved[: COLS * SLOTS].astype(BF)


def near_kernel(place_ref, rows_ref, extra_ref, first_ref, third_ref, pick_ref):
    @pl.when(pl.program_id(0) == 0)
    def _():
        column = iota((EXPERTS * BOTH, EXPERTS * LANES), 1)
        pick = jnp.zeros(column.shape, F32)
        for target, _, _ in slot_targets(place_ref, extra_ref[...].astype(F32)):
            pick = jnp.where(column == target, 1.0, pick)
        pick_ref[...] = pick.T.astype(BF)

    move(pick_ref, rows_ref, (1, 3), (first_ref, third_ref))


def rest_kernel(
    place_ref, rows_ref, extra_ref, pick_ref, own_ref, second_ref, back_ref
):
    @pl.when(pl.program_id(0) == 0)
    def _():
        column = iota((EXPERTS * BOTH, EXPERTS * LANES), 1)
        high_m = jnp.zeros(column.shape, F32)
        low_m = jnp.zeros(column.shape, F32)
        for target, high, low in slot_targets(place_ref, extra_ref[...].astype(F32)):
            here = column == target
            high_m = jnp.where(here, high, high_m)
            low_m = jnp.where(here, low, low_m)
        back_ref[:, : EXPERTS * LANES] = high_m.astype(BF)
        back_ref[:, EXPERTS * LANES :] = low_m.astype(BF)

    move(pick_ref, rows_ref, (0, 2), (own_ref, second_ref))


def expert_kernel(steps, count, *refs):
    rows_refs = refs[:count]
    g0_ref, u0_ref, d0_ref, g1_ref, u1_ref, d1_ref = refs[count : count + 6]
    features = d0_ref.shape[1]
    width = g0_ref.shape[1]
    token_ref, gate_acc, up_acc, hid_ref = refs[-4:]
    out_refs = refs[-4 - count : -4]
    step = pl.program_id(0)
    token_ref[...] = jnp.zeros_like(token_ref)

    @pl.when(step < steps)
    def _():
        gate_w = jnp.concatenate([g0_ref[...], g1_ref[...]], axis=1)
        up_w = jnp.concatenate([u0_ref[...], u1_ref[...]], axis=1)
        for i, rows_ref in enumerate(rows_refs):
            gate = dot(rows_ref[...], gate_w)
            up = dot(rows_ref[...], up_w)

            @pl.when(step == 0)
            def _():
                gate_acc[i] = gate
                up_acc[i] = up

            @pl.when(step > 0)
            def _():
                gate_acc[i] += gate
                up_acc[i] += up

    @pl.when(step == steps - 1)
    def _():
        gate = gate_acc[...]
        hid_ref[...] = (gate / (1.0 + jnp.exp(-gate)) * up_acc[...]).astype(BF)

    @pl.when(step >= steps)
    def _():
        other = [d1_ref[i * width : (i + 1) * width, :] for i in range(features // width)]
        down = jnp.concatenate([d0_ref[...], jnp.concatenate(other, axis=1)], axis=0)
        for i, out_ref in enumerate(out_refs):
            out_ref[...] = dot(hid_ref[i], down).astype(BF)


def gather_kernel(parts, last, back_ref, *refs):
    rows_refs, so_far_ref, out_ref = refs[: len(parts)], refs[len(parts)], refs[-1]
    width = rows_refs[0].shape[1]
    used = COLS * SLOTS
    for start in range(0, width, CHUNK):
        cut = slice(start, min(start + CHUNK, width))
        total = so_far_ref[:, cut] if last else 0.0
        for part, ref in zip(parts, rows_refs):
            high = slice(part * LANES, part * LANES + used)
            low = slice((EXPERTS + part) * LANES, (EXPERTS + part) * LANES + used)
            rows = ref[:, cut]
            total += dot(back_ref[:, high], rows) + dot(back_ref[:, low], rows)
        out_ref[:, cut] = total.astype(out_ref.dtype)


def finish_kernel(place_ref, meta_ref, rows_ref, fwd_ref, bwd_ref, _, of_ref, ob_ref):
    meta = meta_ref[...]
    total = EXPERTS * BOTH
    column = iota((BOTH, total), 1)
    row = iota((BOTH, total), 0)
    high = jnp.zeros((BOTH, total), F32)
    low = jnp.zeros((BOTH, total), F32)
    for k in range(2):
        there = (meta[:, 8 + k : 9 + k] * BOTH + meta[:, 2 * k + 1 : 2 * k + 2]).astype(jnp.int32)
        high = jnp.where(column == there, meta[:, 4 + 2 * k : 5 + 2 * k], high)
        low = jnp.where(column == there, meta[:, 5 + 2 * k : 6 + 2 * k], low)
    same = column == row
    for part in range(1, COLS):
        same = same | (column == row + part * BOTH)
    ones = jnp.where(same, 1.0, 0.0)
    on_first = place_ref[0] == 0
    high = jnp.where(on_first, high, ones).astype(BF)
    low = jnp.where(on_first, low, 0.0).astype(BF)
    width = fwd_ref.shape[1]
    for start in range(0, width, CHUNK):
        cut = slice(start, min(start + CHUNK, width))
        rows = rows_ref[:, cut]
        mixture = dot(high, rows) + dot(low, rows)
        of_ref[:, cut] = (fwd_ref[:, cut].astype(F32) + mixture[:ROWS]).astype(BF)
        ob_ref[:, cut] = (bwd_ref[:, cut].astype(F32) + mixture[ROWS:]).astype(BF)


def ends_kernel(place_ref, left_ref, right_ref, fwd_ref, bwd_ref, out_ref):
    count, _, part = out_ref.shape
    at_start = place_ref[2] == 0
    for r in range(count):
        near, far = [slice(j * part, (j + 1) * part) for j in (r, 2 * count - 1 - r)]

        @pl.when(at_start)
        def _():
            out_ref[r, :ROWS, :] = left_ref[:, near]
            out_ref[r, ROWS:, :] = bwd_ref[:, near]

        @pl.when(jnp.logical_not(at_start))
        def _():
            out_ref[r, :ROWS, :] = fwd_ref[:, far]
            out_ref[r, ROWS:, :] = right_ref[:, far]


def entered_kernel(place_ref, held_ref, got_ref, out_ref):
    count, _, part = held_ref.shape
    at_start = place_ref[2] == 0
    for r in range(count):
        near, far = [slice(j * part, (j + 1) * part) for j in (r, 2 * count - 1 - r)]

        @pl.when(at_start)
        def _():
            out_ref[:, near] = held_ref[r, :ROWS, :]
            out_ref[:, far] = got_ref[r]

        @pl.when(jnp.logical_not(at_start))
        def _():
            out_ref[:, near] = got_ref[r]
            out_ref[:, far] = held_ref[r, ROWS:, :]


SMEM = pl.BlockSpec(memory_space=pltpu.SMEM)


def params(mib=20):
    return pltpu.CompilerParams(vmem_limit_bytes=mib * 1024 * 1024)


def whole(shape):
    return pl.BlockSpec(shape, lambda i: (0,) * len(shape))


def tile(rows, width=WIDE):
    return pl.BlockSpec((rows, width), lambda i: (0, i))


def shape(rows, columns, dtype=BF):
    return jax.ShapeDtypeStruct((rows, columns), dtype)


def make_send(place, fwd, bwd, gain, ids, gates):
    features = fwd.shape[1]
    vmem = pl.BlockSpec(memory_space=pltpu.VMEM)
    return pl.pallas_call(
        send_kernel,
        out_shape=(shape(EXPERTS * BOTH, features + EXTRA), shape(BOTH, EXTRA, F32)),
        in_specs=[SMEM] + [vmem] * 5,
        out_specs=(vmem, vmem),
        compiler_params=params(),
        name="normed",
    )(place, fwd, bwd, gain, ids, gates)


def make_near(place, rows):
    features = rows.shape[1] - EXTRA
    total = EXPERTS * BOTH
    lanes = EXPERTS * LANES
    return pl.pallas_call(
        near_kernel,
        grid=(features // WIDE,),
        out_shape=(shape(COLS * SLOTS, features),) * 2 + (shape(lanes, total),),
        in_specs=[SMEM, tile(total), whole_extra(total, features)],
        out_specs=(tile(COLS * SLOTS),) * 2 + (whole((lanes, total)),),
        compiler_params=params(),
        name="near",
    )(place, rows, rows)


def pack_kernel(gate_ref, up_ref, down_ref, _, out_ref):
    features, width = gate_ref.shape
    out_ref[:features, :] = gate_ref[...]
    out_ref[features : 2 * features, :] = up_ref[...]
    for i in range(features // width):
        at = 2 * features + i * width
        out_ref[at : at + width, :] = down_ref[:, i * width : (i + 1) * width]


def make_pack(gate, up, down, before):
    features, width = gate.shape
    vmem = pl.BlockSpec(memory_space=pltpu.VMEM)
    return pl.pallas_call(
        pack_kernel,
        out_shape=shape(3 * features, width),
        in_specs=[vmem] * 3 + [pl.BlockSpec(memory_space=pl.ANY)],
        out_specs=vmem,
        compiler_params=params(),
        name="pack",
    )(gate, up, down, before)


def make_rest(place, rows, pick):
    features = rows.shape[1] - EXTRA
    total = EXPERTS * BOTH
    lanes = EXPERTS * LANES
    return pl.pallas_call(
        rest_kernel,
        grid=(features // WIDE,),
        out_shape=(shape(COLS * SLOTS, features),) * 2
        + (shape(total, 2 * lanes),),
        in_specs=[SMEM, tile(total), whole_extra(total, features), whole((lanes, total))],
        out_specs=(tile(COLS * SLOTS),) * 2 + (whole((total, 2 * lanes)),),
        compiler_params=params(),
        name="rest",
    )(place, rows, rows, pick)


def whole_extra(total, features):
    return pl.BlockSpec((total, EXTRA), lambda i: (0, features // EXTRA))


def run_experts(blocks, own, packed, *before):
    count = len(blocks)
    rows, features = blocks[0].shape
    width = own[0].shape[1]
    steps = features // WIDE
    first = lambda i: jnp.minimum(i, steps - 1)
    later = lambda i: jnp.maximum(i - steps, 0)
    tall = pl.BlockSpec((WIDE, width), lambda i: (first(i), 0))
    parts = [
        tall,
        pl.BlockSpec((WIDE, width), lambda i: (steps + first(i), 0)),
        pl.BlockSpec((WIDE, width), lambda i: (2 * steps + later(i), 0)),
    ]
    flat = pl.BlockSpec((width, WIDE), lambda i: (0, later(i)))
    token = (8, LANES)

    def body(*refs):
        expert_kernel(steps, count, *refs)

    return pl.pallas_call(
        body,
        grid=(2 * steps,),
        out_shape=(shape(rows, features),) * count + (shape(*token, jnp.int32),),
        in_specs=[pl.BlockSpec((rows, WIDE), lambda i: (0, first(i)))] * count
        + [tall, tall, flat]
        + parts
        + [pl.BlockSpec(memory_space=pl.ANY)] * len(before),
        out_specs=(pl.BlockSpec((rows, WIDE), lambda i: (0, later(i))),) * count + (whole(token),),
        scratch_shapes=[
            pltpu.VMEM((count, rows, 2 * width), F32),
            pltpu.VMEM((count, rows, 2 * width), F32),
            pltpu.VMEM((count, rows, 2 * width), BF),
        ],
        compiler_params=params(),
        name="experts",
    )(*blocks, *own, packed, packed, packed, *before)


def make_gather(back, blocks, parts, so_far=None, before=()):
    rows, features = blocks[0].shape
    total = back.shape[0]
    last = so_far is not None

    def body(*refs):
        gather_kernel(parts, last, *refs)

    return pl.pallas_call(
        body,
        grid=(features // WIDE,),
        out_shape=shape(total, features, BF if last else F32),
        in_specs=[whole(back.shape)]
        + [tile(rows)] * len(blocks)
        + [tile(total)] * last
        + [pl.BlockSpec(memory_space=pl.ANY)] * len(before),
        out_specs=tile(total),
        compiler_params=params(),
        name="gather",
    )(back, *blocks, *([so_far] if last else []), *before)


def make_finish(place, meta, rows, fwd, bwd, before):
    features = fwd.shape[1]
    vmem = pl.BlockSpec(memory_space=pltpu.VMEM)
    return pl.pallas_call(
        finish_kernel,
        out_shape=(shape(ROWS, features),) * 2,
        in_specs=[SMEM] + [vmem] * 4 + [pl.BlockSpec(memory_space=pl.ANY)],
        out_specs=(vmem,) * 2,
        compiler_params=params(),
        name="finish",
    )(place, meta, rows, fwd, bwd, before)


def make_simple(kernel, out, place, *arrays):
    vmem = pl.BlockSpec(memory_space=pltpu.VMEM)
    return pl.pallas_call(
        kernel,
        out_shape=jax.ShapeDtypeStruct(out, BF),
        in_specs=[SMEM] + [vmem] * len(arrays),
        out_specs=vmem,
        compiler_params=params(),
        name="blocks",
    )(place, *arrays)


def shifted(block, distance, count):
    return lax.ppermute(block, "pp", [(i, (i + distance) % count) for i in range(count)])


def mirrored(pairs, sections):
    return pairs + [(sections - 1 - i, sections - 1 - j) for i, j in pairs]


def from_other_core(block):
    return lax.ppermute(block, "ep", [(i, i ^ 1) for i in range(lax.axis_size("ep"))])


def inward(held, step, sections):
    bit = 1 << step
    pairs = [(i, i - bit) for i in range(bit, sections // 2, 2 * bit)]
    got = lax.ppermute(held, "pp", mirrored(pairs, sections))
    return jnp.concatenate([held, got], axis=0), got


def outward(own, place, sections):
    def move(block, *pairs):
        return lax.ppermute(block, "pp", mirrored(list(pairs), sections))

    a = move(own[2:8], (0, 2))
    b = move(jnp.where(place == 0, own[1:5], a[2:6]), (0, 1), (2, 4))
    c = move(jnp.where(place == 2, a[1:3], b[2:4]), (2, 3), (4, 6))
    d = move(jnp.where(place == 4, b[1:2], c[1:2]), (4, 5), (6, 7))
    mine = own[0]
    for at, block in ((1, b), (2, a), (3, c), (4, b), (5, d), (6, c), (7, d)):
        mine = jnp.where(place == at, block[0], mine)
    return mine


def body(
    state_fwd,
    state_bwd,
    enter_fwd,
    enter_bwd,
    norm_gain,
    w_gate,
    w_up,
    w_down,
    route_ids,
    route_gates,
):
    sections = lax.axis_size("pp")
    section = lax.axis_index("pp")
    position = lax.axis_index("ep")
    place = jnp.stack([position % 2, position // (2 * COLS), section]).astype(jnp.int32)
    fwd, bwd = state_fwd[0], state_bwd[0]
    features = fwd.shape[1]
    part = features // sections
    ids = route_ids[0, 0].transpose(0, 2, 1)
    gates = route_gates[0, 0].transpose(0, 2, 1)

    sent, meta = make_send(place, fwd, bwd, norm_gain, ids, gates)
    rows = exchange(sent)
    send1, send3, pick = make_near(place, rows)
    near, far = hop(send1, 1), hop(send3, 3)
    own = (w_gate[0], w_up[0], w_down[0])
    weights = own, from_other_core(make_pack(*own, pick))
    send0, send2, back = make_rest(place, rows, pick)
    last = hop(send2, 2)
    done0, done1, done3, token = run_experts([send0, near, far], *weights)
    back1, back3 = hop(done1, -1), hop(done3, -3)
    done2, token = run_experts([last], *weights, token)
    back2 = hop(done2, -2)

    half = sections // 2
    entering = jnp.concatenate([enter_fwd, enter_bwd], axis=1)
    entering = jnp.where(section + token[0, 0] >= 0, entering, 0)
    held, _ = inward(entering, 0, sections)
    held, got = inward(held, 1, sections)
    begun = make_gather(back, [done0, back1, back3], (0, 1, 3))
    gathered = make_gather(back, [back2], (2,), begun, (got,))
    held, got = inward(held, 2, sections)
    fwd_out, bwd_out = make_finish(place, meta, exchange(gathered), fwd, bwd, got)
    at_start = section == 0
    passed_on = jnp.where(at_start, held[:, ROWS:], held[:, :ROWS])
    got = lax.ppermute(passed_on, "pp", [(0, sections - 1), (sections - 1, 0)])
    entered = make_simple(entered_kernel, (ROWS, features), place, held, got)

    from_left, from_right = shifted(fwd_out, 1, sections), shifted(bwd_out, -1, sections)
    ends = make_simple(
        ends_kernel, (half, BOTH, part), place, from_left, from_right, fwd_out, bwd_out
    )
    mine = outward(ends, jnp.minimum(section, sections - 1 - section), sections)
    fwd_next = jnp.where(at_start, entered, from_left)
    bwd_next = jnp.where(section == sections - 1, entered, from_right)
    return (fwd_next[None], bwd_next[None], mine[None, :ROWS], mine[None, ROWS:])


def solution(mesh):
    placed = (
        P("pp", "ep", None),
        P("pp", "ep", None),
        P(None, "ep", "pp"),
        P(None, "ep", "pp"),
        P("pp", None),
        P("pp", None, "ep"),
        P("pp", None, "ep"),
        P("pp", "ep", None),
        P("pp", None, None, "ep", None),
        P("pp", None, None, "ep", None),
    )
    return jax.shard_map(
        body,
        mesh=mesh,
        in_specs=placed,
        out_specs=(
            P("pp", "ep", None),
            P("pp", "ep", None),
            P(None, "ep", "pp"),
            P(None, "ep", "pp"),
        ),
        check_vma=False,
    )
```

```python
import jax
import jax.numpy as jnp
from jax import lax
from jax.experimental import pallas as pl
from jax.experimental.pallas import tpu as pltpu
from jax.sharding import PartitionSpec as P

EPS = 1e-06
BF = jnp.bfloat16
F32 = jnp.float32
EXPERTS = 4
COLS = 4
CAP = 15
ROWS = 24
BOTH = 2 * ROWS
SLOTS = 2 * CAP
EXTRA = 128
WIDE = 1792
CHUNK = 512
LANES = 128


def device(y, x, core):
    return (y * COLS + x) * 2 + core


def hop(block, distance):
    route = []
    for y in range(EXPERTS):
        for x in range(COLS):
            for core in range(2):
                along_y = core == 1
                there = ((y + distance) % EXPERTS, x) if along_y else (y, (x + distance) % COLS)
                route.append((device(y, x, core), device(*there, core)))
    return lax.ppermute(block, "ep", route)


def rings(along_y):
    groups = []
    for core in range(2):
        if (core == 0) == along_y:
            groups += [[device(y, x, core) for y in range(EXPERTS)] for x in range(COLS)]
        else:
            groups += [[device(y, x, core) for x in range(COLS)] for y in range(EXPERTS)]
    return groups


def exchange(rows):
    return lax.all_to_all(
        rows, "ep", split_axis=0, concat_axis=0, axis_index_groups=rings(True), tiled=True
    )


def iota(shape, dim):
    return lax.broadcasted_iota(jnp.int32, shape, dim)


def dot(a, b):
    return jnp.dot(a, b, preferred_element_type=F32)


def split_gate(gate):
    high = gate.astype(BF).astype(F32)
    return high, (gate - high).astype(BF).astype(F32)


def send_kernel(place_ref, fwd_ref, bwd_ref, gain_ref, ids_ref, gates_ref, out_ref, meta_ref):
    lanes = iota((BOTH, EXTRA), 1)
    row = iota((BOTH, EXTRA), 0)
    in_fwd = row < ROWS
    own = lanes[:, :ROWS] == row[:, :ROWS] - jnp.where(in_fwd[:, :ROWS], 0, ROWS)

    def column(ref, k):
        both = jnp.where(in_fwd[:, :ROWS], ref[0, k : k + 1, :], ref[1, k : k + 1, :])
        return jnp.sum(jnp.where(own, both, jnp.zeros_like(both)), axis=1, keepdims=True)

    first, second = column(ids_ref, 0), column(ids_ref, 1)
    named = jnp.where((lanes == first) | (lanes == second), 1.0, 0.0)
    r0, r1 = iota((BOTH, BOTH), 0), iota((BOTH, BOTH), 1)
    earlier = jnp.where((r1 < r0) & ((r1 < ROWS) == (r0 < ROWS)), 1.0, 0.0)
    rank = dot(earlier.astype(BF), named.astype(BF))
    offset = jnp.where(in_fwd[:, 0:1], 0, CAP)
    slots = []
    for chosen in (first, second):
        taken = jnp.sum(jnp.where(lanes == chosen, rank, 0.0), axis=1, keepdims=True)
        slots.append(taken.astype(jnp.int32) + offset)
    ahead = [
        jnp.bitwise_and(chosen - place_ref[1] + EXPERTS, EXPERTS - 1) for chosen in (first, second)
    ]
    fields = [ahead[0].astype(F32), slots[0].astype(F32), ahead[1].astype(F32), slots[1].astype(F32)]
    fields += split_gate(column(gates_ref, 0))
    fields += split_gate(column(gates_ref, 1))
    fields += [first.astype(F32), second.astype(F32)]
    meta = jnp.zeros((BOTH, EXTRA), F32)
    for place, field in enumerate(fields):
        meta = jnp.where(lanes == place, field, meta)
    meta_ref[...] = meta

    def as_row(column):
        return jnp.sum(jnp.where(r0 == r1, column, 0), axis=0, keepdims=True)

    target = iota((EXPERTS * BOTH, BOTH), 0)
    source = iota((EXPERTS * BOTH, BOTH), 1)
    routed = (target == as_row(first * BOTH + slots[0])) | (
        target == as_row(second * BOTH + slots[1])
    )
    copied = target == source
    for part in range(1, COLS):
        copied = copied | (target == source + part * BOTH)
    routed_f = jnp.where(routed, 1.0, 0.0)
    copied_f = jnp.where(copied, 1.0, 0.0)
    pick = jnp.where(place_ref[0] == 0, routed_f, copied_f).astype(BF)
    values = jnp.concatenate([fwd_ref[...].astype(F32), bwd_ref[...].astype(F32)], axis=0)
    features = values.shape[1]
    inverse = lax.rsqrt(jnp.mean(values * values, axis=-1, keepdims=True) + EPS)
    normed = (values * inverse * gain_ref[...]).astype(BF)
    for start in range(0, features, CHUNK):
        out_ref[:, start : start + CHUNK] = dot(pick, normed[:, start : start + CHUNK]).astype(BF)
    out_ref[:, features:] = dot(pick, meta.astype(BF)).astype(BF)


def slot_targets(place_ref, rows_ref):
    total = EXPERTS * BOTH
    features = rows_ref.shape[1] - EXTRA
    extra = rows_ref[:, features:].astype(F32)
    row = iota((total, 1), 0)
    part = (
        (row >= BOTH).astype(jnp.int32)
        + (row >= 2 * BOTH).astype(jnp.int32)
        + (row >= 3 * BOTH).astype(jnp.int32)
    )
    place = row - part * BOTH
    on_first = place_ref[0] == 0
    packed = jnp.where(place < SLOTS, part * SLOTS + place, -EXPERTS * LANES)
    found = []
    for k in range(COLS):
        there, high, low = -1, 0.0, 0.0
        if k < 2:
            expert = extra[:, 2 * k : 2 * k + 1].astype(jnp.int32)
            slot = extra[:, 2 * k + 1 : 2 * k + 2].astype(jnp.int32)
            there = expert * LANES + part * SLOTS + slot
            high = extra[:, 4 + 2 * k : 5 + 2 * k]
            low = extra[:, 5 + 2 * k : 6 + 2 * k]
        target = jnp.where(on_first, packed + k * LANES, there)
        found.append((target, jnp.where(on_first, 1.0, high), jnp.where(on_first, 0.0, low)))
    return found


def move(pick_ref, rows_ref, parts, out_refs):
    width = rows_ref.shape[1] - EXTRA
    for start in range(0, width, CHUNK):
        cut = slice(start, start + CHUNK)
        rows = rows_ref[:, cut]
        for part, out_ref in zip(parts, out_refs):
            moved = dot(pick_ref[part * LANES : (part + 1) * LANES, :], rows)
            out_ref[:, cut] = moved[: COLS * SLOTS].astype(BF)


def near_kernel(place_ref, rows_ref, first_ref, third_ref, pick_ref, token_ref):
    token_ref[...] = jnp.zeros_like(token_ref)
    column = iota((EXPERTS * BOTH, EXPERTS * LANES), 1)
    pick = jnp.zeros(column.shape, F32)
    for target, _, _ in slot_targets(place_ref, rows_ref):
        pick = jnp.where(column == target, 1.0, pick)
    pick_ref[...] = pick.T.astype(BF)
    move(pick_ref, rows_ref, (1, 3), (first_ref, third_ref))


def rest_kernel(place_ref, rows_ref, pick_ref, own_ref, back_ref):
    column = iota((EXPERTS * BOTH, EXPERTS * LANES), 1)
    high_m = jnp.zeros(column.shape, F32)
    low_m = jnp.zeros(column.shape, F32)
    for target, high, low in slot_targets(place_ref, rows_ref):
        here = column == target
        high_m = jnp.where(here, high, high_m)
        low_m = jnp.where(here, low, low_m)
    back_ref[:, : EXPERTS * LANES] = high_m.astype(BF)
    back_ref[:, EXPERTS * LANES :] = low_m.astype(BF)
    move(pick_ref, rows_ref, (0,), (own_ref,))


def far_kernel(rows_ref, pick_ref, *refs):
    move(pick_ref, rows_ref, (2,), refs[-1:])


def expert_kernel(count, *refs):
    rows_refs = refs[:count]
    gate_ref, up_ref, down_ref, other_ref = refs[count : count + 4]
    out_refs, token_ref = refs[-1 - count : -1], refs[-1]
    token_ref[...] = jnp.zeros_like(token_ref)
    features, width = gate_ref.shape
    hidden = []
    for rows_ref in rows_refs:
        gate, up = 0.0, 0.0
        for start in range(0, features, WIDE):
            cut = slice(start, start + WIDE)
            more = slice(features + start, features + start + WIDE)
            rows = rows_ref[:, cut]
            gate += dot(rows, jnp.concatenate([gate_ref[cut, :], other_ref[cut, :]], axis=1))
            up += dot(rows, jnp.concatenate([up_ref[cut, :], other_ref[more, :]], axis=1))
        hidden.append((gate / (1.0 + jnp.exp(-gate)) * up).astype(BF))
    for start in range(0, features, CHUNK):
        cut = slice(start, start + CHUNK)
        at = [2 * features + start + i * width for i in range(CHUNK // width)]
        other = jnp.concatenate([other_ref[i : i + width, :] for i in at], axis=1)
        down = jnp.concatenate([down_ref[:, cut], other], axis=0)
        for rows, out_ref in zip(hidden, out_refs):
            out_ref[:, cut] = dot(rows, down).astype(BF)


def gather_kernel(parts, last, back_ref, *refs):
    rows_refs, so_far_ref, out_ref = refs[: len(parts)], refs[len(parts)], refs[-1]
    width = rows_refs[0].shape[1]
    used = COLS * SLOTS
    for start in range(0, width, CHUNK):
        cut = slice(start, min(start + CHUNK, width))
        total = so_far_ref[:, cut] if last else 0.0
        for part, ref in zip(parts, rows_refs):
            high = slice(part * LANES, part * LANES + used)
            low = slice((EXPERTS + part) * LANES, (EXPERTS + part) * LANES + used)
            rows = ref[:, cut]
            total += dot(back_ref[:, high], rows) + dot(back_ref[:, low], rows)
        out_ref[:, cut] = total.astype(out_ref.dtype)


def finish_kernel(place_ref, meta_ref, rows_ref, fwd_ref, bwd_ref, _, of_ref, ob_ref):
    meta = meta_ref[...]
    total = EXPERTS * BOTH
    column = iota((BOTH, total), 1)
    row = iota((BOTH, total), 0)
    high = jnp.zeros((BOTH, total), F32)
    low = jnp.zeros((BOTH, total), F32)
    for k in range(2):
        there = (meta[:, 8 + k : 9 + k] * BOTH + meta[:, 2 * k + 1 : 2 * k + 2]).astype(jnp.int32)
        high = jnp.where(column == there, meta[:, 4 + 2 * k : 5 + 2 * k], high)
        low = jnp.where(column == there, meta[:, 5 + 2 * k : 6 + 2 * k], low)
    same = column == row
    for part in range(1, COLS):
        same = same | (column == row + part * BOTH)
    ones = jnp.where(same, 1.0, 0.0)
    on_first = place_ref[0] == 0
    high = jnp.where(on_first, high, ones).astype(BF)
    low = jnp.where(on_first, low, 0.0).astype(BF)
    width = fwd_ref.shape[1]
    for start in range(0, width, CHUNK):
        cut = slice(start, min(start + CHUNK, width))
        rows = rows_ref[:, cut]
        mixture = dot(high, rows) + dot(low, rows)
        of_ref[:, cut] = (fwd_ref[:, cut].astype(F32) + mixture[:ROWS]).astype(BF)
        ob_ref[:, cut] = (bwd_ref[:, cut].astype(F32) + mixture[ROWS:]).astype(BF)


def ends_kernel(place_ref, left_ref, right_ref, fwd_ref, bwd_ref, out_ref):
    count, _, part = out_ref.shape
    at_start = place_ref[2] == 0
    for r in range(count):
        near, far = [slice(j * part, (j + 1) * part) for j in (r, 2 * count - 1 - r)]

        @pl.when(at_start)
        def _():
            out_ref[r, :ROWS, :] = left_ref[:, near]
            out_ref[r, ROWS:, :] = bwd_ref[:, near]

        @pl.when(jnp.logical_not(at_start))
        def _():
            out_ref[r, :ROWS, :] = fwd_ref[:, far]
            out_ref[r, ROWS:, :] = right_ref[:, far]


def entered_kernel(place_ref, held_ref, got_ref, out_ref):
    count, _, part = held_ref.shape
    at_start = place_ref[2] == 0
    for r in range(count):
        near, far = [slice(j * part, (j + 1) * part) for j in (r, 2 * count - 1 - r)]

        @pl.when(at_start)
        def _():
            out_ref[:, near] = held_ref[r, :ROWS, :]
            out_ref[:, far] = got_ref[r]

        @pl.when(jnp.logical_not(at_start))
        def _():
            out_ref[:, near] = got_ref[r]
            out_ref[:, far] = held_ref[r, ROWS:, :]


SMEM = pl.BlockSpec(memory_space=pltpu.SMEM)


def params(mib=20):
    return pltpu.CompilerParams(vmem_limit_bytes=mib * 1024 * 1024)


VMEM = pl.BlockSpec(memory_space=pltpu.VMEM)
ANY = pl.BlockSpec(memory_space=pl.ANY)


def shape(rows, columns, dtype=BF):
    return jax.ShapeDtypeStruct((rows, columns), dtype)


def make_send(place, fwd, bwd, gain, ids, gates):
    features = fwd.shape[1]
    return pl.pallas_call(
        send_kernel,
        out_shape=(shape(EXPERTS * BOTH, features + EXTRA), shape(BOTH, EXTRA, F32)),
        in_specs=[SMEM] + [VMEM] * 5,
        out_specs=(VMEM, VMEM),
        compiler_params=params(),
        name="normed",
    )(place, fwd, bwd, gain, ids, gates)


def make_near(place, rows):
    features = rows.shape[1] - EXTRA
    total = EXPERTS * BOTH
    return pl.pallas_call(
        near_kernel,
        out_shape=(shape(COLS * SLOTS, features),) * 2
        + (shape(EXPERTS * LANES, total), shape(8, LANES, jnp.int32)),
        in_specs=[SMEM, VMEM],
        out_specs=(VMEM,) * 4,
        compiler_params=params(),
        name="near",
    )(place, rows)


def pack_kernel(gate_ref, up_ref, down_ref, _, out_ref):
    features, width = gate_ref.shape
    out_ref[:features, :] = gate_ref[...]
    out_ref[features : 2 * features, :] = up_ref[...]
    for i in range(features // width):
        at = 2 * features + i * width
        out_ref[at : at + width, :] = down_ref[:, i * width : (i + 1) * width]


def make_pack(gate, up, down, before):
    features, width = gate.shape
    return pl.pallas_call(
        pack_kernel,
        out_shape=shape(3 * features, width),
        in_specs=[VMEM] * 3 + [ANY],
        out_specs=VMEM,
        compiler_params=params(),
        name="pack",
    )(gate, up, down, before)


def make_rest(place, rows, pick):
    features = rows.shape[1] - EXTRA
    return pl.pallas_call(
        rest_kernel,
        out_shape=(
            shape(COLS * SLOTS, features),
            shape(EXPERTS * BOTH, 2 * EXPERTS * LANES),
        ),
        in_specs=[SMEM, VMEM, VMEM],
        out_specs=(VMEM, VMEM),
        compiler_params=params(),
        name="rest",
    )(place, rows, pick)


def make_far(rows, pick, *before):
    return pl.pallas_call(
        far_kernel,
        out_shape=shape(COLS * SLOTS, rows.shape[1] - EXTRA),
        in_specs=[VMEM, VMEM] + [ANY] * len(before),
        out_specs=VMEM,
        compiler_params=params(),
        name="far",
    )(rows, pick, *before)


def run_experts(blocks, own, packed, *before):
    count = len(blocks)

    def body(*refs):
        expert_kernel(count, *refs)

    return pl.pallas_call(
        body,
        out_shape=(shape(*blocks[0].shape),) * count + (shape(8, LANES, jnp.int32),),
        in_specs=[VMEM] * (count + 4) + [ANY] * len(before),
        out_specs=(VMEM,) * (count + 1),
        compiler_params=params(),
        name="experts",
    )(*blocks, *own, packed, *before)


def make_gather(back, blocks, parts, so_far=None, before=()):
    features = blocks[0].shape[1]
    total = back.shape[0]
    last = so_far is not None

    def body(*refs):
        gather_kernel(parts, last, *refs)

    return pl.pallas_call(
        body,
        out_shape=shape(total, features, BF if last else F32),
        in_specs=[VMEM] * (1 + len(blocks) + last) + [ANY] * len(before),
        out_specs=VMEM,
        compiler_params=params(),
        name="gather",
    )(back, *blocks, *([so_far] if last else []), *before)


def make_finish(place, meta, rows, fwd, bwd, before):
    features = fwd.shape[1]
    return pl.pallas_call(
        finish_kernel,
        out_shape=(shape(ROWS, features),) * 2,
        in_specs=[SMEM] + [VMEM] * 4 + [ANY],
        out_specs=(VMEM,) * 2,
        compiler_params=params(),
        name="finish",
    )(place, meta, rows, fwd, bwd, before)


def make_simple(kernel, out, place, *arrays):
    return pl.pallas_call(
        kernel,
        out_shape=jax.ShapeDtypeStruct(out, BF),
        in_specs=[SMEM] + [VMEM] * len(arrays),
        out_specs=VMEM,
        compiler_params=params(),
        name="blocks",
    )(place, *arrays)


def shifted(block, distance, count):
    return lax.ppermute(block, "pp", [(i, (i + distance) % count) for i in range(count)])


def mirrored(pairs, sections):
    return pairs + [(sections - 1 - i, sections - 1 - j) for i, j in pairs]


def from_other_core(block):
    return lax.ppermute(block, "ep", [(i, i ^ 1) for i in range(lax.axis_size("ep"))])


def inward(held, step, sections):
    bit = 1 << step
    pairs = [(i, i - bit) for i in range(bit, sections // 2, 2 * bit)]
    got = lax.ppermute(held, "pp", mirrored(pairs, sections))
    return jnp.concatenate([held, got], axis=0), got


def outward(own, place, sections):
    def move(block, *pairs):
        return lax.ppermute(block, "pp", mirrored(list(pairs), sections))

    a = move(own[2:8], (0, 2))
    b = move(jnp.where(place == 0, own[1:5], a[2:6]), (0, 1), (2, 4))
    c = move(jnp.where(place == 2, a[1:3], b[2:4]), (2, 3), (4, 6))
    d = move(jnp.where(place == 4, b[1:2], c[1:2]), (4, 5), (6, 7))
    mine = own[0]
    for at, block in ((1, b), (2, a), (3, c), (4, b), (5, d), (6, c), (7, d)):
        mine = jnp.where(place == at, block[0], mine)
    return mine


def body(
    state_fwd,
    state_bwd,
    enter_fwd,
    enter_bwd,
    norm_gain,
    w_gate,
    w_up,
    w_down,
    route_ids,
    route_gates,
):
    sections = lax.axis_size("pp")
    section = lax.axis_index("pp")
    position = lax.axis_index("ep")
    place = jnp.stack([position % 2, position // (2 * COLS), section]).astype(jnp.int32)
    fwd, bwd = state_fwd[0], state_bwd[0]
    features = fwd.shape[1]
    part = features // sections
    ids = route_ids[0, 0].transpose(0, 2, 1)
    gates = route_gates[0, 0].transpose(0, 2, 1)

    sent, meta = make_send(place, fwd, bwd, norm_gain, ids, gates)
    rows = exchange(sent)
    send1, send3, pick, token = make_near(place, rows)
    near, far = hop(send1, 1), hop(send3, 3)
    own = (w_gate[0], w_up[0], w_down[0])
    weights = own, from_other_core(make_pack(*own, pick))
    send0, back = make_rest(place, rows, pick)
    last = hop(make_far(rows, pick, near, far, back), 2)

    half = sections // 2
    at_start = section == 0
    entering = jnp.concatenate([enter_fwd, enter_bwd], axis=1)
    held, got = inward(entering, 0, sections)
    done0, done1, done3, token = run_experts([send0, near, far], *weights)
    back1, back3 = hop(done1, -1), hop(done3, -3)
    done2, token = run_experts([last], *weights, token)
    back2 = hop(done2, -2)
    held, got0 = inward(held, 1, sections)
    held, got = inward(held, 2, sections)
    begun = make_gather(back, [done0, back1, back3], (0, 1, 3))
    gathered = make_gather(back, [back2], (2,), begun, (got,))
    passed_on = jnp.where(at_start, held[:, ROWS:], held[:, :ROWS])
    got = lax.ppermute(passed_on, "pp", [(0, sections - 1), (sections - 1, 0)])
    entered = make_simple(entered_kernel, (ROWS, features), place, held, got)
    fwd_out, bwd_out = make_finish(place, meta, exchange(gathered), fwd, bwd, entered)
    from_left, from_right = shifted(fwd_out, 1, sections), shifted(bwd_out, -1, sections)
    ends = make_simple(
        ends_kernel, (half, BOTH, part), place, from_left, from_right, fwd_out, bwd_out
    )
    mine = outward(ends, jnp.minimum(section, sections - 1 - section), sections)
    fwd_next = jnp.where(at_start, entered, from_left)
    bwd_next = jnp.where(section == sections - 1, entered, from_right)
    return (fwd_next[None], bwd_next[None], mine[None, :ROWS], mine[None, ROWS:])


def solution(mesh):
    placed = (
        P("pp", "ep", None),
        P("pp", "ep", None),
        P(None, "ep", "pp"),
        P(None, "ep", "pp"),
        P("pp", None),
        P("pp", None, "ep"),
        P("pp", None, "ep"),
        P("pp", "ep", None),
        P("pp", None, None, "ep", None),
        P("pp", None, None, "ep", None),
    )
    return jax.shard_map(
        body,
        mesh=mesh,
        in_specs=placed,
        out_specs=(
            P("pp", "ep", None),
            P("pp", "ep", None),
            P(None, "ep", "pp"),
            P(None, "ep", "pp"),
        ),
        check_vma=False,
    )
```

```python
import jax
import jax.numpy as jnp
from jax import lax
from jax.experimental import pallas as pl
from jax.experimental.pallas import tpu as pltpu
from jax.sharding import PartitionSpec as P

EPS = 1e-06
BF = jnp.bfloat16
F32 = jnp.float32
EXPERTS = 4
COLS = 4
CAP = 15
ROWS = 24
BOTH = 2 * ROWS
SLOTS = 2 * CAP
EXTRA = 128
WIDE = 1792
CHUNK = 512
LANES = 128


def device(y, x, core):
    return (y * COLS + x) * 2 + core


def hop(block, distance):
    route = []
    for y in range(EXPERTS):
        for x in range(COLS):
            for core in range(2):
                along_y = core == 1
                there = ((y + distance) % EXPERTS, x) if along_y else (y, (x + distance) % COLS)
                route.append((device(y, x, core), device(*there, core)))
    return lax.ppermute(block, "ep", route)


def rings(along_y):
    groups = []
    for core in range(2):
        if (core == 0) == along_y:
            groups += [[device(y, x, core) for y in range(EXPERTS)] for x in range(COLS)]
        else:
            groups += [[device(y, x, core) for x in range(COLS)] for y in range(EXPERTS)]
    return groups


def exchange(rows):
    return lax.all_to_all(
        rows, "ep", split_axis=0, concat_axis=0, axis_index_groups=rings(True), tiled=True
    )


def iota(shape, dim):
    return lax.broadcasted_iota(jnp.int32, shape, dim)


def dot(a, b):
    return jnp.dot(a, b, preferred_element_type=F32)


def split_gate(gate):
    high = gate.astype(BF).astype(F32)
    return high, (gate - high).astype(BF).astype(F32)


def send_kernel(place_ref, fwd_ref, bwd_ref, gain_ref, ids_ref, gates_ref, out_ref, meta_ref):
    lanes = iota((BOTH, EXTRA), 1)
    row = iota((BOTH, EXTRA), 0)
    in_fwd = row < ROWS
    own = lanes[:, :ROWS] == row[:, :ROWS] - jnp.where(in_fwd[:, :ROWS], 0, ROWS)

    def column(ref, k):
        both = jnp.where(in_fwd[:, :ROWS], ref[0, k : k + 1, :], ref[1, k : k + 1, :])
        return jnp.sum(jnp.where(own, both, jnp.zeros_like(both)), axis=1, keepdims=True)

    first, second = column(ids_ref, 0), column(ids_ref, 1)
    named = jnp.where((lanes == first) | (lanes == second), 1.0, 0.0)
    r0, r1 = iota((BOTH, BOTH), 0), iota((BOTH, BOTH), 1)
    earlier = jnp.where((r1 < r0) & ((r1 < ROWS) == (r0 < ROWS)), 1.0, 0.0)
    rank = dot(earlier.astype(BF), named.astype(BF))
    offset = jnp.where(in_fwd[:, 0:1], 0, CAP)
    slots = []
    for chosen in (first, second):
        taken = jnp.sum(jnp.where(lanes == chosen, rank, 0.0), axis=1, keepdims=True)
        slots.append(taken.astype(jnp.int32) + offset)
    ahead = [
        jnp.bitwise_and(chosen - place_ref[1] + EXPERTS, EXPERTS - 1) for chosen in (first, second)
    ]
    fields = [ahead[0].astype(F32), slots[0].astype(F32), ahead[1].astype(F32), slots[1].astype(F32)]
    fields += split_gate(column(gates_ref, 0))
    fields += split_gate(column(gates_ref, 1))
    fields += [first.astype(F32), second.astype(F32)]
    meta = jnp.zeros((BOTH, EXTRA), F32)
    for place, field in enumerate(fields):
        meta = jnp.where(lanes == place, field, meta)
    meta_ref[...] = meta

    def as_row(column):
        return jnp.sum(jnp.where(r0 == r1, column, 0), axis=0, keepdims=True)

    target = iota((EXPERTS * BOTH, BOTH), 0)
    source = iota((EXPERTS * BOTH, BOTH), 1)
    routed = (target == as_row(first * BOTH + slots[0])) | (
        target == as_row(second * BOTH + slots[1])
    )
    copied = target == source
    for part in range(1, COLS):
        copied = copied | (target == source + part * BOTH)
    routed_f = jnp.where(routed, 1.0, 0.0)
    copied_f = jnp.where(copied, 1.0, 0.0)
    pick = jnp.where(place_ref[0] == 0, routed_f, copied_f).astype(BF)
    values = jnp.concatenate([fwd_ref[...].astype(F32), bwd_ref[...].astype(F32)], axis=0)
    features = values.shape[1]
    inverse = lax.rsqrt(jnp.mean(values * values, axis=-1, keepdims=True) + EPS)
    normed = (values * inverse * gain_ref[...]).astype(BF)
    for start in range(0, features, CHUNK):
        out_ref[:, start : start + CHUNK] = dot(pick, normed[:, start : start + CHUNK]).astype(BF)
    out_ref[:, features:] = dot(pick, meta.astype(BF)).astype(BF)


def slot_targets(place_ref, rows_ref):
    total = EXPERTS * BOTH
    features = rows_ref.shape[1] - EXTRA
    extra = rows_ref[:, features:].astype(F32)
    row = iota((total, 1), 0)
    part = (
        (row >= BOTH).astype(jnp.int32)
        + (row >= 2 * BOTH).astype(jnp.int32)
        + (row >= 3 * BOTH).astype(jnp.int32)
    )
    place = row - part * BOTH
    on_first = place_ref[0] == 0
    packed = jnp.where(place < SLOTS, part * SLOTS + place, -EXPERTS * LANES)
    found = []
    for k in range(COLS):
        there, high, low = -1, 0.0, 0.0
        if k < 2:
            expert = extra[:, 2 * k : 2 * k + 1].astype(jnp.int32)
            slot = extra[:, 2 * k + 1 : 2 * k + 2].astype(jnp.int32)
            there = expert * LANES + part * SLOTS + slot
            high = extra[:, 4 + 2 * k : 5 + 2 * k]
            low = extra[:, 5 + 2 * k : 6 + 2 * k]
        target = jnp.where(on_first, packed + k * LANES, there)
        found.append((target, jnp.where(on_first, 1.0, high), jnp.where(on_first, 0.0, low)))
    return found


def move(pick_ref, rows_ref, parts, out_refs):
    width = rows_ref.shape[1] - EXTRA
    for start in range(0, width, CHUNK):
        cut = slice(start, start + CHUNK)
        rows = rows_ref[:, cut]
        for part, out_ref in zip(parts, out_refs):
            moved = dot(pick_ref[part * LANES : (part + 1) * LANES, :], rows)
            out_ref[:, cut] = moved[: COLS * SLOTS].astype(BF)


def near_kernel(place_ref, rows_ref, first_ref, third_ref, pick_ref, token_ref):
    token_ref[...] = jnp.zeros_like(token_ref)
    column = iota((EXPERTS * BOTH, EXPERTS * LANES), 1)
    pick = jnp.zeros(column.shape, F32)
    for target, _, _ in slot_targets(place_ref, rows_ref):
        pick = jnp.where(column == target, 1.0, pick)
    pick_ref[...] = pick.T.astype(BF)
    move(pick_ref, rows_ref, (1, 3), (first_ref, third_ref))


def rest_kernel(place_ref, rows_ref, pick_ref, own_ref, back_ref):
    column = iota((EXPERTS * BOTH, EXPERTS * LANES), 1)
    high_m = jnp.zeros(column.shape, F32)
    low_m = jnp.zeros(column.shape, F32)
    for target, high, low in slot_targets(place_ref, rows_ref):
        here = column == target
        high_m = jnp.where(here, high, high_m)
        low_m = jnp.where(here, low, low_m)
    back_ref[:, : EXPERTS * LANES] = high_m.astype(BF)
    back_ref[:, EXPERTS * LANES :] = low_m.astype(BF)
    move(pick_ref, rows_ref, (0,), (own_ref,))


def far_kernel(rows_ref, pick_ref, *refs):
    move(pick_ref, rows_ref, (2,), refs[-1:])


def expert_kernel(count, *refs):
    rows_refs = refs[:count]
    gate_ref, up_ref, down_ref, other_ref = refs[count : count + 4]
    out_refs, token_ref = refs[-1 - count : -1], refs[-1]
    token_ref[...] = jnp.zeros_like(token_ref)
    features, width = gate_ref.shape
    hidden = []
    for rows_ref in rows_refs:
        gate, up = 0.0, 0.0
        for start in range(0, features, WIDE):
            cut = slice(start, start + WIDE)
            more = slice(features + start, features + start + WIDE)
            rows = rows_ref[:, cut]
            gate += dot(rows, jnp.concatenate([gate_ref[cut, :], other_ref[cut, :]], axis=1))
            up += dot(rows, jnp.concatenate([up_ref[cut, :], other_ref[more, :]], axis=1))
        hidden.append((gate / (1.0 + jnp.exp(-gate)) * up).astype(BF))
    for start in range(0, features, CHUNK):
        cut = slice(start, start + CHUNK)
        at = [2 * features + start + i * width for i in range(CHUNK // width)]
        other = jnp.concatenate([other_ref[i : i + width, :] for i in at], axis=1)
        down = jnp.concatenate([down_ref[:, cut], other], axis=0)
        for rows, out_ref in zip(hidden, out_refs):
            out_ref[:, cut] = dot(rows, down).astype(BF)


def gather_kernel(parts, last, back_ref, *refs):
    rows_refs, so_far_ref, out_ref = refs[: len(parts)], refs[len(parts)], refs[-1]
    width = rows_refs[0].shape[1]
    used = COLS * SLOTS
    for start in range(0, width, CHUNK):
        cut = slice(start, min(start + CHUNK, width))
        total = so_far_ref[:, cut] if last else 0.0
        for part, ref in zip(parts, rows_refs):
            high = slice(part * LANES, part * LANES + used)
            low = slice((EXPERTS + part) * LANES, (EXPERTS + part) * LANES + used)
            rows = ref[:, cut]
            total += dot(back_ref[:, high], rows) + dot(back_ref[:, low], rows)
        out_ref[:, cut] = total.astype(out_ref.dtype)


def finish_kernel(place_ref, meta_ref, rows_ref, fwd_ref, bwd_ref, of_ref, ob_ref):
    meta = meta_ref[...]
    total = EXPERTS * BOTH
    column = iota((BOTH, total), 1)
    row = iota((BOTH, total), 0)
    high = jnp.zeros((BOTH, total), F32)
    low = jnp.zeros((BOTH, total), F32)
    for k in range(2):
        there = (meta[:, 8 + k : 9 + k] * BOTH + meta[:, 2 * k + 1 : 2 * k + 2]).astype(jnp.int32)
        high = jnp.where(column == there, meta[:, 4 + 2 * k : 5 + 2 * k], high)
        low = jnp.where(column == there, meta[:, 5 + 2 * k : 6 + 2 * k], low)
    same = column == row
    for part in range(1, COLS):
        same = same | (column == row + part * BOTH)
    ones = jnp.where(same, 1.0, 0.0)
    on_first = place_ref[0] == 0
    high = jnp.where(on_first, high, ones).astype(BF)
    low = jnp.where(on_first, low, 0.0).astype(BF)
    width = fwd_ref.shape[1]
    for start in range(0, width, CHUNK):
        cut = slice(start, min(start + CHUNK, width))
        rows = rows_ref[:, cut]
        mixture = dot(high, rows) + dot(low, rows)
        of_ref[:, cut] = (fwd_ref[:, cut].astype(F32) + mixture[:ROWS]).astype(BF)
        ob_ref[:, cut] = (bwd_ref[:, cut].astype(F32) + mixture[ROWS:]).astype(BF)


def ends_kernel(place_ref, left_ref, right_ref, fwd_ref, bwd_ref, out_ref):
    count, _, part = out_ref.shape
    at_start = place_ref[2] == 0
    for r in range(count):
        near, far = [slice(j * part, (j + 1) * part) for j in (r, 2 * count - 1 - r)]

        @pl.when(at_start)
        def _():
            out_ref[r, :ROWS, :] = left_ref[:, near]
            out_ref[r, ROWS:, :] = bwd_ref[:, near]

        @pl.when(jnp.logical_not(at_start))
        def _():
            out_ref[r, :ROWS, :] = fwd_ref[:, far]
            out_ref[r, ROWS:, :] = right_ref[:, far]


def entered_kernel(place_ref, held_ref, got_ref, out_ref):
    count, _, part = held_ref.shape
    at_start = place_ref[2] == 0
    for r in range(count):
        near, far = [slice(j * part, (j + 1) * part) for j in (r, 2 * count - 1 - r)]

        @pl.when(at_start)
        def _():
            out_ref[:, near] = held_ref[r, :ROWS, :]
            out_ref[:, far] = got_ref[r]

        @pl.when(jnp.logical_not(at_start))
        def _():
            out_ref[:, near] = got_ref[r]
            out_ref[:, far] = held_ref[r, ROWS:, :]


SMEM = pl.BlockSpec(memory_space=pltpu.SMEM)


def params(mib=20):
    return pltpu.CompilerParams(vmem_limit_bytes=mib * 1024 * 1024)


VMEM = pl.BlockSpec(memory_space=pltpu.VMEM)
ANY = pl.BlockSpec(memory_space=pl.ANY)


def shape(rows, columns, dtype=BF):
    return jax.ShapeDtypeStruct((rows, columns), dtype)


def make_send(place, fwd, bwd, gain, ids, gates):
    features = fwd.shape[1]
    return pl.pallas_call(
        send_kernel,
        out_shape=(shape(EXPERTS * BOTH, features + EXTRA), shape(BOTH, EXTRA, F32)),
        in_specs=[SMEM] + [VMEM] * 5,
        out_specs=(VMEM, VMEM),
        compiler_params=params(),
        name="normed",
    )(place, fwd, bwd, gain, ids, gates)


def make_near(place, rows):
    features = rows.shape[1] - EXTRA
    total = EXPERTS * BOTH
    return pl.pallas_call(
        near_kernel,
        out_shape=(shape(COLS * SLOTS, features),) * 2
        + (shape(EXPERTS * LANES, total), shape(8, LANES, jnp.int32)),
        in_specs=[SMEM, VMEM],
        out_specs=(VMEM,) * 4,
        compiler_params=params(),
        name="near",
    )(place, rows)


def pack_kernel(gate_ref, up_ref, down_ref, _, out_ref):
    features, width = gate_ref.shape
    out_ref[:features, :] = gate_ref[...]
    out_ref[features : 2 * features, :] = up_ref[...]
    for i in range(features // width):
        at = 2 * features + i * width
        out_ref[at : at + width, :] = down_ref[:, i * width : (i + 1) * width]


def make_pack(gate, up, down, before):
    features, width = gate.shape
    return pl.pallas_call(
        pack_kernel,
        out_shape=shape(3 * features, width),
        in_specs=[VMEM] * 3 + [ANY],
        out_specs=VMEM,
        compiler_params=params(),
        name="pack",
    )(gate, up, down, before)


def make_rest(place, rows, pick):
    features = rows.shape[1] - EXTRA
    return pl.pallas_call(
        rest_kernel,
        out_shape=(
            shape(COLS * SLOTS, features),
            shape(EXPERTS * BOTH, 2 * EXPERTS * LANES),
        ),
        in_specs=[SMEM, VMEM, VMEM],
        out_specs=(VMEM, VMEM),
        compiler_params=params(),
        name="rest",
    )(place, rows, pick)


def make_far(rows, pick, *before):
    return pl.pallas_call(
        far_kernel,
        out_shape=shape(COLS * SLOTS, rows.shape[1] - EXTRA),
        in_specs=[VMEM, VMEM] + [ANY] * len(before),
        out_specs=VMEM,
        compiler_params=params(),
        name="far",
    )(rows, pick, *before)


def run_experts(blocks, own, packed, *before):
    count = len(blocks)

    def body(*refs):
        expert_kernel(count, *refs)

    return pl.pallas_call(
        body,
        out_shape=(shape(*blocks[0].shape),) * count + (shape(8, LANES, jnp.int32),),
        in_specs=[VMEM] * (count + 4) + [ANY] * len(before),
        out_specs=(VMEM,) * (count + 1),
        compiler_params=params(),
        name="experts",
    )(*blocks, *own, packed, *before)


def make_gather(back, blocks, parts, so_far=None, before=()):
    features = blocks[0].shape[1]
    total = back.shape[0]
    last = so_far is not None

    def body(*refs):
        gather_kernel(parts, last, *refs)

    return pl.pallas_call(
        body,
        out_shape=shape(total, features, BF if last else F32),
        in_specs=[VMEM] * (1 + len(blocks) + last) + [ANY] * len(before),
        out_specs=VMEM,
        compiler_params=params(),
        name="gather",
    )(back, *blocks, *([so_far] if last else []), *before)


def make_finish(place, meta, rows, fwd, bwd):
    features = fwd.shape[1]
    return pl.pallas_call(
        finish_kernel,
        out_shape=(shape(ROWS, features),) * 2,
        in_specs=[SMEM] + [VMEM] * 4,
        out_specs=(VMEM,) * 2,
        compiler_params=params(),
        name="finish",
    )(place, meta, rows, fwd, bwd)


def make_simple(kernel, out, place, *arrays):
    return pl.pallas_call(
        kernel,
        out_shape=jax.ShapeDtypeStruct(out, BF),
        in_specs=[SMEM] + [VMEM] * len(arrays),
        out_specs=VMEM,
        compiler_params=params(),
        name="blocks",
    )(place, *arrays)


def shifted(block, distance, count):
    return lax.ppermute(block, "pp", [(i, (i + distance) % count) for i in range(count)])


def mirrored(pairs, sections):
    return pairs + [(sections - 1 - i, sections - 1 - j) for i, j in pairs]


def from_other_core(block):
    return lax.ppermute(block, "ep", [(i, i ^ 1) for i in range(lax.axis_size("ep"))])


def inward(held, step, sections):
    bit = 1 << step
    pairs = [(i, i - bit) for i in range(bit, sections // 2, 2 * bit)]
    got = lax.ppermute(held, "pp", mirrored(pairs, sections))
    return jnp.concatenate([held, got], axis=0), got


def outward(own, place, sections):
    def move(block, *pairs):
        return lax.ppermute(block, "pp", mirrored(list(pairs), sections))

    a = move(own[4:8], (0, 4))
    b = move(jnp.where(place == 0, own[2:4], a[2:4]), (0, 2), (4, 6))
    c = jnp.where(place == 0, own[1:2], jnp.where(place == 4, a[1:2], b[1:2]))
    c = move(c, (0, 1), (2, 3), (4, 5), (6, 7))
    mine = jnp.where(place == 0, own[0], jnp.where(place == 4, a[0], b[0]))
    return jnp.where((place & 1) == 1, c[0], mine)


def body(
    state_fwd,
    state_bwd,
    enter_fwd,
    enter_bwd,
    norm_gain,
    w_gate,
    w_up,
    w_down,
    route_ids,
    route_gates,
):
    sections = lax.axis_size("pp")
    section = lax.axis_index("pp")
    position = lax.axis_index("ep")
    place = jnp.stack([position % 2, position // (2 * COLS), section]).astype(jnp.int32)
    fwd, bwd = state_fwd[0], state_bwd[0]
    features = fwd.shape[1]
    part = features // sections
    ids = route_ids[0, 0].transpose(0, 2, 1)
    gates = route_gates[0, 0].transpose(0, 2, 1)

    sent, meta = make_send(place, fwd, bwd, norm_gain, ids, gates)
    rows = exchange(sent)
    send1, send3, pick, token = make_near(place, rows)
    near, far = hop(send1, 1), hop(send3, 3)
    own = (w_gate[0], w_up[0], w_down[0])
    weights = own, from_other_core(make_pack(*own, pick))
    send0, back = make_rest(place, rows, pick)
    last = hop(make_far(rows, pick, near, far, back), 2)

    half = sections // 2
    at_start = section == 0
    entering = jnp.concatenate([enter_fwd, enter_bwd], axis=1)
    held, got = inward(entering, 0, sections)
    done0, done1, done3, token = run_experts([send0, near, far], *weights)
    back1, back3 = hop(done1, -1), hop(done3, -3)
    done2, token = run_experts([last], *weights, token)
    back2 = hop(done2, -2)
    held, got = inward(held, 1, sections)
    begun = make_gather(back, [done0, back1, back3], (0, 1, 3))
    gathered = make_gather(back, [back2], (2,), begun, (got,))
    held, _ = inward(held, 2, sections)
    passed_on = jnp.where(at_start, held[:, ROWS:], held[:, :ROWS])
    got = lax.ppermute(passed_on, "pp", [(0, sections - 1), (sections - 1, 0)])
    entered = make_simple(entered_kernel, (ROWS, features), place, held, got)
    fwd_out, bwd_out = make_finish(place, meta, exchange(gathered), fwd, bwd)
    from_left, from_right = shifted(fwd_out, 1, sections), shifted(bwd_out, -1, sections)
    ends = make_simple(
        ends_kernel, (half, BOTH, part), place, from_left, from_right, fwd_out, bwd_out
    )
    mine = outward(ends, jnp.minimum(section, sections - 1 - section), sections)
    fwd_next = jnp.where(at_start, entered, from_left)
    bwd_next = jnp.where(section == sections - 1, entered, from_right)
    return (fwd_next[None], bwd_next[None], mine[None, :ROWS], mine[None, ROWS:])


def solution(mesh):
    placed = (
        P("pp", "ep", None),
        P("pp", "ep", None),
        P(None, "ep", "pp"),
        P(None, "ep", "pp"),
        P("pp", None),
        P("pp", None, "ep"),
        P("pp", None, "ep"),
        P("pp", "ep", None),
        P("pp", None, None, "ep", None),
        P("pp", None, None, "ep", None),
    )
    return jax.shard_map(
        body,
        mesh=mesh,
        in_specs=placed,
        out_specs=(
            P("pp", "ep", None),
            P("pp", "ep", None),
            P(None, "ep", "pp"),
            P(None, "ep", "pp"),
        ),
        check_vma=False,
    )
```

```python
import jax
import jax.numpy as jnp
from jax import lax
from jax.experimental import pallas as pl
from jax.experimental.pallas import tpu as pltpu
from jax.sharding import PartitionSpec as P

EPS = 1e-06
BF = jnp.bfloat16
F32 = jnp.float32
EXPERTS = 4
COLS = 4
CAP = 15
ROWS = 24
BOTH = 2 * ROWS
SLOTS = 2 * CAP
EXTRA = 128
WIDE = 1792
CHUNK = 512
LANES = 128


def device(y, x, core):
    return (y * COLS + x) * 2 + core


def hop(block, distance):
    route = []
    for y in range(EXPERTS):
        for x in range(COLS):
            for core in range(2):
                along_y = core == 1
                there = ((y + distance) % EXPERTS, x) if along_y else (y, (x + distance) % COLS)
                route.append((device(y, x, core), device(*there, core)))
    return lax.ppermute(block, "ep", route)


def rings(along_y):
    groups = []
    for core in range(2):
        if (core == 0) == along_y:
            groups += [[device(y, x, core) for y in range(EXPERTS)] for x in range(COLS)]
        else:
            groups += [[device(y, x, core) for x in range(COLS)] for y in range(EXPERTS)]
    return groups


def exchange(rows):
    return lax.all_to_all(
        rows, "ep", split_axis=0, concat_axis=0, axis_index_groups=rings(True), tiled=True
    )


def iota(shape, dim):
    return lax.broadcasted_iota(jnp.int32, shape, dim)


def dot(a, b):
    return jnp.dot(a, b, preferred_element_type=F32)


def split_gate(gate):
    high = gate.astype(BF).astype(F32)
    return high, (gate - high).astype(BF).astype(F32)


def send_kernel(place_ref, fwd_ref, bwd_ref, gain_ref, ids_ref, gates_ref, out_ref, meta_ref):
    lanes = iota((BOTH, EXTRA), 1)
    row = iota((BOTH, EXTRA), 0)
    in_fwd = row < ROWS
    own = lanes[:, :ROWS] == row[:, :ROWS] - jnp.where(in_fwd[:, :ROWS], 0, ROWS)

    def column(ref, k):
        both = jnp.where(in_fwd[:, :ROWS], ref[0, k : k + 1, :], ref[1, k : k + 1, :])
        return jnp.sum(jnp.where(own, both, jnp.zeros_like(both)), axis=1, keepdims=True)

    first, second = column(ids_ref, 0), column(ids_ref, 1)
    named = jnp.where((lanes == first) | (lanes == second), 1.0, 0.0)
    r0, r1 = iota((BOTH, BOTH), 0), iota((BOTH, BOTH), 1)
    earlier = jnp.where((r1 < r0) & ((r1 < ROWS) == (r0 < ROWS)), 1.0, 0.0)
    rank = dot(earlier.astype(BF), named.astype(BF))
    offset = jnp.where(in_fwd[:, 0:1], 0, CAP)
    slots = []
    for chosen in (first, second):
        taken = jnp.sum(jnp.where(lanes == chosen, rank, 0.0), axis=1, keepdims=True)
        slots.append(taken.astype(jnp.int32) + offset)
    ahead = [
        jnp.bitwise_and(chosen - place_ref[1] + EXPERTS, EXPERTS - 1) for chosen in (first, second)
    ]
    fields = [ahead[0].astype(F32), slots[0].astype(F32), ahead[1].astype(F32), slots[1].astype(F32)]
    fields += split_gate(column(gates_ref, 0))
    fields += split_gate(column(gates_ref, 1))
    fields += [first.astype(F32), second.astype(F32)]
    meta = jnp.zeros((BOTH, EXTRA), F32)
    for place, field in enumerate(fields):
        meta = jnp.where(lanes == place, field, meta)
    meta_ref[...] = meta

    def as_row(column):
        return jnp.sum(jnp.where(r0 == r1, column, 0), axis=0, keepdims=True)

    target = iota((EXPERTS * BOTH, BOTH), 0)
    source = iota((EXPERTS * BOTH, BOTH), 1)
    routed = (target == as_row(first * BOTH + slots[0])) | (
        target == as_row(second * BOTH + slots[1])
    )
    copied = target == source
    for part in range(1, COLS):
        copied = copied | (target == source + part * BOTH)
    routed_f = jnp.where(routed, 1.0, 0.0)
    copied_f = jnp.where(copied, 1.0, 0.0)
    pick = jnp.where(place_ref[0] == 0, routed_f, copied_f).astype(BF)
    values = jnp.concatenate([fwd_ref[...].astype(F32), bwd_ref[...].astype(F32)], axis=0)
    features = values.shape[1]
    inverse = lax.rsqrt(jnp.mean(values * values, axis=-1, keepdims=True) + EPS)
    normed = (values * inverse * gain_ref[...]).astype(BF)
    for start in range(0, features, CHUNK):
        out_ref[:, start : start + CHUNK] = dot(pick, normed[:, start : start + CHUNK]).astype(BF)
    out_ref[:, features:] = dot(pick, meta.astype(BF)).astype(BF)


def slot_targets(place_ref, rows_ref):
    total = EXPERTS * BOTH
    features = rows_ref.shape[1] - EXTRA
    extra = rows_ref[:, features:].astype(F32)
    row = iota((total, 1), 0)
    part = (
        (row >= BOTH).astype(jnp.int32)
        + (row >= 2 * BOTH).astype(jnp.int32)
        + (row >= 3 * BOTH).astype(jnp.int32)
    )
    place = row - part * BOTH
    on_first = place_ref[0] == 0
    packed = jnp.where(place < SLOTS, part * SLOTS + place, -EXPERTS * LANES)
    found = []
    for k in range(COLS):
        there, high, low = -1, 0.0, 0.0
        if k < 2:
            expert = extra[:, 2 * k : 2 * k + 1].astype(jnp.int32)
            slot = extra[:, 2 * k + 1 : 2 * k + 2].astype(jnp.int32)
            there = expert * LANES + part * SLOTS + slot
            high = extra[:, 4 + 2 * k : 5 + 2 * k]
            low = extra[:, 5 + 2 * k : 6 + 2 * k]
        target = jnp.where(on_first, packed + k * LANES, there)
        found.append((target, jnp.where(on_first, 1.0, high), jnp.where(on_first, 0.0, low)))
    return found


def move(pick_ref, rows_ref, parts, out_refs):
    width = rows_ref.shape[1] - EXTRA
    for start in range(0, width, CHUNK):
        cut = slice(start, start + CHUNK)
        rows = rows_ref[:, cut]
        for part, out_ref in zip(parts, out_refs):
            moved = dot(pick_ref[part * LANES : (part + 1) * LANES, :], rows)
            out_ref[:, cut] = moved[: COLS * SLOTS].astype(BF)


def near_kernel(place_ref, rows_ref, first_ref, third_ref, pick_ref, token_ref):
    token_ref[...] = jnp.zeros_like(token_ref)
    column = iota((EXPERTS * BOTH, EXPERTS * LANES), 1)
    pick = jnp.zeros(column.shape, F32)
    for target, _, _ in slot_targets(place_ref, rows_ref):
        pick = jnp.where(column == target, 1.0, pick)
    pick_ref[...] = pick.T.astype(BF)
    move(pick_ref, rows_ref, (1, 3), (first_ref, third_ref))


def rest_kernel(place_ref, rows_ref, pick_ref, own_ref, back_ref):
    column = iota((EXPERTS * BOTH, EXPERTS * LANES), 1)
    high_m = jnp.zeros(column.shape, F32)
    low_m = jnp.zeros(column.shape, F32)
    for target, high, low in slot_targets(place_ref, rows_ref):
        here = column == target
        high_m = jnp.where(here, high, high_m)
        low_m = jnp.where(here, low, low_m)
    back_ref[:, : EXPERTS * LANES] = high_m.astype(BF)
    back_ref[:, EXPERTS * LANES :] = low_m.astype(BF)
    move(pick_ref, rows_ref, (0,), (own_ref,))


def far_kernel(rows_ref, pick_ref, *refs):
    move(pick_ref, rows_ref, (2,), refs[-1:])


def expert_kernel(count, *refs):
    rows_refs = refs[:count]
    gate_ref, up_ref, down_ref, other_ref = refs[count : count + 4]
    out_refs, token_ref = refs[-1 - count : -1], refs[-1]
    token_ref[...] = jnp.zeros_like(token_ref)
    features, width = gate_ref.shape
    hidden = []
    for rows_ref in rows_refs:
        gate, up = 0.0, 0.0
        for start in range(0, features, WIDE):
            cut = slice(start, start + WIDE)
            more = slice(features + start, features + start + WIDE)
            rows = rows_ref[:, cut]
            gate += dot(rows, jnp.concatenate([gate_ref[cut, :], other_ref[cut, :]], axis=1))
            up += dot(rows, jnp.concatenate([up_ref[cut, :], other_ref[more, :]], axis=1))
        hidden.append((gate / (1.0 + jnp.exp(-gate)) * up).astype(BF))
    for start in range(0, features, CHUNK):
        cut = slice(start, start + CHUNK)
        at = [2 * features + start + i * width for i in range(CHUNK // width)]
        other = jnp.concatenate([other_ref[i : i + width, :] for i in at], axis=1)
        down = jnp.concatenate([down_ref[:, cut], other], axis=0)
        for rows, out_ref in zip(hidden, out_refs):
            out_ref[:, cut] = dot(rows, down).astype(BF)


def gather_kernel(parts, last, back_ref, *refs):
    rows_refs, so_far_ref, out_ref = refs[: len(parts)], refs[len(parts)], refs[-1]
    width = rows_refs[0].shape[1]
    used = COLS * SLOTS
    for start in range(0, width, CHUNK):
        cut = slice(start, min(start + CHUNK, width))
        total = so_far_ref[:, cut] if last else 0.0
        for part, ref in zip(parts, rows_refs):
            high = slice(part * LANES, part * LANES + used)
            low = slice((EXPERTS + part) * LANES, (EXPERTS + part) * LANES + used)
            rows = ref[:, cut]
            total += dot(back_ref[:, high], rows) + dot(back_ref[:, low], rows)
        out_ref[:, cut] = total.astype(out_ref.dtype)


def finish_kernel(direction, place_ref, meta_ref, rows_ref, own_ref, *refs):
    out_ref = refs[-1]
    mine = slice(direction * ROWS, (direction + 1) * ROWS)
    meta = meta_ref[...]
    total = EXPERTS * BOTH
    column = iota((BOTH, total), 1)
    row = iota((BOTH, total), 0)
    high = jnp.zeros((BOTH, total), F32)
    low = jnp.zeros((BOTH, total), F32)
    for k in range(2):
        there = (meta[:, 8 + k : 9 + k] * BOTH + meta[:, 2 * k + 1 : 2 * k + 2]).astype(jnp.int32)
        high = jnp.where(column == there, meta[:, 4 + 2 * k : 5 + 2 * k], high)
        low = jnp.where(column == there, meta[:, 5 + 2 * k : 6 + 2 * k], low)
    same = column == row
    for part in range(1, COLS):
        same = same | (column == row + part * BOTH)
    ones = jnp.where(same, 1.0, 0.0)
    on_first = place_ref[0] == 0
    high = jnp.where(on_first, high, ones)[mine].astype(BF)
    low = jnp.where(on_first, low, 0.0)[mine].astype(BF)
    width = own_ref.shape[1]
    for start in range(0, width, CHUNK):
        cut = slice(start, min(start + CHUNK, width))
        rows = rows_ref[:, cut]
        mixture = dot(high, rows) + dot(low, rows)
        out_ref[:, cut] = (own_ref[:, cut].astype(F32) + mixture).astype(BF)


def ends_kernel(place_ref, right_ref, left_ref, fwd_ref, bwd_ref, _, out_ref):
    count, _, part = out_ref.shape
    at_start = place_ref[2] == 0
    for r in range(count):
        near, far = [slice(j * part, (j + 1) * part) for j in (r, 2 * count - 1 - r)]

        @pl.when(at_start)
        def _():
            out_ref[r, :ROWS, :] = left_ref[:, near]
            out_ref[r, ROWS:, :] = bwd_ref[:, near]

        @pl.when(jnp.logical_not(at_start))
        def _():
            out_ref[r, :ROWS, :] = fwd_ref[:, far]
            out_ref[r, ROWS:, :] = right_ref[:, far]


def entered_kernel(place_ref, held_ref, got_ref, out_ref):
    count, _, part = held_ref.shape
    at_start = place_ref[2] == 0
    for r in range(count):
        near, far = [slice(j * part, (j + 1) * part) for j in (r, 2 * count - 1 - r)]

        @pl.when(at_start)
        def _():
            out_ref[:, near] = held_ref[r, :ROWS, :]
            out_ref[:, far] = got_ref[r]

        @pl.when(jnp.logical_not(at_start))
        def _():
            out_ref[:, near] = got_ref[r]
            out_ref[:, far] = held_ref[r, ROWS:, :]


SMEM = pl.BlockSpec(memory_space=pltpu.SMEM)


def params(mib=20):
    return pltpu.CompilerParams(vmem_limit_bytes=mib * 1024 * 1024)


VMEM = pl.BlockSpec(memory_space=pltpu.VMEM)
ANY = pl.BlockSpec(memory_space=pl.ANY)


def shape(rows, columns, dtype=BF):
    return jax.ShapeDtypeStruct((rows, columns), dtype)


def make_send(place, fwd, bwd, gain, ids, gates):
    features = fwd.shape[1]
    return pl.pallas_call(
        send_kernel,
        out_shape=(shape(EXPERTS * BOTH, features + EXTRA), shape(BOTH, EXTRA, F32)),
        in_specs=[SMEM] + [VMEM] * 5,
        out_specs=(VMEM, VMEM),
        compiler_params=params(),
        name="normed",
    )(place, fwd, bwd, gain, ids, gates)


def make_near(place, rows):
    features = rows.shape[1] - EXTRA
    total = EXPERTS * BOTH
    return pl.pallas_call(
        near_kernel,
        out_shape=(shape(COLS * SLOTS, features),) * 2
        + (shape(EXPERTS * LANES, total), shape(8, LANES, jnp.int32)),
        in_specs=[SMEM, VMEM],
        out_specs=(VMEM,) * 4,
        compiler_params=params(),
        name="near",
    )(place, rows)


def pack_kernel(gate_ref, up_ref, down_ref, _, out_ref):
    features, width = gate_ref.shape
    out_ref[:features, :] = gate_ref[...]
    out_ref[features : 2 * features, :] = up_ref[...]
    for i in range(features // width):
        at = 2 * features + i * width
        out_ref[at : at + width, :] = down_ref[:, i * width : (i + 1) * width]


def make_pack(gate, up, down, before):
    features, width = gate.shape
    return pl.pallas_call(
        pack_kernel,
        out_shape=shape(3 * features, width),
        in_specs=[VMEM] * 3 + [ANY],
        out_specs=VMEM,
        compiler_params=params(),
        name="pack",
    )(gate, up, down, before)


def make_rest(place, rows, pick):
    features = rows.shape[1] - EXTRA
    return pl.pallas_call(
        rest_kernel,
        out_shape=(
            shape(COLS * SLOTS, features),
            shape(EXPERTS * BOTH, 2 * EXPERTS * LANES),
        ),
        in_specs=[SMEM, VMEM, VMEM],
        out_specs=(VMEM, VMEM),
        compiler_params=params(),
        name="rest",
    )(place, rows, pick)


def make_far(rows, pick, *before):
    return pl.pallas_call(
        far_kernel,
        out_shape=shape(COLS * SLOTS, rows.shape[1] - EXTRA),
        in_specs=[VMEM, VMEM] + [ANY] * len(before),
        out_specs=VMEM,
        compiler_params=params(),
        name="far",
    )(rows, pick, *before)


def run_experts(blocks, own, packed, *before):
    count = len(blocks)

    def body(*refs):
        expert_kernel(count, *refs)

    return pl.pallas_call(
        body,
        out_shape=(shape(*blocks[0].shape),) * count + (shape(8, LANES, jnp.int32),),
        in_specs=[VMEM] * (count + 4) + [ANY] * len(before),
        out_specs=(VMEM,) * (count + 1),
        compiler_params=params(),
        name="experts",
    )(*blocks, *own, packed, *before)


def make_gather(back, blocks, parts, so_far=None, before=()):
    features = blocks[0].shape[1]
    total = back.shape[0]
    last = so_far is not None

    def body(*refs):
        gather_kernel(parts, last, *refs)

    return pl.pallas_call(
        body,
        out_shape=shape(total, features, BF if last else F32),
        in_specs=[VMEM] * (1 + len(blocks) + last) + [ANY] * len(before),
        out_specs=VMEM,
        compiler_params=params(),
        name="gather",
    )(back, *blocks, *([so_far] if last else []), *before)


def make_finish(direction, place, meta, rows, own, *before):
    def body(*refs):
        finish_kernel(direction, *refs)

    return pl.pallas_call(
        body,
        out_shape=shape(*own.shape),
        in_specs=[SMEM] + [VMEM] * 3 + [ANY] * len(before),
        out_specs=VMEM,
        compiler_params=params(),
        name="finish",
    )(place, meta, rows, own, *before)


def make_simple(kernel, out, place, *arrays, before=()):
    return pl.pallas_call(
        kernel,
        out_shape=jax.ShapeDtypeStruct(out, BF),
        in_specs=[SMEM] + [VMEM] * len(arrays) + [ANY] * len(before),
        out_specs=VMEM,
        compiler_params=params(),
        name="blocks",
    )(place, *arrays, *before)


def shifted(block, distance, count):
    return lax.ppermute(block, "pp", [(i, (i + distance) % count) for i in range(count)])


def mirrored(pairs, sections):
    return pairs + [(sections - 1 - i, sections - 1 - j) for i, j in pairs]


def from_other_core(block):
    return lax.ppermute(block, "ep", [(i, i ^ 1) for i in range(lax.axis_size("ep"))])


def inward(held, step, sections):
    bit = 1 << step
    pairs = [(i, i - bit) for i in range(bit, sections // 2, 2 * bit)]
    got = lax.ppermute(held, "pp", mirrored(pairs, sections))
    return jnp.concatenate([held, got], axis=0), got


def outward(own, place, sections):
    def move(block, *pairs):
        return lax.ppermute(block, "pp", mirrored(list(pairs), sections))

    a = move(own[4:8], (0, 4))
    b = move(jnp.where(place == 0, own[2:4], a[2:4]), (0, 2), (4, 6))
    c = jnp.where(place == 0, own[1:2], jnp.where(place == 4, a[1:2], b[1:2]))
    c = move(c, (0, 1), (2, 3), (4, 5), (6, 7))
    mine = jnp.where(place == 0, own[0], jnp.where(place == 4, a[0], b[0]))
    return jnp.where((place & 1) == 1, c[0], mine)


def body(
    state_fwd,
    state_bwd,
    enter_fwd,
    enter_bwd,
    norm_gain,
    w_gate,
    w_up,
    w_down,
    route_ids,
    route_gates,
):
    sections = lax.axis_size("pp")
    section = lax.axis_index("pp")
    position = lax.axis_index("ep")
    place = jnp.stack([position % 2, position // (2 * COLS), section]).astype(jnp.int32)
    fwd, bwd = state_fwd[0], state_bwd[0]
    features = fwd.shape[1]
    part = features // sections
    ids = route_ids[0, 0].transpose(0, 2, 1)
    gates = route_gates[0, 0].transpose(0, 2, 1)

    sent, meta = make_send(place, fwd, bwd, norm_gain, ids, gates)
    rows = exchange(sent)
    send1, send3, pick, token = make_near(place, rows)
    near, far = hop(send1, 1), hop(send3, 3)
    own = (w_gate[0], w_up[0], w_down[0])
    weights = own, from_other_core(make_pack(*own, pick))
    send0, back = make_rest(place, rows, pick)
    last = hop(make_far(rows, pick, near, far, back), 2)

    half = sections // 2
    at_start = section == 0
    entering = jnp.concatenate([enter_fwd, enter_bwd], axis=1)
    held, got = inward(entering, 0, sections)
    done0, done1, done3, token = run_experts([send0, near, far], *weights)
    back1, back3 = hop(done1, -1), hop(done3, -3)
    done2, token = run_experts([last], *weights, token)
    back2 = hop(done2, -2)
    held, got = inward(held, 1, sections)
    begun = make_gather(back, [done0, back1, back3], (0, 1, 3))
    gathered = make_gather(back, [back2], (2,), begun, (got,))
    held, _ = inward(held, 2, sections)
    passed_on = jnp.where(at_start, held[:, ROWS:], held[:, :ROWS])
    got = lax.ppermute(passed_on, "pp", [(0, sections - 1), (sections - 1, 0)])
    rows = exchange(gathered)
    fwd_out = make_finish(0, place, meta, rows, fwd)
    bwd_out = make_finish(1, place, meta, rows, bwd, fwd_out)
    from_right = shifted(bwd_out, -1, sections)
    from_left = shifted(fwd_out, 1, sections)
    entered = make_simple(
        entered_kernel, (ROWS, features), place, held, got
    )
    ends = make_simple(
        ends_kernel, (half, BOTH, part), place, from_right, from_left, fwd_out, bwd_out, before=(got,)
    )
    mine = outward(ends, jnp.minimum(section, sections - 1 - section), sections)
    fwd_next = jnp.where(at_start, entered, from_left)
    bwd_next = jnp.where(section == sections - 1, entered, from_right)
    return (fwd_next[None], bwd_next[None], mine[None, :ROWS], mine[None, ROWS:])


def solution(mesh):
    placed = (
        P("pp", "ep", None),
        P("pp", "ep", None),
        P(None, "ep", "pp"),
        P(None, "ep", "pp"),
        P("pp", None),
        P("pp", None, "ep"),
        P("pp", None, "ep"),
        P("pp", "ep", None),
        P("pp", None, None, "ep", None),
        P("pp", None, None, "ep", None),
    )
    return jax.shard_map(
        body,
        mesh=mesh,
        in_specs=placed,
        out_specs=(
            P("pp", "ep", None),
            P("pp", "ep", None),
            P(None, "ep", "pp"),
            P(None, "ep", "pp"),
        ),
        check_vma=False,
    )
```

```python
import jax
import jax.numpy as jnp
from jax import lax
from jax.experimental import pallas as pl
from jax.experimental.pallas import tpu as pltpu
from jax.sharding import PartitionSpec as P

EPS = 1e-06
BF = jnp.bfloat16
F32 = jnp.float32
EXPERTS = 4
COLS = 4
CAP = 15
ROWS = 24
BOTH = 2 * ROWS
SLOTS = 2 * CAP
EXTRA = 128
WIDE = 1792
CHUNK = 512
LANES = 128


def device(y, x, core):
    return (y * COLS + x) * 2 + core


def hop(block, distance):
    route = []
    for y in range(EXPERTS):
        for x in range(COLS):
            for core in range(2):
                along_y = core == 1
                there = ((y + distance) % EXPERTS, x) if along_y else (y, (x + distance) % COLS)
                route.append((device(y, x, core), device(*there, core)))
    return lax.ppermute(block, "ep", route)


def rings(along_y):
    groups = []
    for core in range(2):
        if (core == 0) == along_y:
            groups += [[device(y, x, core) for y in range(EXPERTS)] for x in range(COLS)]
        else:
            groups += [[device(y, x, core) for x in range(COLS)] for y in range(EXPERTS)]
    return groups


def exchange(rows):
    return lax.all_to_all(
        rows, "ep", split_axis=0, concat_axis=0, axis_index_groups=rings(True), tiled=True
    )


def iota(shape, dim):
    return lax.broadcasted_iota(jnp.int32, shape, dim)


def dot(a, b):
    return jnp.dot(a, b, preferred_element_type=F32)


def split_gate(gate):
    high = gate.astype(BF).astype(F32)
    return high, (gate - high).astype(BF).astype(F32)


def send_kernel(place_ref, fwd_ref, bwd_ref, gain_ref, ids_ref, gates_ref, out_ref, meta_ref):
    lanes = iota((BOTH, EXTRA), 1)
    row = iota((BOTH, EXTRA), 0)
    in_fwd = row < ROWS
    own = lanes[:, :ROWS] == row[:, :ROWS] - jnp.where(in_fwd[:, :ROWS], 0, ROWS)

    def column(ref, k):
        both = jnp.where(in_fwd[:, :ROWS], ref[0, k : k + 1, :], ref[1, k : k + 1, :])
        return jnp.sum(jnp.where(own, both, jnp.zeros_like(both)), axis=1, keepdims=True)

    first, second = column(ids_ref, 0), column(ids_ref, 1)
    named = jnp.where((lanes == first) | (lanes == second), 1.0, 0.0)
    r0, r1 = iota((BOTH, BOTH), 0), iota((BOTH, BOTH), 1)
    earlier = jnp.where((r1 < r0) & ((r1 < ROWS) == (r0 < ROWS)), 1.0, 0.0)
    rank = dot(earlier.astype(BF), named.astype(BF))
    offset = jnp.where(in_fwd[:, 0:1], 0, CAP)
    slots = []
    for chosen in (first, second):
        taken = jnp.sum(jnp.where(lanes == chosen, rank, 0.0), axis=1, keepdims=True)
        slots.append(taken.astype(jnp.int32) + offset)
    ahead = [
        jnp.bitwise_and(chosen - place_ref[1] + EXPERTS, EXPERTS - 1) for chosen in (first, second)
    ]
    fields = [ahead[0].astype(F32), slots[0].astype(F32), ahead[1].astype(F32), slots[1].astype(F32)]
    fields += split_gate(column(gates_ref, 0))
    fields += split_gate(column(gates_ref, 1))
    fields += [first.astype(F32), second.astype(F32)]
    meta = jnp.zeros((BOTH, EXTRA), F32)
    for place, field in enumerate(fields):
        meta = jnp.where(lanes == place, field, meta)
    meta_ref[...] = meta

    def as_row(column):
        return jnp.sum(jnp.where(r0 == r1, column, 0), axis=0, keepdims=True)

    target = iota((EXPERTS * BOTH, BOTH), 0)
    source = iota((EXPERTS * BOTH, BOTH), 1)
    routed = (target == as_row(first * BOTH + slots[0])) | (
        target == as_row(second * BOTH + slots[1])
    )
    copied = target == source
    for part in range(1, COLS):
        copied = copied | (target == source + part * BOTH)
    routed_f = jnp.where(routed, 1.0, 0.0)
    copied_f = jnp.where(copied, 1.0, 0.0)
    pick = jnp.where(place_ref[0] == 0, routed_f, copied_f).astype(BF)
    values = jnp.concatenate([fwd_ref[...].astype(F32), bwd_ref[...].astype(F32)], axis=0)
    features = values.shape[1]
    inverse = lax.rsqrt(jnp.mean(values * values, axis=-1, keepdims=True) + EPS)
    normed = (values * inverse * gain_ref[...]).astype(BF)
    for start in range(0, features, CHUNK):
        out_ref[:, start : start + CHUNK] = dot(pick, normed[:, start : start + CHUNK]).astype(BF)
    out_ref[:, features:] = dot(pick, meta.astype(BF)).astype(BF)


def slot_targets(place_ref, rows_ref):
    total = EXPERTS * BOTH
    features = rows_ref.shape[1] - EXTRA
    extra = rows_ref[:, features:].astype(F32)
    row = iota((total, 1), 0)
    part = (
        (row >= BOTH).astype(jnp.int32)
        + (row >= 2 * BOTH).astype(jnp.int32)
        + (row >= 3 * BOTH).astype(jnp.int32)
    )
    place = row - part * BOTH
    on_first = place_ref[0] == 0
    packed = jnp.where(place < SLOTS, part * SLOTS + place, -EXPERTS * LANES)
    found = []
    for k in range(COLS):
        there, high, low = -1, 0.0, 0.0
        if k < 2:
            expert = extra[:, 2 * k : 2 * k + 1].astype(jnp.int32)
            slot = extra[:, 2 * k + 1 : 2 * k + 2].astype(jnp.int32)
            there = expert * LANES + part * SLOTS + slot
            high = extra[:, 4 + 2 * k : 5 + 2 * k]
            low = extra[:, 5 + 2 * k : 6 + 2 * k]
        target = jnp.where(on_first, packed + k * LANES, there)
        found.append((target, jnp.where(on_first, 1.0, high), jnp.where(on_first, 0.0, low)))
    return found


def move(pick_ref, rows_ref, parts, out_refs):
    width = rows_ref.shape[1] - EXTRA
    for start in range(0, width, CHUNK):
        cut = slice(start, start + CHUNK)
        rows = rows_ref[:, cut]
        for part, out_ref in zip(parts, out_refs):
            moved = dot(pick_ref[part * LANES : (part + 1) * LANES, :], rows)
            out_ref[:, cut] = moved[: COLS * SLOTS].astype(BF)


def near_kernel(place_ref, rows_ref, first_ref, third_ref, pick_ref, token_ref):
    token_ref[...] = jnp.zeros_like(token_ref)
    column = iota((EXPERTS * BOTH, EXPERTS * LANES), 1)
    pick = jnp.zeros(column.shape, F32)
    for target, _, _ in slot_targets(place_ref, rows_ref):
        pick = jnp.where(column == target, 1.0, pick)
    pick_ref[...] = pick.T.astype(BF)
    move(pick_ref, rows_ref, (1, 3), (first_ref, third_ref))


def rest_kernel(place_ref, rows_ref, pick_ref, _, own_ref, back_ref):
    column = iota((EXPERTS * BOTH, EXPERTS * LANES), 1)
    high_m = jnp.zeros(column.shape, F32)
    low_m = jnp.zeros(column.shape, F32)
    for target, high, low in slot_targets(place_ref, rows_ref):
        here = column == target
        high_m = jnp.where(here, high, high_m)
        low_m = jnp.where(here, low, low_m)
    back_ref[:, : EXPERTS * LANES] = high_m.astype(BF)
    back_ref[:, EXPERTS * LANES :] = low_m.astype(BF)
    move(pick_ref, rows_ref, (0,), (own_ref,))


def far_kernel(rows_ref, pick_ref, *refs):
    move(pick_ref, rows_ref, (2,), refs[-1:])


def expert_kernel(count, *refs):
    rows_refs = refs[:count]
    gate_ref, up_ref, down_ref, other_ref = refs[count : count + 4]
    out_refs, token_ref = refs[-1 - count : -1], refs[-1]
    token_ref[...] = jnp.zeros_like(token_ref)
    features, width = gate_ref.shape
    hidden = []
    for rows_ref in rows_refs:
        gate, up = 0.0, 0.0
        for start in range(0, features, WIDE):
            cut = slice(start, start + WIDE)
            more = slice(features + start, features + start + WIDE)
            rows = rows_ref[:, cut]
            gate += dot(rows, jnp.concatenate([gate_ref[cut, :], other_ref[cut, :]], axis=1))
            up += dot(rows, jnp.concatenate([up_ref[cut, :], other_ref[more, :]], axis=1))
        hidden.append((gate / (1.0 + jnp.exp(-gate)) * up).astype(BF))
    for start in range(0, features, CHUNK):
        cut = slice(start, start + CHUNK)
        at = [2 * features + start + i * width for i in range(CHUNK // width)]
        other = jnp.concatenate([other_ref[i : i + width, :] for i in at], axis=1)
        down = jnp.concatenate([down_ref[:, cut], other], axis=0)
        for rows, out_ref in zip(hidden, out_refs):
            out_ref[:, cut] = dot(rows, down).astype(BF)


def gather_kernel(parts, last, back_ref, *refs):
    rows_refs, so_far_ref, out_ref = refs[: len(parts)], refs[len(parts)], refs[-1]
    width = rows_refs[0].shape[1]
    used = COLS * SLOTS
    for start in range(0, width, CHUNK):
        cut = slice(start, min(start + CHUNK, width))
        total = so_far_ref[:, cut] if last else 0.0
        for part, ref in zip(parts, rows_refs):
            high = slice(part * LANES, part * LANES + used)
            low = slice((EXPERTS + part) * LANES, (EXPERTS + part) * LANES + used)
            rows = ref[:, cut]
            total += dot(back_ref[:, high], rows) + dot(back_ref[:, low], rows)
        out_ref[:, cut] = total.astype(out_ref.dtype)


def finish_kernel(direction, place_ref, meta_ref, rows_ref, own_ref, *refs):
    out_ref = refs[-1]
    mine = slice(direction * ROWS, (direction + 1) * ROWS)
    meta = meta_ref[...]
    total = EXPERTS * BOTH
    column = iota((BOTH, total), 1)
    row = iota((BOTH, total), 0)
    high = jnp.zeros((BOTH, total), F32)
    low = jnp.zeros((BOTH, total), F32)
    for k in range(2):
        there = (meta[:, 8 + k : 9 + k] * BOTH + meta[:, 2 * k + 1 : 2 * k + 2]).astype(jnp.int32)
        high = jnp.where(column == there, meta[:, 4 + 2 * k : 5 + 2 * k], high)
        low = jnp.where(column == there, meta[:, 5 + 2 * k : 6 + 2 * k], low)
    same = column == row
    for part in range(1, COLS):
        same = same | (column == row + part * BOTH)
    ones = jnp.where(same, 1.0, 0.0)
    on_first = place_ref[0] == 0
    high = jnp.where(on_first, high, ones)[mine].astype(BF)
    low = jnp.where(on_first, low, 0.0)[mine].astype(BF)
    width = own_ref.shape[1]
    for start in range(0, width, CHUNK):
        cut = slice(start, min(start + CHUNK, width))
        rows = rows_ref[:, cut]
        mixture = dot(high, rows) + dot(low, rows)
        out_ref[:, cut] = (own_ref[:, cut].astype(F32) + mixture).astype(BF)


def ends_fwd_kernel(place_ref, left_ref, fwd_ref, out_ref):
    count, _, part = out_ref.shape
    for r in range(count):
        near, far = [slice(j * part, (j + 1) * part) for j in (r, 2 * count - 1 - r)]

        @pl.when(place_ref[2] == 0)
        def _():
            out_ref[r] = left_ref[:, near]

        @pl.when(place_ref[2] != 0)
        def _():
            out_ref[r] = fwd_ref[:, far]


def ends_kernel(place_ref, fwds_ref, right_ref, bwd_ref, out_ref):
    count, _, part = out_ref.shape
    for r in range(count):
        near, far = [slice(j * part, (j + 1) * part) for j in (r, 2 * count - 1 - r)]
        out_ref[r, :ROWS, :] = fwds_ref[r]

        @pl.when(place_ref[2] == 0)
        def _():
            out_ref[r, ROWS:, :] = bwd_ref[:, near]

        @pl.when(place_ref[2] != 0)
        def _():
            out_ref[r, ROWS:, :] = right_ref[:, far]


def entered_kernel(place_ref, held_ref, got_ref, out_ref):
    count, _, part = held_ref.shape
    at_start = place_ref[2] == 0
    for r in range(count):
        near, far = [slice(j * part, (j + 1) * part) for j in (r, 2 * count - 1 - r)]

        @pl.when(at_start)
        def _():
            out_ref[:, near] = held_ref[r, :ROWS, :]
            out_ref[:, far] = got_ref[r]

        @pl.when(jnp.logical_not(at_start))
        def _():
            out_ref[:, near] = got_ref[r]
            out_ref[:, far] = held_ref[r, ROWS:, :]


SMEM = pl.BlockSpec(memory_space=pltpu.SMEM)


def params(mib=20):
    return pltpu.CompilerParams(vmem_limit_bytes=mib * 1024 * 1024)


VMEM = pl.BlockSpec(memory_space=pltpu.VMEM)
ANY = pl.BlockSpec(memory_space=pl.ANY)


def shape(rows, columns, dtype=BF):
    return jax.ShapeDtypeStruct((rows, columns), dtype)


def make_send(place, fwd, bwd, gain, ids, gates):
    features = fwd.shape[1]
    return pl.pallas_call(
        send_kernel,
        out_shape=(shape(EXPERTS * BOTH, features + EXTRA), shape(BOTH, EXTRA, F32)),
        in_specs=[SMEM] + [VMEM] * 5,
        out_specs=(VMEM, VMEM),
        compiler_params=params(),
        name="normed",
    )(place, fwd, bwd, gain, ids, gates)


def make_near(place, rows):
    features = rows.shape[1] - EXTRA
    total = EXPERTS * BOTH
    return pl.pallas_call(
        near_kernel,
        out_shape=(shape(COLS * SLOTS, features),) * 2
        + (shape(EXPERTS * LANES, total), shape(8, LANES, jnp.int32)),
        in_specs=[SMEM, VMEM],
        out_specs=(VMEM,) * 4,
        compiler_params=params(),
        name="near",
    )(place, rows)


def pack_kernel(gate_ref, up_ref, down_ref, _, out_ref):
    features, width = gate_ref.shape
    out_ref[:features, :] = gate_ref[...]
    out_ref[features : 2 * features, :] = up_ref[...]
    for i in range(features // width):
        at = 2 * features + i * width
        out_ref[at : at + width, :] = down_ref[:, i * width : (i + 1) * width]


def make_pack(gate, up, down, before):
    features, width = gate.shape
    return pl.pallas_call(
        pack_kernel,
        out_shape=shape(3 * features, width),
        in_specs=[VMEM] * 3 + [ANY],
        out_specs=VMEM,
        compiler_params=params(),
        name="pack",
    )(gate, up, down, before)


def make_rest(place, rows, pick, before):
    features = rows.shape[1] - EXTRA
    return pl.pallas_call(
        rest_kernel,
        out_shape=(
            shape(COLS * SLOTS, features),
            shape(EXPERTS * BOTH, 2 * EXPERTS * LANES),
        ),
        in_specs=[SMEM, VMEM, VMEM, ANY],
        out_specs=(VMEM, VMEM),
        compiler_params=params(),
        name="rest",
    )(place, rows, pick, before)


def make_far(rows, pick, *before):
    return pl.pallas_call(
        far_kernel,
        out_shape=shape(COLS * SLOTS, rows.shape[1] - EXTRA),
        in_specs=[VMEM, VMEM] + [ANY] * len(before),
        out_specs=VMEM,
        compiler_params=params(),
        name="far",
    )(rows, pick, *before)


def run_experts(blocks, own, packed, *before):
    count = len(blocks)

    def body(*refs):
        expert_kernel(count, *refs)

    return pl.pallas_call(
        body,
        out_shape=(shape(*blocks[0].shape),) * count + (shape(8, LANES, jnp.int32),),
        in_specs=[VMEM] * (count + 4) + [ANY] * len(before),
        out_specs=(VMEM,) * (count + 1),
        compiler_params=params(),
        name="experts",
    )(*blocks, *own, packed, *before)


def make_gather(back, blocks, parts, so_far=None, before=()):
    features = blocks[0].shape[1]
    total = back.shape[0]
    last = so_far is not None

    def body(*refs):
        gather_kernel(parts, last, *refs)

    return pl.pallas_call(
        body,
        out_shape=shape(total, features, BF if last else F32),
        in_specs=[VMEM] * (1 + len(blocks) + last) + [ANY] * len(before),
        out_specs=VMEM,
        compiler_params=params(),
        name="gather",
    )(back, *blocks, *([so_far] if last else []), *before)


def make_finish(direction, place, meta, rows, own, *before):
    def body(*refs):
        finish_kernel(direction, *refs)

    return pl.pallas_call(
        body,
        out_shape=shape(*own.shape),
        in_specs=[SMEM] + [VMEM] * 3 + [ANY] * len(before),
        out_specs=VMEM,
        compiler_params=params(),
        name="finish",
    )(place, meta, rows, own, *before)


def make_simple(kernel, out, place, *arrays, before=()):
    return pl.pallas_call(
        kernel,
        out_shape=jax.ShapeDtypeStruct(out, BF),
        in_specs=[SMEM] + [VMEM] * len(arrays) + [ANY] * len(before),
        out_specs=VMEM,
        compiler_params=params(),
        name="blocks",
    )(place, *arrays, *before)


def shifted(block, distance, count):
    return lax.ppermute(block, "pp", [(i, (i + distance) % count) for i in range(count)])


def mirrored(pairs, sections):
    return pairs + [(sections - 1 - i, sections - 1 - j) for i, j in pairs]


def from_other_core(block):
    return lax.ppermute(block, "ep", [(i, i ^ 1) for i in range(lax.axis_size("ep"))])


def inward(held, bit, radix, sections):
    got = []
    for k in range(1, radix):
        pairs = [(i + k * bit, i) for i in range(0, sections // 2, radix * bit)]
        got.append(lax.ppermute(held, "pp", mirrored(pairs, sections)))
    return jnp.concatenate([held] + got, axis=0), got[-1]


def outward(own, place, sections):
    def move(block, *pairs):
        return lax.ppermute(block, "pp", mirrored(list(pairs), sections))

    a = move(own[4:8], (0, 4))
    b = move(jnp.where(place == 0, own[2:4], a[2:4]), (0, 2), (4, 6))
    c = jnp.where(place == 0, own[1:2], jnp.where(place == 4, a[1:2], b[1:2]))
    c = move(c, (0, 1), (2, 3), (4, 5), (6, 7))
    mine = jnp.where(place == 0, own[0], jnp.where(place == 4, a[0], b[0]))
    return jnp.where((place & 1) == 1, c[0], mine)


def body(
    state_fwd,
    state_bwd,
    enter_fwd,
    enter_bwd,
    norm_gain,
    w_gate,
    w_up,
    w_down,
    route_ids,
    route_gates,
):
    sections = lax.axis_size("pp")
    section = lax.axis_index("pp")
    position = lax.axis_index("ep")
    place = jnp.stack([position % 2, position // (2 * COLS), section]).astype(jnp.int32)
    fwd, bwd = state_fwd[0], state_bwd[0]
    features = fwd.shape[1]
    part = features // sections
    ids = route_ids[0, 0].transpose(0, 2, 1)
    gates = route_gates[0, 0].transpose(0, 2, 1)

    sent, meta = make_send(place, fwd, bwd, norm_gain, ids, gates)
    rows = exchange(sent)
    send1, send3, pick, token = make_near(place, rows)
    near, far = hop(send1, 1), hop(send3, 3)
    own = (w_gate[0], w_up[0], w_down[0])
    weights = own, from_other_core(make_pack(*own, pick))
    send0, back = make_rest(place, rows, pick, weights[1])
    done0, token = run_experts([send0], *weights)
    last = hop(make_far(rows, pick, token), 2)
    done1, done3, token = run_experts([near, far], *weights)
    back1, back3 = hop(done1, -1), hop(done3, -3)
    done2, token = run_experts([last], *weights, token)
    back2 = hop(done2, -2)

    half = sections // 2
    at_start = section == 0
    held, _ = inward(jnp.concatenate([enter_fwd, enter_bwd], axis=1), 1, 4, sections)
    held, got = inward(held, 4, 2, sections)
    begun = make_gather(back, [done0, back1, back3], (0, 1, 3))
    gathered = make_gather(back, [back2], (2,), begun, (got,))
    passed_on = jnp.where(at_start, held[:, ROWS:], held[:, :ROWS])
    got = lax.ppermute(passed_on, "pp", [(0, sections - 1), (sections - 1, 0)])
    rows = exchange(gathered)
    fwd_out = make_finish(0, place, meta, rows, fwd, got)
    bwd_out = make_finish(1, place, meta, rows, bwd, fwd_out)
    from_right = shifted(bwd_out, -1, sections)
    from_left = shifted(fwd_out, 1, sections)
    entered = make_simple(
        entered_kernel, (ROWS, features), place, held, got
    )
    fwds = make_simple(ends_fwd_kernel, (half, ROWS, part), place, from_left, fwd_out)
    ends = make_simple(ends_kernel, (half, BOTH, part), place, fwds, from_right, bwd_out)
    mine = outward(ends, jnp.minimum(section, sections - 1 - section), sections)
    fwd_next = jnp.where(at_start, entered, from_left)
    bwd_next = jnp.where(section == sections - 1, entered, from_right)
    return (fwd_next[None], bwd_next[None], mine[None, :ROWS], mine[None, ROWS:])


def solution(mesh):
    placed = (
        P("pp", "ep", None),
        P("pp", "ep", None),
        P(None, "ep", "pp"),
        P(None, "ep", "pp"),
        P("pp", None),
        P("pp", None, "ep"),
        P("pp", None, "ep"),
        P("pp", "ep", None),
        P("pp", None, None, "ep", None),
        P("pp", None, None, "ep", None),
    )
    return jax.shard_map(
        body,
        mesh=mesh,
        in_specs=placed,
        out_specs=(
            P("pp", "ep", None),
            P("pp", "ep", None),
            P(None, "ep", "pp"),
            P(None, "ep", "pp"),
        ),
        check_vma=False,
    )
```

```python
import jax
import jax.numpy as jnp
from jax import lax
from jax.experimental import pallas as pl
from jax.experimental.pallas import tpu as pltpu
from jax.sharding import PartitionSpec as P

EPS = 1e-06
BF = jnp.bfloat16
F32 = jnp.float32
EXPERTS = 4
COLS = 4
CAP = 15
ROWS = 24
BOTH = 2 * ROWS
SLOTS = 2 * CAP
EXTRA = 128
WIDE = 1792
CHUNK = 512
LANES = 128


def device(y, x, core):
    return (y * COLS + x) * 2 + core


def hop(block, distance):
    route = []
    for y in range(EXPERTS):
        for x in range(COLS):
            for core in range(2):
                along_y = core == 1
                there = ((y + distance) % EXPERTS, x) if along_y else (y, (x + distance) % COLS)
                route.append((device(y, x, core), device(*there, core)))
    return lax.ppermute(block, "ep", route)


def rings(along_y):
    groups = []
    for core in range(2):
        if (core == 0) == along_y:
            groups += [[device(y, x, core) for y in range(EXPERTS)] for x in range(COLS)]
        else:
            groups += [[device(y, x, core) for x in range(COLS)] for y in range(EXPERTS)]
    return groups


def exchange(rows):
    return lax.all_to_all(
        rows, "ep", split_axis=0, concat_axis=0, axis_index_groups=rings(True), tiled=True
    )


def iota(shape, dim):
    return lax.broadcasted_iota(jnp.int32, shape, dim)


def dot(a, b):
    return jnp.dot(a, b, preferred_element_type=F32)


def split_gate(gate):
    high = gate.astype(BF).astype(F32)
    return high, (gate - high).astype(BF).astype(F32)


def send_kernel(place_ref, fwd_ref, bwd_ref, gain_ref, ids_ref, gates_ref, out_ref, meta_ref):
    lanes = iota((BOTH, EXTRA), 1)
    row = iota((BOTH, EXTRA), 0)
    in_fwd = row < ROWS
    own = lanes[:, :ROWS] == row[:, :ROWS] - jnp.where(in_fwd[:, :ROWS], 0, ROWS)

    def column(ref, k):
        both = jnp.where(in_fwd[:, :ROWS], ref[0, k : k + 1, :], ref[1, k : k + 1, :])
        return jnp.sum(jnp.where(own, both, jnp.zeros_like(both)), axis=1, keepdims=True)

    first, second = column(ids_ref, 0), column(ids_ref, 1)
    named = jnp.where((lanes == first) | (lanes == second), 1.0, 0.0)
    r0, r1 = iota((BOTH, BOTH), 0), iota((BOTH, BOTH), 1)
    earlier = jnp.where((r1 < r0) & ((r1 < ROWS) == (r0 < ROWS)), 1.0, 0.0)
    rank = dot(earlier.astype(BF), named.astype(BF))
    offset = jnp.where(in_fwd[:, 0:1], 0, CAP)
    slots = []
    for chosen in (first, second):
        taken = jnp.sum(jnp.where(lanes == chosen, rank, 0.0), axis=1, keepdims=True)
        slots.append(taken.astype(jnp.int32) + offset)
    ahead = [
        jnp.bitwise_and(chosen - place_ref[1] + EXPERTS, EXPERTS - 1) for chosen in (first, second)
    ]
    fields = [ahead[0].astype(F32), slots[0].astype(F32), ahead[1].astype(F32), slots[1].astype(F32)]
    fields += split_gate(column(gates_ref, 0))
    fields += split_gate(column(gates_ref, 1))
    fields += [first.astype(F32), second.astype(F32)]
    meta = jnp.zeros((BOTH, EXTRA), F32)
    for place, field in enumerate(fields):
        meta = jnp.where(lanes == place, field, meta)
    meta_ref[...] = meta

    def as_row(column):
        return jnp.sum(jnp.where(r0 == r1, column, 0), axis=0, keepdims=True)

    target = iota((EXPERTS * BOTH, BOTH), 0)
    source = iota((EXPERTS * BOTH, BOTH), 1)
    routed = (target == as_row(first * BOTH + slots[0])) | (
        target == as_row(second * BOTH + slots[1])
    )
    copied = target == source
    for part in range(1, COLS):
        copied = copied | (target == source + part * BOTH)
    routed_f = jnp.where(routed, 1.0, 0.0)
    copied_f = jnp.where(copied, 1.0, 0.0)
    pick = jnp.where(place_ref[0] == 0, routed_f, copied_f).astype(BF)
    values = jnp.concatenate([fwd_ref[...].astype(F32), bwd_ref[...].astype(F32)], axis=0)
    features = values.shape[1]
    inverse = lax.rsqrt(jnp.mean(values * values, axis=-1, keepdims=True) + EPS)
    normed = (values * inverse * gain_ref[...]).astype(BF)
    for start in range(0, features, CHUNK):
        out_ref[:, start : start + CHUNK] = dot(pick, normed[:, start : start + CHUNK]).astype(BF)
    out_ref[:, features:] = dot(pick, meta.astype(BF)).astype(BF)


def slot_targets(place_ref, rows_ref):
    total = EXPERTS * BOTH
    features = rows_ref.shape[1] - EXTRA
    extra = rows_ref[:, features:].astype(F32)
    row = iota((total, 1), 0)
    part = (
        (row >= BOTH).astype(jnp.int32)
        + (row >= 2 * BOTH).astype(jnp.int32)
        + (row >= 3 * BOTH).astype(jnp.int32)
    )
    place = row - part * BOTH
    on_first = place_ref[0] == 0
    packed = jnp.where(place < SLOTS, part * SLOTS + place, -EXPERTS * LANES)
    found = []
    for k in range(COLS):
        there, high, low = -1, 0.0, 0.0
        if k < 2:
            expert = extra[:, 2 * k : 2 * k + 1].astype(jnp.int32)
            slot = extra[:, 2 * k + 1 : 2 * k + 2].astype(jnp.int32)
            there = expert * LANES + part * SLOTS + slot
            high = extra[:, 4 + 2 * k : 5 + 2 * k]
            low = extra[:, 5 + 2 * k : 6 + 2 * k]
        target = jnp.where(on_first, packed + k * LANES, there)
        found.append((target, jnp.where(on_first, 1.0, high), jnp.where(on_first, 0.0, low)))
    return found


def move(pick_ref, rows_ref, parts, out_refs):
    width = rows_ref.shape[1] - EXTRA
    for start in range(0, width, CHUNK):
        cut = slice(start, start + CHUNK)
        rows = rows_ref[:, cut]
        for part, out_ref in zip(parts, out_refs):
            moved = dot(pick_ref[part * LANES : (part + 1) * LANES, :], rows)
            out_ref[:, cut] = moved[: COLS * SLOTS].astype(BF)


def near_kernel(place_ref, rows_ref, first_ref, third_ref, pick_ref, token_ref):
    token_ref[...] = jnp.zeros_like(token_ref)
    column = iota((EXPERTS * BOTH, EXPERTS * LANES), 1)
    pick = jnp.zeros(column.shape, F32)
    for target, _, _ in slot_targets(place_ref, rows_ref):
        pick = jnp.where(column == target, 1.0, pick)
    pick_ref[...] = pick.T.astype(BF)
    move(pick_ref, rows_ref, (1, 3), (first_ref, third_ref))


def rest_kernel(place_ref, rows_ref, pick_ref, _, own_ref, back_ref):
    column = iota((EXPERTS * BOTH, EXPERTS * LANES), 1)
    high_m = jnp.zeros(column.shape, F32)
    low_m = jnp.zeros(column.shape, F32)
    for target, high, low in slot_targets(place_ref, rows_ref):
        here = column == target
        high_m = jnp.where(here, high, high_m)
        low_m = jnp.where(here, low, low_m)
    back_ref[:, : EXPERTS * LANES] = high_m.astype(BF)
    back_ref[:, EXPERTS * LANES :] = low_m.astype(BF)
    move(pick_ref, rows_ref, (0,), (own_ref,))


def far_kernel(rows_ref, pick_ref, *refs):
    move(pick_ref, rows_ref, (2,), refs[-1:])


def expert_kernel(count, *refs):
    rows_refs = refs[:count]
    gate_ref, up_ref, down_ref, other_ref = refs[count : count + 4]
    out_refs, token_ref = refs[-1 - count : -1], refs[-1]
    token_ref[...] = jnp.zeros_like(token_ref)
    features, width = gate_ref.shape
    hidden = []
    for rows_ref in rows_refs:
        gate, up = 0.0, 0.0
        for start in range(0, features, WIDE):
            cut = slice(start, start + WIDE)
            more = slice(features + start, features + start + WIDE)
            rows = rows_ref[:, cut]
            gate += dot(rows, jnp.concatenate([gate_ref[cut, :], other_ref[cut, :]], axis=1))
            up += dot(rows, jnp.concatenate([up_ref[cut, :], other_ref[more, :]], axis=1))
        hidden.append((gate / (1.0 + jnp.exp(-gate)) * up).astype(BF))
    for start in range(0, features, CHUNK):
        cut = slice(start, start + CHUNK)
        at = [2 * features + start + i * width for i in range(CHUNK // width)]
        other = jnp.concatenate([other_ref[i : i + width, :] for i in at], axis=1)
        down = jnp.concatenate([down_ref[:, cut], other], axis=0)
        for rows, out_ref in zip(hidden, out_refs):
            out_ref[:, cut] = dot(rows, down).astype(BF)


def gather_kernel(parts, last, back_ref, *refs):
    rows_refs, so_far_ref, out_ref = refs[: len(parts)], refs[len(parts)], refs[-1]
    width = rows_refs[0].shape[1]
    used = COLS * SLOTS
    for start in range(0, width, CHUNK):
        cut = slice(start, min(start + CHUNK, width))
        total = so_far_ref[:, cut] if last else 0.0
        for part, ref in zip(parts, rows_refs):
            high = slice(part * LANES, part * LANES + used)
            low = slice((EXPERTS + part) * LANES, (EXPERTS + part) * LANES + used)
            rows = ref[:, cut]
            total += dot(back_ref[:, high], rows) + dot(back_ref[:, low], rows)
        out_ref[:, cut] = total.astype(out_ref.dtype)


def finish_kernel(direction, place_ref, meta_ref, rows_ref, own_ref, *refs):
    out_ref = refs[-1]
    mine = slice(direction * ROWS, (direction + 1) * ROWS)
    meta = meta_ref[...]
    total = EXPERTS * BOTH
    column = iota((BOTH, total), 1)
    row = iota((BOTH, total), 0)
    high = jnp.zeros((BOTH, total), F32)
    low = jnp.zeros((BOTH, total), F32)
    for k in range(2):
        there = (meta[:, 8 + k : 9 + k] * BOTH + meta[:, 2 * k + 1 : 2 * k + 2]).astype(jnp.int32)
        high = jnp.where(column == there, meta[:, 4 + 2 * k : 5 + 2 * k], high)
        low = jnp.where(column == there, meta[:, 5 + 2 * k : 6 + 2 * k], low)
    same = column == row
    for part in range(1, COLS):
        same = same | (column == row + part * BOTH)
    ones = jnp.where(same, 1.0, 0.0)
    on_first = place_ref[0] == 0
    high = jnp.where(on_first, high, ones)[mine].astype(BF)
    low = jnp.where(on_first, low, 0.0)[mine].astype(BF)
    width = own_ref.shape[1]
    for start in range(0, width, CHUNK):
        cut = slice(start, min(start + CHUNK, width))
        rows = rows_ref[:, cut]
        mixture = dot(high, rows) + dot(low, rows)
        out_ref[:, cut] = (own_ref[:, cut].astype(F32) + mixture).astype(BF)


def enter_kernel(place_ref, fwd_ref, bwd_ref, _, out_ref):
    out_ref[:, :ROWS, :] = fwd_ref[...]
    out_ref[:, ROWS:, :] = bwd_ref[...]


def ends_fwd_kernel(place_ref, left_ref, fwd_ref, out_ref):
    count, _, part = out_ref.shape
    for r in range(count):
        near, far = [slice(j * part, (j + 1) * part) for j in (r, 2 * count - 1 - r)]

        @pl.when(place_ref[2] == 0)
        def _():
            out_ref[r] = left_ref[:, near]

        @pl.when(place_ref[2] != 0)
        def _():
            out_ref[r] = fwd_ref[:, far]


def ends_kernel(place_ref, fwds_ref, right_ref, bwd_ref, out_ref):
    count, _, part = out_ref.shape
    for r in range(count):
        near, far = [slice(j * part, (j + 1) * part) for j in (r, 2 * count - 1 - r)]
        out_ref[r, :ROWS, :] = fwds_ref[r]

        @pl.when(place_ref[2] == 0)
        def _():
            out_ref[r, ROWS:, :] = bwd_ref[:, near]

        @pl.when(place_ref[2] != 0)
        def _():
            out_ref[r, ROWS:, :] = right_ref[:, far]


def entered_kernel(place_ref, held_ref, got_ref, out_ref):
    count, _, part = held_ref.shape
    at_start = place_ref[2] == 0
    for r in range(count):
        near, far = [slice(j * part, (j + 1) * part) for j in (r, 2 * count - 1 - r)]

        @pl.when(at_start)
        def _():
            out_ref[:, near] = held_ref[r, :ROWS, :]
            out_ref[:, far] = got_ref[r]

        @pl.when(jnp.logical_not(at_start))
        def _():
            out_ref[:, near] = got_ref[r]
            out_ref[:, far] = held_ref[r, ROWS:, :]


SMEM = pl.BlockSpec(memory_space=pltpu.SMEM)


def params(mib=20):
    return pltpu.CompilerParams(vmem_limit_bytes=mib * 1024 * 1024)


VMEM = pl.BlockSpec(memory_space=pltpu.VMEM)
ANY = pl.BlockSpec(memory_space=pl.ANY)


def shape(rows, columns, dtype=BF):
    return jax.ShapeDtypeStruct((rows, columns), dtype)


def make_send(place, fwd, bwd, gain, ids, gates):
    features = fwd.shape[1]
    return pl.pallas_call(
        send_kernel,
        out_shape=(shape(EXPERTS * BOTH, features + EXTRA), shape(BOTH, EXTRA, F32)),
        in_specs=[SMEM] + [VMEM] * 5,
        out_specs=(VMEM, VMEM),
        compiler_params=params(),
        name="normed",
    )(place, fwd, bwd, gain, ids, gates)


def make_near(place, rows):
    features = rows.shape[1] - EXTRA
    total = EXPERTS * BOTH
    return pl.pallas_call(
        near_kernel,
        out_shape=(shape(COLS * SLOTS, features),) * 2
        + (shape(EXPERTS * LANES, total), shape(8, LANES, jnp.int32)),
        in_specs=[SMEM, VMEM],
        out_specs=(VMEM,) * 4,
        compiler_params=params(),
        name="near",
    )(place, rows)


def pack_kernel(gate_ref, up_ref, down_ref, _, out_ref):
    features, width = gate_ref.shape
    out_ref[:features, :] = gate_ref[...]
    out_ref[features : 2 * features, :] = up_ref[...]
    for i in range(features // width):
        at = 2 * features + i * width
        out_ref[at : at + width, :] = down_ref[:, i * width : (i + 1) * width]


def make_pack(gate, up, down, before):
    features, width = gate.shape
    return pl.pallas_call(
        pack_kernel,
        out_shape=shape(3 * features, width),
        in_specs=[VMEM] * 3 + [ANY],
        out_specs=VMEM,
        compiler_params=params(),
        name="pack",
    )(gate, up, down, before)


def make_rest(place, rows, pick, before):
    features = rows.shape[1] - EXTRA
    return pl.pallas_call(
        rest_kernel,
        out_shape=(
            shape(COLS * SLOTS, features),
            shape(EXPERTS * BOTH, 2 * EXPERTS * LANES),
        ),
        in_specs=[SMEM, VMEM, VMEM, ANY],
        out_specs=(VMEM, VMEM),
        compiler_params=params(),
        name="rest",
    )(place, rows, pick, before)


def make_far(rows, pick, *before):
    return pl.pallas_call(
        far_kernel,
        out_shape=shape(COLS * SLOTS, rows.shape[1] - EXTRA),
        in_specs=[VMEM, VMEM] + [ANY] * len(before),
        out_specs=VMEM,
        compiler_params=params(),
        name="far",
    )(rows, pick, *before)


def run_experts(blocks, own, packed, *before):
    count = len(blocks)

    def body(*refs):
        expert_kernel(count, *refs)

    return pl.pallas_call(
        body,
        out_shape=(shape(*blocks[0].shape),) * count + (shape(8, LANES, jnp.int32),),
        in_specs=[VMEM] * (count + 4) + [ANY] * len(before),
        out_specs=(VMEM,) * (count + 1),
        compiler_params=params(),
        name="experts",
    )(*blocks, *own, packed, *before)


def make_gather(back, blocks, parts, so_far=None, before=()):
    features = blocks[0].shape[1]
    total = back.shape[0]
    last = so_far is not None

    def body(*refs):
        gather_kernel(parts, last, *refs)

    return pl.pallas_call(
        body,
        out_shape=shape(total, features, BF if last else F32),
        in_specs=[VMEM] * (1 + len(blocks) + last) + [ANY] * len(before),
        out_specs=VMEM,
        compiler_params=params(),
        name="gather",
    )(back, *blocks, *([so_far] if last else []), *before)


def make_finish(direction, place, meta, rows, own, *before):
    def body(*refs):
        finish_kernel(direction, *refs)

    return pl.pallas_call(
        body,
        out_shape=shape(*own.shape),
        in_specs=[SMEM] + [VMEM] * 3 + [ANY] * len(before),
        out_specs=VMEM,
        compiler_params=params(),
        name="finish",
    )(place, meta, rows, own, *before)


def make_simple(kernel, out, place, *arrays, before=()):
    return pl.pallas_call(
        kernel,
        out_shape=jax.ShapeDtypeStruct(out, BF),
        in_specs=[SMEM] + [VMEM] * len(arrays) + [ANY] * len(before),
        out_specs=VMEM,
        compiler_params=params(),
        name="blocks",
    )(place, *arrays, *before)


def shifted(block, distance, count):
    return lax.ppermute(block, "pp", [(i, (i + distance) % count) for i in range(count)])


def mirrored(pairs, sections):
    return pairs + [(sections - 1 - i, sections - 1 - j) for i, j in pairs]


def from_other_core(block):
    return lax.ppermute(block, "ep", [(i, i ^ 1) for i in range(lax.axis_size("ep"))])


def inward(held, bit, radix, sections):
    got = []
    for k in range(1, radix):
        pairs = [(i + k * bit, i) for i in range(0, sections // 2, radix * bit)]
        got.append(lax.ppermute(held, "pp", mirrored(pairs, sections)))
    return jnp.concatenate([held] + got, axis=0), got[-1]


def outward(own, place, sections):
    def move(block, *pairs):
        return lax.ppermute(block, "pp", mirrored(list(pairs), sections))

    first = move(own[1:2], (0, 1))
    a = move(own[4:8], (0, 4))
    b = jnp.where(place == 0, own[2:4], jnp.where(place == 1, first, a[2:4]))
    b = move(b, (0, 2), (4, 6))
    c = move(jnp.where(place == 4, a[1:2], b[1:2]), (2, 3), (4, 5), (6, 7))
    mine = jnp.where(place == 0, own[0], jnp.where(place == 4, a[0], b[0]))
    return jnp.where((place & 1) == 1, jnp.where(place == 1, first[0], c[0]), mine)


def body(
    state_fwd,
    state_bwd,
    enter_fwd,
    enter_bwd,
    norm_gain,
    w_gate,
    w_up,
    w_down,
    route_ids,
    route_gates,
):
    sections = lax.axis_size("pp")
    section = lax.axis_index("pp")
    position = lax.axis_index("ep")
    place = jnp.stack([position % 2, position // (2 * COLS), section]).astype(jnp.int32)
    fwd, bwd = state_fwd[0], state_bwd[0]
    features = fwd.shape[1]
    part = features // sections
    ids = route_ids[0, 0].transpose(0, 2, 1)
    gates = route_gates[0, 0].transpose(0, 2, 1)

    sent, meta = make_send(place, fwd, bwd, norm_gain, ids, gates)
    rows = exchange(sent)
    send1, send3, pick, token = make_near(place, rows)
    near, far = hop(send1, 1), hop(send3, 3)
    own = (w_gate[0], w_up[0], w_down[0])
    weights = own, from_other_core(make_pack(*own, pick))
    send0, back = make_rest(place, rows, pick, weights[1])
    done0, token = run_experts([send0], *weights)
    half = sections // 2
    at_start = section == 0
    entering = make_simple(
        enter_kernel, (1, BOTH, part), place, enter_fwd, enter_bwd, before=(weights[1],)
    )
    held, got = inward(entering, 1, 2, sections)
    last = hop(make_far(rows, pick, near, far, got, token), 2)
    done1, done3, token = run_experts([near, far], *weights)
    back1, back3 = hop(done1, -1), hop(done3, -3)
    done2, token = run_experts([last], *weights, token)
    back2 = hop(done2, -2)

    held, _ = inward(held, 2, 2, sections)
    held, got = inward(held, 4, 2, sections)
    begun = make_gather(back, [done0, back1, back3], (0, 1, 3))
    gathered = make_gather(back, [back2], (2,), begun, (got,))
    passed_on = jnp.where(at_start, held[:, ROWS:], held[:, :ROWS])
    got = lax.ppermute(passed_on, "pp", [(0, sections - 1), (sections - 1, 0)])
    rows = exchange(gathered)
    fwd_out = make_finish(0, place, meta, rows, fwd, got)
    bwd_out = make_finish(1, place, meta, rows, bwd, fwd_out)
    from_right = shifted(bwd_out, -1, sections)
    from_left = shifted(fwd_out, 1, sections)
    entered = make_simple(
        entered_kernel, (ROWS, features), place, held, got
    )
    fwds = make_simple(ends_fwd_kernel, (half, ROWS, part), place, from_left, fwd_out)
    ends = make_simple(ends_kernel, (half, BOTH, part), place, fwds, from_right, bwd_out)
    mine = outward(ends, jnp.minimum(section, sections - 1 - section), sections)
    fwd_next = jnp.where(at_start, entered, from_left)
    bwd_next = jnp.where(section == sections - 1, entered, from_right)
    return (fwd_next[None], bwd_next[None], mine[None, :ROWS], mine[None, ROWS:])


def solution(mesh):
    placed = (
        P("pp", "ep", None),
        P("pp", "ep", None),
        P(None, "ep", "pp"),
        P(None, "ep", "pp"),
        P("pp", None),
        P("pp", None, "ep"),
        P("pp", None, "ep"),
        P("pp", "ep", None),
        P("pp", None, None, "ep", None),
        P("pp", None, None, "ep", None),
    )
    return jax.shard_map(
        body,
        mesh=mesh,
        in_specs=placed,
        out_specs=(
            P("pp", "ep", None),
            P("pp", "ep", None),
            P(None, "ep", "pp"),
            P(None, "ep", "pp"),
        ),
        check_vma=False,
    )
```

```python
import jax
import jax.numpy as jnp
from jax import lax
from jax.experimental import pallas as pl
from jax.experimental.pallas import tpu as pltpu
from jax.sharding import PartitionSpec as P

EPS = 1e-06
BF = jnp.bfloat16
F32 = jnp.float32
EXPERTS = 4
COLS = 4
CAP = 15
ROWS = 24
BOTH = 2 * ROWS
SLOTS = 2 * CAP
EXTRA = 128
WIDE = 1792
CHUNK = 512
LANES = 128


def device(y, x, core):
    return (y * COLS + x) * 2 + core


def hop(block, distance):
    route = []
    for y in range(EXPERTS):
        for x in range(COLS):
            for core in range(2):
                along_y = core == 1
                there = ((y + distance) % EXPERTS, x) if along_y else (y, (x + distance) % COLS)
                route.append((device(y, x, core), device(*there, core)))
    return lax.ppermute(block, "ep", route)


def rings(along_y):
    groups = []
    for core in range(2):
        if (core == 0) == along_y:
            groups += [[device(y, x, core) for y in range(EXPERTS)] for x in range(COLS)]
        else:
            groups += [[device(y, x, core) for x in range(COLS)] for y in range(EXPERTS)]
    return groups


def exchange(rows):
    return lax.all_to_all(
        rows, "ep", split_axis=0, concat_axis=0, axis_index_groups=rings(True), tiled=True
    )


def iota(shape, dim):
    return lax.broadcasted_iota(jnp.int32, shape, dim)


def dot(a, b):
    return jnp.dot(a, b, preferred_element_type=F32)


def split_gate(gate):
    high = gate.astype(BF).astype(F32)
    return high, (gate - high).astype(BF).astype(F32)


def send_kernel(place_ref, fwd_ref, bwd_ref, gain_ref, ids_ref, gates_ref, out_ref, meta_ref):
    lanes = iota((BOTH, EXTRA), 1)
    row = iota((BOTH, EXTRA), 0)
    in_fwd = row < ROWS
    own = lanes[:, :ROWS] == row[:, :ROWS] - jnp.where(in_fwd[:, :ROWS], 0, ROWS)

    def column(ref, k):
        both = jnp.where(in_fwd[:, :ROWS], ref[0, k : k + 1, :], ref[1, k : k + 1, :])
        return jnp.sum(jnp.where(own, both, jnp.zeros_like(both)), axis=1, keepdims=True)

    first, second = column(ids_ref, 0), column(ids_ref, 1)
    named = jnp.where((lanes == first) | (lanes == second), 1.0, 0.0)
    r0, r1 = iota((BOTH, BOTH), 0), iota((BOTH, BOTH), 1)
    earlier = jnp.where((r1 < r0) & ((r1 < ROWS) == (r0 < ROWS)), 1.0, 0.0)
    rank = dot(earlier.astype(BF), named.astype(BF))
    offset = jnp.where(in_fwd[:, 0:1], 0, CAP)
    slots = []
    for chosen in (first, second):
        taken = jnp.sum(jnp.where(lanes == chosen, rank, 0.0), axis=1, keepdims=True)
        slots.append(taken.astype(jnp.int32) + offset)
    ahead = [
        jnp.bitwise_and(chosen - place_ref[1] + EXPERTS, EXPERTS - 1) for chosen in (first, second)
    ]
    fields = [ahead[0].astype(F32), slots[0].astype(F32), ahead[1].astype(F32), slots[1].astype(F32)]
    fields += split_gate(column(gates_ref, 0))
    fields += split_gate(column(gates_ref, 1))
    fields += [first.astype(F32), second.astype(F32)]
    meta = jnp.zeros((BOTH, EXTRA), F32)
    for place, field in enumerate(fields):
        meta = jnp.where(lanes == place, field, meta)
    meta_ref[...] = meta

    def as_row(column):
        return jnp.sum(jnp.where(r0 == r1, column, 0), axis=0, keepdims=True)

    target = iota((EXPERTS * BOTH, BOTH), 0)
    source = iota((EXPERTS * BOTH, BOTH), 1)
    routed = (target == as_row(first * BOTH + slots[0])) | (
        target == as_row(second * BOTH + slots[1])
    )
    copied = target == source
    for part in range(1, COLS):
        copied = copied | (target == source + part * BOTH)
    routed_f = jnp.where(routed, 1.0, 0.0)
    copied_f = jnp.where(copied, 1.0, 0.0)
    pick = jnp.where(place_ref[0] == 0, routed_f, copied_f).astype(BF)
    values = jnp.concatenate([fwd_ref[...].astype(F32), bwd_ref[...].astype(F32)], axis=0)
    features = values.shape[1]
    inverse = lax.rsqrt(jnp.mean(values * values, axis=-1, keepdims=True) + EPS)
    normed = (values * inverse * gain_ref[...]).astype(BF)
    for start in range(0, features, CHUNK):
        out_ref[:, start : start + CHUNK] = dot(pick, normed[:, start : start + CHUNK]).astype(BF)
    out_ref[:, features:] = dot(pick, meta.astype(BF)).astype(BF)


def slot_targets(place_ref, rows_ref):
    total = EXPERTS * BOTH
    features = rows_ref.shape[1] - EXTRA
    extra = rows_ref[:, features:].astype(F32)
    row = iota((total, 1), 0)
    part = (
        (row >= BOTH).astype(jnp.int32)
        + (row >= 2 * BOTH).astype(jnp.int32)
        + (row >= 3 * BOTH).astype(jnp.int32)
    )
    place = row - part * BOTH
    on_first = place_ref[0] == 0
    packed = jnp.where(place < SLOTS, part * SLOTS + place, -EXPERTS * LANES)
    found = []
    for k in range(COLS):
        there, high, low = -1, 0.0, 0.0
        if k < 2:
            expert = extra[:, 2 * k : 2 * k + 1].astype(jnp.int32)
            slot = extra[:, 2 * k + 1 : 2 * k + 2].astype(jnp.int32)
            there = expert * LANES + part * SLOTS + slot
            high = extra[:, 4 + 2 * k : 5 + 2 * k]
            low = extra[:, 5 + 2 * k : 6 + 2 * k]
        target = jnp.where(on_first, packed + k * LANES, there)
        found.append((target, jnp.where(on_first, 1.0, high), jnp.where(on_first, 0.0, low)))
    return found


def move(pick_ref, rows_ref, parts, out_refs):
    width = rows_ref.shape[1] - EXTRA
    for start in range(0, width, CHUNK):
        cut = slice(start, start + CHUNK)
        rows = rows_ref[:, cut]
        for part, out_ref in zip(parts, out_refs):
            moved = dot(pick_ref[part * LANES : (part + 1) * LANES, :], rows)
            out_ref[:, cut] = moved[: COLS * SLOTS].astype(BF)


def near_kernel(place_ref, rows_ref, first_ref, third_ref, pick_ref, token_ref):
    token_ref[...] = jnp.zeros_like(token_ref)
    column = iota((EXPERTS * BOTH, EXPERTS * LANES), 1)
    pick = jnp.zeros(column.shape, F32)
    for target, _, _ in slot_targets(place_ref, rows_ref):
        pick = jnp.where(column == target, 1.0, pick)
    pick_ref[...] = pick.T.astype(BF)
    move(pick_ref, rows_ref, (1, 3), (first_ref, third_ref))


def rest_kernel(place_ref, rows_ref, pick_ref, _, own_ref, back_ref):
    column = iota((EXPERTS * BOTH, EXPERTS * LANES), 1)
    high_m = jnp.zeros(column.shape, F32)
    low_m = jnp.zeros(column.shape, F32)
    for target, high, low in slot_targets(place_ref, rows_ref):
        here = column == target
        high_m = jnp.where(here, high, high_m)
        low_m = jnp.where(here, low, low_m)
    back_ref[:, : EXPERTS * LANES] = high_m.astype(BF)
    back_ref[:, EXPERTS * LANES :] = low_m.astype(BF)
    move(pick_ref, rows_ref, (0,), (own_ref,))


def far_kernel(rows_ref, pick_ref, *refs):
    move(pick_ref, rows_ref, (2,), refs[-1:])


def expert_kernel(count, *refs):
    rows_refs = refs[:count]
    gate_ref, up_ref, down_ref, other_ref = refs[count : count + 4]
    out_refs, token_ref = refs[-1 - count : -1], refs[-1]
    token_ref[...] = jnp.zeros_like(token_ref)
    features, width = gate_ref.shape
    hidden = []
    for rows_ref in rows_refs:
        gate, up = 0.0, 0.0
        for start in range(0, features, WIDE):
            cut = slice(start, start + WIDE)
            more = slice(features + start, features + start + WIDE)
            rows = rows_ref[:, cut]
            gate += dot(rows, jnp.concatenate([gate_ref[cut, :], other_ref[cut, :]], axis=1))
            up += dot(rows, jnp.concatenate([up_ref[cut, :], other_ref[more, :]], axis=1))
        hidden.append((gate / (1.0 + jnp.exp(-gate)) * up).astype(BF))
    for start in range(0, features, CHUNK):
        cut = slice(start, start + CHUNK)
        at = [2 * features + start + i * width for i in range(CHUNK // width)]
        other = jnp.concatenate([other_ref[i : i + width, :] for i in at], axis=1)
        down = jnp.concatenate([down_ref[:, cut], other], axis=0)
        for rows, out_ref in zip(hidden, out_refs):
            out_ref[:, cut] = dot(rows, down).astype(BF)


def gather_kernel(parts, last, back_ref, *refs):
    rows_refs, so_far_ref, out_ref = refs[: len(parts)], refs[len(parts)], refs[-1]
    width = rows_refs[0].shape[1]
    used = COLS * SLOTS
    for start in range(0, width, CHUNK):
        cut = slice(start, min(start + CHUNK, width))
        total = so_far_ref[:, cut] if last else 0.0
        for part, ref in zip(parts, rows_refs):
            high = slice(part * LANES, part * LANES + used)
            low = slice((EXPERTS + part) * LANES, (EXPERTS + part) * LANES + used)
            rows = ref[:, cut]
            total += dot(back_ref[:, high], rows) + dot(back_ref[:, low], rows)
        out_ref[:, cut] = total.astype(out_ref.dtype)


def finish_kernel(place_ref, meta_ref, rows_ref, fwd_ref, bwd_ref, _, of_ref, ob_ref, leave_ref):
    meta = meta_ref[...]
    total = EXPERTS * BOTH
    column = iota((BOTH, total), 1)
    row = iota((BOTH, total), 0)
    high = jnp.zeros((BOTH, total), F32)
    low = jnp.zeros((BOTH, total), F32)
    for k in range(2):
        there = (meta[:, 8 + k : 9 + k] * BOTH + meta[:, 2 * k + 1 : 2 * k + 2]).astype(jnp.int32)
        high = jnp.where(column == there, meta[:, 4 + 2 * k : 5 + 2 * k], high)
        low = jnp.where(column == there, meta[:, 5 + 2 * k : 6 + 2 * k], low)
    same = column == row
    for part in range(1, COLS):
        same = same | (column == row + part * BOTH)
    ones = jnp.where(same, 1.0, 0.0)
    on_first = place_ref[0] == 0
    high = jnp.where(on_first, high, ones).astype(BF)
    low = jnp.where(on_first, low, 0.0).astype(BF)
    at_start = place_ref[2] == 0
    width = fwd_ref.shape[1]
    for start in range(0, width, CHUNK):
        cut = slice(start, min(start + CHUNK, width))
        rows = rows_ref[:, cut]
        mixture = dot(high, rows) + dot(low, rows)
        forward = fwd_ref[:, cut].astype(F32) + mixture[:ROWS]
        backward = bwd_ref[:, cut].astype(F32) + mixture[ROWS:]
        of_ref[:, cut] = forward.astype(BF)
        ob_ref[:, cut] = backward.astype(BF)
        leave_ref[:, cut] = jnp.where(at_start, backward, forward).astype(BF)


def enter_kernel(place_ref, fwd_ref, bwd_ref, _, out_ref):
    out_ref[:, :ROWS, :] = fwd_ref[...]
    out_ref[:, ROWS:, :] = bwd_ref[...]


def ends_kernel(place_ref, own_ref, other_ref, out_ref):
    count, _, part = out_ref.shape
    for r in range(count):
        near, far = [slice(j * part, (j + 1) * part) for j in (r, 2 * count - 1 - r)]

        @pl.when(place_ref[2] == 0)
        def _():
            out_ref[r, :ROWS, :] = other_ref[:, near]
            out_ref[r, ROWS:, :] = own_ref[:, near]

        @pl.when(place_ref[2] != 0)
        def _():
            out_ref[r, :ROWS, :] = own_ref[:, far]
            out_ref[r, ROWS:, :] = other_ref[:, far]


def entered_kernel(place_ref, held_ref, got_ref, out_ref):
    count, _, part = held_ref.shape
    at_start = place_ref[2] == 0
    for r in range(count):
        near, far = [slice(j * part, (j + 1) * part) for j in (r, 2 * count - 1 - r)]

        @pl.when(at_start)
        def _():
            out_ref[:, near] = held_ref[r, :ROWS, :]
            out_ref[:, far] = got_ref[r]

        @pl.when(jnp.logical_not(at_start))
        def _():
            out_ref[:, near] = got_ref[r]
            out_ref[:, far] = held_ref[r, ROWS:, :]


SMEM = pl.BlockSpec(memory_space=pltpu.SMEM)


def params(mib=20):
    return pltpu.CompilerParams(vmem_limit_bytes=mib * 1024 * 1024)


VMEM = pl.BlockSpec(memory_space=pltpu.VMEM)
ANY = pl.BlockSpec(memory_space=pl.ANY)


def shape(rows, columns, dtype=BF):
    return jax.ShapeDtypeStruct((rows, columns), dtype)


def make_send(place, fwd, bwd, gain, ids, gates):
    features = fwd.shape[1]
    return pl.pallas_call(
        send_kernel,
        out_shape=(shape(EXPERTS * BOTH, features + EXTRA), shape(BOTH, EXTRA, F32)),
        in_specs=[SMEM] + [VMEM] * 5,
        out_specs=(VMEM, VMEM),
        compiler_params=params(),
        name="normed",
    )(place, fwd, bwd, gain, ids, gates)


def make_near(place, rows):
    features = rows.shape[1] - EXTRA
    total = EXPERTS * BOTH
    return pl.pallas_call(
        near_kernel,
        out_shape=(shape(COLS * SLOTS, features),) * 2
        + (shape(EXPERTS * LANES, total), shape(8, LANES, jnp.int32)),
        in_specs=[SMEM, VMEM],
        out_specs=(VMEM,) * 4,
        compiler_params=params(),
        name="near",
    )(place, rows)


def pack_kernel(gate_ref, up_ref, down_ref, _, out_ref):
    features, width = gate_ref.shape
    out_ref[:features, :] = gate_ref[...]
    out_ref[features : 2 * features, :] = up_ref[...]
    for i in range(features // width):
        at = 2 * features + i * width
        out_ref[at : at + width, :] = down_ref[:, i * width : (i + 1) * width]


def make_pack(gate, up, down, before):
    features, width = gate.shape
    return pl.pallas_call(
        pack_kernel,
        out_shape=shape(3 * features, width),
        in_specs=[VMEM] * 3 + [ANY],
        out_specs=VMEM,
        compiler_params=params(),
        name="pack",
    )(gate, up, down, before)


def make_rest(place, rows, pick, before):
    features = rows.shape[1] - EXTRA
    return pl.pallas_call(
        rest_kernel,
        out_shape=(
            shape(COLS * SLOTS, features),
            shape(EXPERTS * BOTH, 2 * EXPERTS * LANES),
        ),
        in_specs=[SMEM, VMEM, VMEM, ANY],
        out_specs=(VMEM, VMEM),
        compiler_params=params(),
        name="rest",
    )(place, rows, pick, before)


def make_far(rows, pick, *before):
    return pl.pallas_call(
        far_kernel,
        out_shape=shape(COLS * SLOTS, rows.shape[1] - EXTRA),
        in_specs=[VMEM, VMEM] + [ANY] * len(before),
        out_specs=VMEM,
        compiler_params=params(),
        name="far",
    )(rows, pick, *before)


def run_experts(blocks, own, packed, *before):
    count = len(blocks)

    def body(*refs):
        expert_kernel(count, *refs)

    return pl.pallas_call(
        body,
        out_shape=(shape(*blocks[0].shape),) * count + (shape(8, LANES, jnp.int32),),
        in_specs=[VMEM] * (count + 4) + [ANY] * len(before),
        out_specs=(VMEM,) * (count + 1),
        compiler_params=params(),
        name="experts",
    )(*blocks, *own, packed, *before)


def make_gather(back, blocks, parts, so_far=None, before=()):
    features = blocks[0].shape[1]
    total = back.shape[0]
    last = so_far is not None

    def body(*refs):
        gather_kernel(parts, last, *refs)

    return pl.pallas_call(
        body,
        out_shape=shape(total, features, BF if last else F32),
        in_specs=[VMEM] * (1 + len(blocks) + last) + [ANY] * len(before),
        out_specs=VMEM,
        compiler_params=params(),
        name="gather",
    )(back, *blocks, *([so_far] if last else []), *before)


def make_finish(place, meta, rows, fwd, bwd, before):
    return pl.pallas_call(
        finish_kernel,
        out_shape=(shape(*fwd.shape),) * 3,
        in_specs=[SMEM] + [VMEM] * 4 + [ANY],
        out_specs=(VMEM,) * 3,
        compiler_params=params(),
        name="finish",
    )(place, meta, rows, fwd, bwd, before)


def make_simple(kernel, out, place, *arrays, before=()):
    return pl.pallas_call(
        kernel,
        out_shape=jax.ShapeDtypeStruct(out, BF),
        in_specs=[SMEM] + [VMEM] * len(arrays) + [ANY] * len(before),
        out_specs=VMEM,
        compiler_params=params(),
        name="blocks",
    )(place, *arrays, *before)


def shifted(block, distance, count):
    route = [(i, i + distance) for i in range(count) if 0 <= i + distance < count]
    return lax.ppermute(block, "pp", route)


def swapped(block, count):
    return lax.ppermute(block, "pp", [(0, count - 1), (count - 1, 0)])


def mirrored(pairs, sections):
    return pairs + [(sections - 1 - i, sections - 1 - j) for i, j in pairs]


def from_other_core(block):
    return lax.ppermute(block, "ep", [(i, i ^ 1) for i in range(lax.axis_size("ep"))])


def inward(held, bit, radix, sections):
    got = []
    for k in range(1, radix):
        pairs = [(i + k * bit, i) for i in range(0, sections // 2, radix * bit)]
        got.append(lax.ppermute(held, "pp", mirrored(pairs, sections)))
    return jnp.concatenate([held] + got, axis=0), got[-1]


def outward(own, place, sections):
    def move(block, *pairs):
        return lax.ppermute(block, "pp", mirrored(list(pairs), sections))

    to4, to6, to2 = [move(own[r : r + 2], (0, r)) for r in (4, 6, 2)]
    pair = jnp.where(place >= 6, to6, jnp.where(place >= 4, to4, to2))
    pair = jnp.where(place < 2, own[:2], pair)
    odd = move(pair[1:], (0, 1), (2, 3), (4, 5), (6, 7))
    return jnp.where((place & 1) == 1, odd[0], pair[0])


def body(
    state_fwd,
    state_bwd,
    enter_fwd,
    enter_bwd,
    norm_gain,
    w_gate,
    w_up,
    w_down,
    route_ids,
    route_gates,
):
    sections = lax.axis_size("pp")
    section = lax.axis_index("pp")
    position = lax.axis_index("ep")
    place = jnp.stack([position % 2, position // (2 * COLS), section]).astype(jnp.int32)
    fwd, bwd = state_fwd[0], state_bwd[0]
    features = fwd.shape[1]
    part = features // sections
    ids = route_ids[0, 0].transpose(0, 2, 1)
    gates = route_gates[0, 0].transpose(0, 2, 1)

    sent, meta = make_send(place, fwd, bwd, norm_gain, ids, gates)
    rows = exchange(sent)
    send1, send3, pick, token = make_near(place, rows)
    near, far = hop(send1, 1), hop(send3, 3)
    own = (w_gate[0], w_up[0], w_down[0])
    weights = own, from_other_core(make_pack(*own, pick))
    send0, back = make_rest(place, rows, pick, weights[1])
    done0, token = run_experts([send0], *weights)
    half = sections // 2
    at_start = section == 0
    entering = make_simple(
        enter_kernel, (1, BOTH, part), place, enter_fwd, enter_bwd, before=(weights[1],)
    )
    held, got = inward(entering, 1, 2, sections)
    last = hop(make_far(rows, pick, near, far, got, token), 2)
    done1, done3, token = run_experts([near, far], *weights)
    back1, back3 = hop(done1, -1), hop(done3, -3)
    done2, token = run_experts([last], *weights, token)
    back2 = hop(done2, -2)

    held, _ = inward(held, 2, 2, sections)
    held, got = inward(held, 4, 2, sections)
    begun = make_gather(back, [done0, back1, back3], (0, 1, 3))
    gathered = make_gather(back, [back2], (2,), begun, (got,))
    passed_on = jnp.where(at_start, held[:, ROWS:], held[:, :ROWS])
    got = swapped(passed_on, sections)
    rows = exchange(gathered)
    fwd_out, bwd_out, leaving = make_finish(place, meta, rows, fwd, bwd, got)
    entered = make_simple(entered_kernel, (ROWS, features), place, held, got)
    other = swapped(leaving, sections)
    ends = make_simple(ends_kernel, (half, BOTH, part), place, leaving, other)
    mine = outward(ends, jnp.minimum(section, sections - 1 - section), sections)
    from_left, from_right = shifted(fwd_out, 1, sections), shifted(bwd_out, -1, sections)
    fwd_next = jnp.where(at_start, entered, from_left)
    bwd_next = jnp.where(section == sections - 1, entered, from_right)
    return (fwd_next[None], bwd_next[None], mine[None, :ROWS], mine[None, ROWS:])


def solution(mesh):
    placed = (
        P("pp", "ep", None),
        P("pp", "ep", None),
        P(None, "ep", "pp"),
        P(None, "ep", "pp"),
        P("pp", None),
        P("pp", None, "ep"),
        P("pp", None, "ep"),
        P("pp", "ep", None),
        P("pp", None, None, "ep", None),
        P("pp", None, None, "ep", None),
    )
    return jax.shard_map(
        body,
        mesh=mesh,
        in_specs=placed,
        out_specs=(
            P("pp", "ep", None),
            P("pp", "ep", None),
            P(None, "ep", "pp"),
            P(None, "ep", "pp"),
        ),
        check_vma=False,
    )
```

```python
import jax
import jax.numpy as jnp
from jax import lax
from jax.experimental import pallas as pl
from jax.experimental.pallas import tpu as pltpu
from jax.sharding import PartitionSpec as P

EPS = 1e-06
BF = jnp.bfloat16
F32 = jnp.float32
EXPERTS = 4
COLS = 4
CAP = 15
ROWS = 24
BOTH = 2 * ROWS
SLOTS = 2 * CAP
EXTRA = 128
WIDE = 1792
CHUNK = 512
LANES = 128


def device(y, x, core):
    return (y * COLS + x) * 2 + core


def hop(block, distance):
    route = []
    for y in range(EXPERTS):
        for x in range(COLS):
            for core in range(2):
                along_y = core == 1
                there = ((y + distance) % EXPERTS, x) if along_y else (y, (x + distance) % COLS)
                route.append((device(y, x, core), device(*there, core)))
    return lax.ppermute(block, "ep", route)


def rings(along_y):
    groups = []
    for core in range(2):
        if (core == 0) == along_y:
            groups += [[device(y, x, core) for y in range(EXPERTS)] for x in range(COLS)]
        else:
            groups += [[device(y, x, core) for x in range(COLS)] for y in range(EXPERTS)]
    return groups


def exchange(rows):
    return lax.all_to_all(
        rows, "ep", split_axis=0, concat_axis=0, axis_index_groups=rings(True), tiled=True
    )


def iota(shape, dim):
    return lax.broadcasted_iota(jnp.int32, shape, dim)


def dot(a, b):
    return jnp.dot(a, b, preferred_element_type=F32)


def split_gate(gate):
    high = gate.astype(BF).astype(F32)
    return high, (gate - high).astype(BF).astype(F32)


def send_kernel(place_ref, fwd_ref, bwd_ref, gain_ref, ids_ref, gates_ref, out_ref, meta_ref):
    lanes = iota((BOTH, EXTRA), 1)
    row = iota((BOTH, EXTRA), 0)
    in_fwd = row < ROWS
    own = lanes[:, :ROWS] == row[:, :ROWS] - jnp.where(in_fwd[:, :ROWS], 0, ROWS)

    def column(ref, k):
        both = jnp.where(in_fwd[:, :ROWS], ref[0, k : k + 1, :], ref[1, k : k + 1, :])
        return jnp.sum(jnp.where(own, both, jnp.zeros_like(both)), axis=1, keepdims=True)

    first, second = column(ids_ref, 0), column(ids_ref, 1)
    named = jnp.where((lanes == first) | (lanes == second), 1.0, 0.0)
    r0, r1 = iota((BOTH, BOTH), 0), iota((BOTH, BOTH), 1)
    earlier = jnp.where((r1 < r0) & ((r1 < ROWS) == (r0 < ROWS)), 1.0, 0.0)
    rank = dot(earlier.astype(BF), named.astype(BF))
    offset = jnp.where(in_fwd[:, 0:1], 0, CAP)
    slots = []
    for chosen in (first, second):
        taken = jnp.sum(jnp.where(lanes == chosen, rank, 0.0), axis=1, keepdims=True)
        slots.append(taken.astype(jnp.int32) + offset)
    ahead = [
        jnp.bitwise_and(chosen - place_ref[1] + EXPERTS, EXPERTS - 1) for chosen in (first, second)
    ]
    fields = [ahead[0].astype(F32), slots[0].astype(F32), ahead[1].astype(F32), slots[1].astype(F32)]
    fields += split_gate(column(gates_ref, 0))
    fields += split_gate(column(gates_ref, 1))
    fields += [first.astype(F32), second.astype(F32)]
    meta = jnp.zeros((BOTH, EXTRA), F32)
    for place, field in enumerate(fields):
        meta = jnp.where(lanes == place, field, meta)
    meta_ref[...] = meta

    def as_row(column):
        return jnp.sum(jnp.where(r0 == r1, column, 0), axis=0, keepdims=True)

    target = iota((EXPERTS * BOTH, BOTH), 0)
    source = iota((EXPERTS * BOTH, BOTH), 1)
    routed = (target == as_row(first * BOTH + slots[0])) | (
        target == as_row(second * BOTH + slots[1])
    )
    copied = target == source
    for part in range(1, COLS):
        copied = copied | (target == source + part * BOTH)
    routed_f = jnp.where(routed, 1.0, 0.0)
    copied_f = jnp.where(copied, 1.0, 0.0)
    pick = jnp.where(place_ref[0] == 0, routed_f, copied_f).astype(BF)
    values = jnp.concatenate([fwd_ref[...].astype(F32), bwd_ref[...].astype(F32)], axis=0)
    features = values.shape[1]
    inverse = lax.rsqrt(jnp.mean(values * values, axis=-1, keepdims=True) + EPS)
    normed = (values * inverse * gain_ref[...]).astype(BF)
    for start in range(0, features, CHUNK):
        out_ref[:, start : start + CHUNK] = dot(pick, normed[:, start : start + CHUNK]).astype(BF)
    out_ref[:, features:] = dot(pick, meta.astype(BF)).astype(BF)


def slot_targets(place_ref, rows_ref):
    total = EXPERTS * BOTH
    features = rows_ref.shape[1] - EXTRA
    extra = rows_ref[:, features:].astype(F32)
    row = iota((total, 1), 0)
    part = (
        (row >= BOTH).astype(jnp.int32)
        + (row >= 2 * BOTH).astype(jnp.int32)
        + (row >= 3 * BOTH).astype(jnp.int32)
    )
    place = row - part * BOTH
    on_first = place_ref[0] == 0
    packed = jnp.where(place < SLOTS, part * SLOTS + place, -EXPERTS * LANES)
    found = []
    for k in range(COLS):
        there, high, low = -1, 0.0, 0.0
        if k < 2:
            expert = extra[:, 2 * k : 2 * k + 1].astype(jnp.int32)
            slot = extra[:, 2 * k + 1 : 2 * k + 2].astype(jnp.int32)
            there = expert * LANES + part * SLOTS + slot
            high = extra[:, 4 + 2 * k : 5 + 2 * k]
            low = extra[:, 5 + 2 * k : 6 + 2 * k]
        target = jnp.where(on_first, packed + k * LANES, there)
        found.append((target, jnp.where(on_first, 1.0, high), jnp.where(on_first, 0.0, low)))
    return found


def move(pick_ref, rows_ref, parts, out_refs):
    width = rows_ref.shape[1] - EXTRA
    for start in range(0, width, CHUNK):
        cut = slice(start, start + CHUNK)
        rows = rows_ref[:, cut]
        for part, out_ref in zip(parts, out_refs):
            moved = dot(pick_ref[part * LANES : (part + 1) * LANES, :], rows)
            out_ref[:, cut] = moved[: COLS * SLOTS].astype(BF)


def near_kernel(place_ref, rows_ref, first_ref, third_ref, pick_ref, token_ref):
    token_ref[...] = jnp.zeros_like(token_ref)
    column = iota((EXPERTS * BOTH, EXPERTS * LANES), 1)
    pick = jnp.zeros(column.shape, F32)
    for target, _, _ in slot_targets(place_ref, rows_ref):
        pick = jnp.where(column == target, 1.0, pick)
    pick_ref[...] = pick.T.astype(BF)
    move(pick_ref, rows_ref, (1, 3), (first_ref, third_ref))


def rest_kernel(place_ref, rows_ref, pick_ref, _, own_ref, back_ref):
    column = iota((EXPERTS * BOTH, EXPERTS * LANES), 1)
    high_m = jnp.zeros(column.shape, F32)
    low_m = jnp.zeros(column.shape, F32)
    for target, high, low in slot_targets(place_ref, rows_ref):
        here = column == target
        high_m = jnp.where(here, high, high_m)
        low_m = jnp.where(here, low, low_m)
    back_ref[:, : EXPERTS * LANES] = high_m.astype(BF)
    back_ref[:, EXPERTS * LANES :] = low_m.astype(BF)
    move(pick_ref, rows_ref, (0,), (own_ref,))


def far_kernel(rows_ref, pick_ref, *refs):
    move(pick_ref, rows_ref, (2,), refs[-1:])


def expert_kernel(count, *refs):
    rows_refs = refs[:count]
    gate_ref, up_ref, down_ref, other_ref = refs[count : count + 4]
    out_refs, token_ref = refs[-1 - count : -1], refs[-1]
    token_ref[...] = jnp.zeros_like(token_ref)
    features, width = gate_ref.shape
    hidden = []
    for rows_ref in rows_refs:
        gate, up = 0.0, 0.0
        for start in range(0, features, WIDE):
            cut = slice(start, start + WIDE)
            more = slice(features + start, features + start + WIDE)
            rows = rows_ref[:, cut]
            gate += dot(rows, jnp.concatenate([gate_ref[cut, :], other_ref[cut, :]], axis=1))
            up += dot(rows, jnp.concatenate([up_ref[cut, :], other_ref[more, :]], axis=1))
        hidden.append((gate / (1.0 + jnp.exp(-gate)) * up).astype(BF))
    for start in range(0, features, CHUNK):
        cut = slice(start, start + CHUNK)
        at = [2 * features + start + i * width for i in range(CHUNK // width)]
        other = jnp.concatenate([other_ref[i : i + width, :] for i in at], axis=1)
        down = jnp.concatenate([down_ref[:, cut], other], axis=0)
        for rows, out_ref in zip(hidden, out_refs):
            out_ref[:, cut] = dot(rows, down).astype(BF)


def gather_kernel(parts, last, back_ref, *refs):
    rows_refs, so_far_ref, out_ref = refs[: len(parts)], refs[len(parts)], refs[-1]
    width = rows_refs[0].shape[1]
    used = COLS * SLOTS
    for start in range(0, width, CHUNK):
        cut = slice(start, min(start + CHUNK, width))
        total = so_far_ref[:, cut] if last else 0.0
        for part, ref in zip(parts, rows_refs):
            high = slice(part * LANES, part * LANES + used)
            low = slice((EXPERTS + part) * LANES, (EXPERTS + part) * LANES + used)
            rows = ref[:, cut]
            total += dot(back_ref[:, high], rows) + dot(back_ref[:, low], rows)
        out_ref[:, cut] = total.astype(out_ref.dtype)


def finish_kernel(place_ref, meta_ref, rows_ref, fwd_ref, bwd_ref, _, toward_ref, away_ref):
    meta = meta_ref[...]
    total = EXPERTS * BOTH
    column = iota((BOTH, total), 1)
    row = iota((BOTH, total), 0)
    high = jnp.zeros((BOTH, total), F32)
    low = jnp.zeros((BOTH, total), F32)
    for k in range(2):
        there = (meta[:, 8 + k : 9 + k] * BOTH + meta[:, 2 * k + 1 : 2 * k + 2]).astype(jnp.int32)
        high = jnp.where(column == there, meta[:, 4 + 2 * k : 5 + 2 * k], high)
        low = jnp.where(column == there, meta[:, 5 + 2 * k : 6 + 2 * k], low)
    same = column == row
    for part in range(1, COLS):
        same = same | (column == row + part * BOTH)
    ones = jnp.where(same, 1.0, 0.0)
    on_first = place_ref[0] == 0
    high = jnp.where(on_first, high, ones).astype(BF)
    low = jnp.where(on_first, low, 0.0).astype(BF)
    lower = place_ref[3] == 1
    width = fwd_ref.shape[1]
    for start in range(0, width, CHUNK):
        cut = slice(start, min(start + CHUNK, width))
        rows = rows_ref[:, cut]
        mixture = dot(high, rows) + dot(low, rows)
        forward = fwd_ref[:, cut].astype(F32) + mixture[:ROWS]
        backward = bwd_ref[:, cut].astype(F32) + mixture[ROWS:]
        toward_ref[:, cut] = jnp.where(lower, backward, forward).astype(BF)
        away_ref[:, cut] = jnp.where(lower, forward, backward).astype(BF)


def enter_kernel(place_ref, fwd_ref, bwd_ref, _, out_ref):
    out_ref[:, :ROWS, :] = fwd_ref[...]
    out_ref[:, ROWS:, :] = bwd_ref[...]


def ends_kernel(place_ref, own_ref, other_ref, _, out_ref):
    count, _, part = out_ref.shape
    for r in range(count):
        near, far = [slice(j * part, (j + 1) * part) for j in (r, 2 * count - 1 - r)]

        @pl.when(place_ref[2] == 0)
        def _():
            out_ref[r, :ROWS, :] = other_ref[:, near]
            out_ref[r, ROWS:, :] = own_ref[:, near]

        @pl.when(place_ref[2] != 0)
        def _():
            out_ref[r, :ROWS, :] = own_ref[:, far]
            out_ref[r, ROWS:, :] = other_ref[:, far]


def entered_kernel(place_ref, held_ref, got_ref, out_ref):
    count, _, part = held_ref.shape
    at_start = place_ref[2] == 0
    for r in range(count):
        near, far = [slice(j * part, (j + 1) * part) for j in (r, 2 * count - 1 - r)]

        @pl.when(at_start)
        def _():
            out_ref[:, near] = held_ref[r, :ROWS, :]
            out_ref[:, far] = got_ref[r]

        @pl.when(jnp.logical_not(at_start))
        def _():
            out_ref[:, near] = got_ref[r]
            out_ref[:, far] = held_ref[r, ROWS:, :]


SMEM = pl.BlockSpec(memory_space=pltpu.SMEM)


def params(mib=20):
    return pltpu.CompilerParams(vmem_limit_bytes=mib * 1024 * 1024)


VMEM = pl.BlockSpec(memory_space=pltpu.VMEM)
ANY = pl.BlockSpec(memory_space=pl.ANY)


def shape(rows, columns, dtype=BF):
    return jax.ShapeDtypeStruct((rows, columns), dtype)


def make_send(place, fwd, bwd, gain, ids, gates):
    features = fwd.shape[1]
    return pl.pallas_call(
        send_kernel,
        out_shape=(shape(EXPERTS * BOTH, features + EXTRA), shape(BOTH, EXTRA, F32)),
        in_specs=[SMEM] + [VMEM] * 5,
        out_specs=(VMEM, VMEM),
        compiler_params=params(),
        name="normed",
    )(place, fwd, bwd, gain, ids, gates)


def make_near(place, rows):
    features = rows.shape[1] - EXTRA
    total = EXPERTS * BOTH
    return pl.pallas_call(
        near_kernel,
        out_shape=(shape(COLS * SLOTS, features),) * 2
        + (shape(EXPERTS * LANES, total), shape(8, LANES, jnp.int32)),
        in_specs=[SMEM, VMEM],
        out_specs=(VMEM,) * 4,
        compiler_params=params(),
        name="near",
    )(place, rows)


def pack_kernel(gate_ref, up_ref, down_ref, _, out_ref):
    features, width = gate_ref.shape
    out_ref[:features, :] = gate_ref[...]
    out_ref[features : 2 * features, :] = up_ref[...]
    for i in range(features // width):
        at = 2 * features + i * width
        out_ref[at : at + width, :] = down_ref[:, i * width : (i + 1) * width]


def make_pack(gate, up, down, before):
    features, width = gate.shape
    return pl.pallas_call(
        pack_kernel,
        out_shape=shape(3 * features, width),
        in_specs=[VMEM] * 3 + [ANY],
        out_specs=VMEM,
        compiler_params=params(),
        name="pack",
    )(gate, up, down, before)


def make_rest(place, rows, pick, before):
    features = rows.shape[1] - EXTRA
    return pl.pallas_call(
        rest_kernel,
        out_shape=(
            shape(COLS * SLOTS, features),
            shape(EXPERTS * BOTH, 2 * EXPERTS * LANES),
        ),
        in_specs=[SMEM, VMEM, VMEM, ANY],
        out_specs=(VMEM, VMEM),
        compiler_params=params(),
        name="rest",
    )(place, rows, pick, before)


def make_far(rows, pick, *before):
    return pl.pallas_call(
        far_kernel,
        out_shape=shape(COLS * SLOTS, rows.shape[1] - EXTRA),
        in_specs=[VMEM, VMEM] + [ANY] * len(before),
        out_specs=VMEM,
        compiler_params=params(),
        name="far",
    )(rows, pick, *before)


def run_experts(blocks, own, packed, *before):
    count = len(blocks)

    def body(*refs):
        expert_kernel(count, *refs)

    return pl.pallas_call(
        body,
        out_shape=(shape(*blocks[0].shape),) * count + (shape(8, LANES, jnp.int32),),
        in_specs=[VMEM] * (count + 4) + [ANY] * len(before),
        out_specs=(VMEM,) * (count + 1),
        compiler_params=params(),
        name="experts",
    )(*blocks, *own, packed, *before)


def make_gather(back, blocks, parts, so_far=None, before=()):
    features = blocks[0].shape[1]
    total = back.shape[0]
    last = so_far is not None

    def body(*refs):
        gather_kernel(parts, last, *refs)

    return pl.pallas_call(
        body,
        out_shape=shape(total, features, BF if last else F32),
        in_specs=[VMEM] * (1 + len(blocks) + last) + [ANY] * len(before),
        out_specs=VMEM,
        compiler_params=params(),
        name="gather",
    )(back, *blocks, *([so_far] if last else []), *before)


def make_finish(place, meta, rows, fwd, bwd, before):
    return pl.pallas_call(
        finish_kernel,
        out_shape=(shape(*fwd.shape),) * 2,
        in_specs=[SMEM] + [VMEM] * 4 + [ANY],
        out_specs=(VMEM,) * 2,
        compiler_params=params(),
        name="finish",
    )(place, meta, rows, fwd, bwd, before)


def make_simple(kernel, out, place, *arrays, before=()):
    return pl.pallas_call(
        kernel,
        out_shape=jax.ShapeDtypeStruct(out, BF),
        in_specs=[SMEM] + [VMEM] * len(arrays) + [ANY] * len(before),
        out_specs=VMEM,
        compiler_params=params(),
        name="blocks",
    )(place, *arrays, *before)


def move_pp(block, pairs, sections):
    return lax.ppermute(block, "pp", mirrored(pairs, sections))


def swapped(block, count):
    return lax.ppermute(block, "pp", [(0, count - 1), (count - 1, 0)])


def mirrored(pairs, sections):
    return pairs + [(sections - 1 - i, sections - 1 - j) for i, j in pairs]


def from_other_core(block):
    return lax.ppermute(block, "ep", [(i, i ^ 1) for i in range(lax.axis_size("ep"))])


def inward(held, bit, radix, sections):
    got = []
    for k in range(1, radix):
        pairs = [(i + k * bit, i) for i in range(0, sections // 2, radix * bit)]
        got.append(lax.ppermute(held, "pp", mirrored(pairs, sections)))
    return jnp.concatenate([held] + got, axis=0), got[-1]


def outward(own, place, sections):
    def move(block, *pairs):
        return lax.ppermute(block, "pp", mirrored(list(pairs), sections))

    to4, to6, to2 = [move(own[r : r + 2], (0, r)) for r in (4, 6, 2)]
    pair = jnp.where(place >= 6, to6, jnp.where(place >= 4, to4, to2))
    pair = jnp.where(place < 2, own[:2], pair)
    odd = move(pair[1:], (0, 1), (2, 3), (4, 5), (6, 7))
    return jnp.where((place & 1) == 1, odd[0], pair[0])


def body(
    state_fwd,
    state_bwd,
    enter_fwd,
    enter_bwd,
    norm_gain,
    w_gate,
    w_up,
    w_down,
    route_ids,
    route_gates,
):
    sections = lax.axis_size("pp")
    section = lax.axis_index("pp")
    position = lax.axis_index("ep")
    half = sections // 2
    lower = section < half
    place = jnp.stack([position % 2, position // (2 * COLS), section, lower]).astype(jnp.int32)
    fwd, bwd = state_fwd[0], state_bwd[0]
    features = fwd.shape[1]
    part = features // sections
    ids = route_ids[0, 0].transpose(0, 2, 1)
    gates = route_gates[0, 0].transpose(0, 2, 1)

    sent, meta = make_send(place, fwd, bwd, norm_gain, ids, gates)
    rows = exchange(sent)
    send1, send3, pick, token = make_near(place, rows)
    near, far = hop(send1, 1), hop(send3, 3)
    own = (w_gate[0], w_up[0], w_down[0])
    weights = own, from_other_core(make_pack(*own, pick))
    send0, back = make_rest(place, rows, pick, weights[1])
    done0, token = run_experts([send0], *weights)
    at_start = section == 0
    entering = make_simple(
        enter_kernel, (1, BOTH, part), place, enter_fwd, enter_bwd, before=(weights[1],)
    )
    held, got = inward(entering, 1, 2, sections)
    last = hop(make_far(rows, pick, near, far, got, token), 2)
    done1, done3, token = run_experts([near, far], *weights)
    back1, back3 = hop(done1, -1), hop(done3, -3)
    done2, token = run_experts([last], *weights, token)
    back2 = hop(done2, -2)

    held, _ = inward(held, 2, 2, sections)
    held, got = inward(held, 4, 2, sections)
    begun = make_gather(back, [done0, back1, back3], (0, 1, 3))
    gathered = make_gather(back, [back2], (2,), begun, (got,))
    passed_on = jnp.where(at_start, held[:, ROWS:], held[:, :ROWS])
    got = swapped(passed_on, sections)
    rows = exchange(gathered)
    toward, away = make_finish(place, meta, rows, fwd, bwd, got)
    entered = make_simple(entered_kernel, (ROWS, features), place, held, got)
    inner = move_pp(toward, [(i, i - 1) for i in range(1, half)], sections)
    other = swapped(toward, sections)
    ends = make_simple(ends_kernel, (half, BOTH, part), place, toward, other, before=(inner,))
    mine = outward(ends, jnp.minimum(section, sections - 1 - section), sections)
    outer = move_pp(away, [(i, i + 1) for i in range(half - 1)], sections)
    middle = move_pp(away, [(half - 1, half)], sections)
    inner = jnp.where((section == half - 1) | (section == half), middle, inner)
    outer = jnp.where(at_start | (section == sections - 1), entered, outer)
    fwd_next = jnp.where(lower, outer, inner)
    bwd_next = jnp.where(lower, inner, outer)
    return (fwd_next[None], bwd_next[None], mine[None, :ROWS], mine[None, ROWS:])


def solution(mesh):
    placed = (
        P("pp", "ep", None),
        P("pp", "ep", None),
        P(None, "ep", "pp"),
        P(None, "ep", "pp"),
        P("pp", None),
        P("pp", None, "ep"),
        P("pp", None, "ep"),
        P("pp", "ep", None),
        P("pp", None, None, "ep", None),
        P("pp", None, None, "ep", None),
    )
    return jax.shard_map(
        body,
        mesh=mesh,
        in_specs=placed,
        out_specs=(
            P("pp", "ep", None),
            P("pp", "ep", None),
            P(None, "ep", "pp"),
            P(None, "ep", "pp"),
        ),
        check_vma=False,
    )
```

```python
import jax
import jax.numpy as jnp
from jax import lax
from jax.experimental import pallas as pl
from jax.experimental.pallas import tpu as pltpu
from jax.sharding import PartitionSpec as P

EPS = 1e-06
BF = jnp.bfloat16
F32 = jnp.float32
EXPERTS = 4
COLS = 4
CAP = 15
ROWS = 24
BOTH = 2 * ROWS
SLOTS = 2 * CAP
EXTRA = 128
WIDE = 1792
CHUNK = 512
LANES = 128


def device(y, x, core):
    return (y * COLS + x) * 2 + core


def hop(block, distance):
    route = []
    for y in range(EXPERTS):
        for x in range(COLS):
            for core in range(2):
                along_y = core == 1
                there = ((y + distance) % EXPERTS, x) if along_y else (y, (x + distance) % COLS)
                route.append((device(y, x, core), device(*there, core)))
    return lax.ppermute(block, "ep", route)


def rings(along_y):
    groups = []
    for core in range(2):
        if (core == 0) == along_y:
            groups += [[device(y, x, core) for y in range(EXPERTS)] for x in range(COLS)]
        else:
            groups += [[device(y, x, core) for x in range(COLS)] for y in range(EXPERTS)]
    return groups


def exchange(rows):
    return lax.all_to_all(
        rows, "ep", split_axis=0, concat_axis=0, axis_index_groups=rings(True), tiled=True
    )


def iota(shape, dim):
    return lax.broadcasted_iota(jnp.int32, shape, dim)


def dot(a, b):
    return jnp.dot(a, b, preferred_element_type=F32)


def split_gate(gate):
    high = gate.astype(BF).astype(F32)
    return high, (gate - high).astype(BF).astype(F32)


def send_kernel(place_ref, fwd_ref, bwd_ref, gain_ref, ids_ref, gates_ref, out_ref, meta_ref):
    lanes = iota((BOTH, EXTRA), 1)
    row = iota((BOTH, EXTRA), 0)
    in_fwd = row < ROWS
    own = lanes[:, :ROWS] == row[:, :ROWS] - jnp.where(in_fwd[:, :ROWS], 0, ROWS)

    def column(ref, k):
        both = jnp.where(in_fwd[:, :ROWS], ref[0, k : k + 1, :], ref[1, k : k + 1, :])
        return jnp.sum(jnp.where(own, both, jnp.zeros_like(both)), axis=1, keepdims=True)

    first, second = column(ids_ref, 0), column(ids_ref, 1)
    named = jnp.where((lanes == first) | (lanes == second), 1.0, 0.0)
    r0, r1 = iota((BOTH, BOTH), 0), iota((BOTH, BOTH), 1)
    earlier = jnp.where((r1 < r0) & ((r1 < ROWS) == (r0 < ROWS)), 1.0, 0.0)
    rank = dot(earlier.astype(BF), named.astype(BF))
    offset = jnp.where(in_fwd[:, 0:1], 0, CAP)
    slots = []
    for chosen in (first, second):
        taken = jnp.sum(jnp.where(lanes == chosen, rank, 0.0), axis=1, keepdims=True)
        slots.append(taken.astype(jnp.int32) + offset)
    ahead = [
        jnp.bitwise_and(chosen - place_ref[1] + EXPERTS, EXPERTS - 1) for chosen in (first, second)
    ]
    fields = [ahead[0].astype(F32), slots[0].astype(F32), ahead[1].astype(F32), slots[1].astype(F32)]
    fields += split_gate(column(gates_ref, 0))
    fields += split_gate(column(gates_ref, 1))
    fields += [first.astype(F32), second.astype(F32)]
    meta = jnp.zeros((BOTH, EXTRA), F32)
    for place, field in enumerate(fields):
        meta = jnp.where(lanes == place, field, meta)
    meta_ref[...] = meta

    def as_row(column):
        return jnp.sum(jnp.where(r0 == r1, column, 0), axis=0, keepdims=True)

    target = iota((EXPERTS * BOTH, BOTH), 0)
    source = iota((EXPERTS * BOTH, BOTH), 1)
    routed = (target == as_row(first * BOTH + slots[0])) | (
        target == as_row(second * BOTH + slots[1])
    )
    copied = target == source
    for part in range(1, COLS):
        copied = copied | (target == source + part * BOTH)
    routed_f = jnp.where(routed, 1.0, 0.0)
    copied_f = jnp.where(copied, 1.0, 0.0)
    pick = jnp.where(place_ref[0] == 0, routed_f, copied_f).astype(BF)
    values = jnp.concatenate([fwd_ref[...].astype(F32), bwd_ref[...].astype(F32)], axis=0)
    features = values.shape[1]
    inverse = lax.rsqrt(jnp.mean(values * values, axis=-1, keepdims=True) + EPS)
    normed = (values * inverse * gain_ref[...]).astype(BF)
    for start in range(0, features, CHUNK):
        out_ref[:, start : start + CHUNK] = dot(pick, normed[:, start : start + CHUNK]).astype(BF)
    out_ref[:, features:] = dot(pick, meta.astype(BF)).astype(BF)


def slot_targets(place_ref, rows_ref):
    total = EXPERTS * BOTH
    features = rows_ref.shape[1] - EXTRA
    extra = rows_ref[:, features:].astype(F32)
    row = iota((total, 1), 0)
    part = (
        (row >= BOTH).astype(jnp.int32)
        + (row >= 2 * BOTH).astype(jnp.int32)
        + (row >= 3 * BOTH).astype(jnp.int32)
    )
    place = row - part * BOTH
    on_first = place_ref[0] == 0
    packed = jnp.where(place < SLOTS, part * SLOTS + place, -EXPERTS * LANES)
    found = []
    for k in range(COLS):
        there, high, low = -1, 0.0, 0.0
        if k < 2:
            expert = extra[:, 2 * k : 2 * k + 1].astype(jnp.int32)
            slot = extra[:, 2 * k + 1 : 2 * k + 2].astype(jnp.int32)
            there = expert * LANES + part * SLOTS + slot
            high = extra[:, 4 + 2 * k : 5 + 2 * k]
            low = extra[:, 5 + 2 * k : 6 + 2 * k]
        target = jnp.where(on_first, packed + k * LANES, there)
        found.append((target, jnp.where(on_first, 1.0, high), jnp.where(on_first, 0.0, low)))
    return found


def move(pick_ref, rows_ref, parts, out_refs):
    width = rows_ref.shape[1] - EXTRA
    for start in range(0, width, CHUNK):
        cut = slice(start, start + CHUNK)
        rows = rows_ref[:, cut]
        for part, out_ref in zip(parts, out_refs):
            moved = dot(pick_ref[part * LANES : (part + 1) * LANES, :], rows)
            out_ref[:, cut] = moved[: COLS * SLOTS].astype(BF)


def near_kernel(place_ref, rows_ref, first_ref, third_ref, pick_ref, token_ref):
    token_ref[...] = jnp.zeros_like(token_ref)
    column = iota((EXPERTS * BOTH, EXPERTS * LANES), 1)
    pick = jnp.zeros(column.shape, F32)
    for target, _, _ in slot_targets(place_ref, rows_ref):
        pick = jnp.where(column == target, 1.0, pick)
    pick_ref[...] = pick.T.astype(BF)
    move(pick_ref, rows_ref, (1, 3), (first_ref, third_ref))


def rest_kernel(place_ref, rows_ref, pick_ref, _, own_ref, back_ref):
    column = iota((EXPERTS * BOTH, EXPERTS * LANES), 1)
    high_m = jnp.zeros(column.shape, F32)
    low_m = jnp.zeros(column.shape, F32)
    for target, high, low in slot_targets(place_ref, rows_ref):
        here = column == target
        high_m = jnp.where(here, high, high_m)
        low_m = jnp.where(here, low, low_m)
    back_ref[:, : EXPERTS * LANES] = high_m.astype(BF)
    back_ref[:, EXPERTS * LANES :] = low_m.astype(BF)
    move(pick_ref, rows_ref, (0,), (own_ref,))


def far_kernel(rows_ref, pick_ref, *refs):
    move(pick_ref, rows_ref, (2,), refs[-1:])


def expert_kernel(count, *refs):
    rows_refs = refs[:count]
    gate_ref, up_ref, down_ref, other_ref = refs[count : count + 4]
    out_refs, token_ref = refs[-1 - count : -1], refs[-1]
    token_ref[...] = jnp.zeros_like(token_ref)
    features, width = gate_ref.shape
    hidden = []
    for rows_ref in rows_refs:
        gate, up = 0.0, 0.0
        for start in range(0, features, WIDE):
            cut = slice(start, start + WIDE)
            more = slice(features + start, features + start + WIDE)
            rows = rows_ref[:, cut]
            gate += dot(rows, jnp.concatenate([gate_ref[cut, :], other_ref[cut, :]], axis=1))
            up += dot(rows, jnp.concatenate([up_ref[cut, :], other_ref[more, :]], axis=1))
        hidden.append((gate / (1.0 + jnp.exp(-gate)) * up).astype(BF))
    for start in range(0, features, CHUNK):
        cut = slice(start, start + CHUNK)
        at = [2 * features + start + i * width for i in range(CHUNK // width)]
        other = jnp.concatenate([other_ref[i : i + width, :] for i in at], axis=1)
        down = jnp.concatenate([down_ref[:, cut], other], axis=0)
        for rows, out_ref in zip(hidden, out_refs):
            out_ref[:, cut] = dot(rows, down).astype(BF)


def gather_kernel(parts, last, back_ref, *refs):
    rows_refs, so_far_ref, out_ref = refs[: len(parts)], refs[len(parts)], refs[-1]
    width = rows_refs[0].shape[1]
    used = COLS * SLOTS
    for start in range(0, width, CHUNK):
        cut = slice(start, min(start + CHUNK, width))
        total = so_far_ref[:, cut] if last else 0.0
        for part, ref in zip(parts, rows_refs):
            high = slice(part * LANES, part * LANES + used)
            low = slice((EXPERTS + part) * LANES, (EXPERTS + part) * LANES + used)
            rows = ref[:, cut]
            total += dot(back_ref[:, high], rows) + dot(back_ref[:, low], rows)
        out_ref[:, cut] = total.astype(out_ref.dtype)


def finish_kernel(place_ref, meta_ref, rows_ref, fwd_ref, bwd_ref, _, toward_ref, away_ref):
    meta = meta_ref[...]
    total = EXPERTS * BOTH
    column = iota((BOTH, total), 1)
    row = iota((BOTH, total), 0)
    high = jnp.zeros((BOTH, total), F32)
    low = jnp.zeros((BOTH, total), F32)
    for k in range(2):
        there = (meta[:, 8 + k : 9 + k] * BOTH + meta[:, 2 * k + 1 : 2 * k + 2]).astype(jnp.int32)
        high = jnp.where(column == there, meta[:, 4 + 2 * k : 5 + 2 * k], high)
        low = jnp.where(column == there, meta[:, 5 + 2 * k : 6 + 2 * k], low)
    same = column == row
    for part in range(1, COLS):
        same = same | (column == row + part * BOTH)
    ones = jnp.where(same, 1.0, 0.0)
    on_first = place_ref[0] == 0
    high = jnp.where(on_first, high, ones).astype(BF)
    low = jnp.where(on_first, low, 0.0).astype(BF)
    lower = place_ref[3] == 1
    width = fwd_ref.shape[1]
    for start in range(0, width, CHUNK):
        cut = slice(start, min(start + CHUNK, width))
        rows = rows_ref[:, cut]
        mixture = dot(high, rows) + dot(low, rows)
        forward = fwd_ref[:, cut].astype(F32) + mixture[:ROWS]
        backward = bwd_ref[:, cut].astype(F32) + mixture[ROWS:]
        toward_ref[:, cut] = jnp.where(lower, backward, forward).astype(BF)
        away_ref[:, cut] = jnp.where(lower, forward, backward).astype(BF)


def enter_kernel(place_ref, fwd_ref, bwd_ref, _, out_ref):
    out_ref[:, :ROWS, :] = fwd_ref[...]
    out_ref[:, ROWS:, :] = bwd_ref[...]


def ends_kernel(place_ref, own_ref, other_ref, *refs):
    out_ref = refs[-1]
    count, _, part = out_ref.shape
    for r in range(count):
        near, far = [slice(j * part, (j + 1) * part) for j in (r, 2 * count - 1 - r)]

        @pl.when(place_ref[2] == 0)
        def _():
            out_ref[r, :ROWS, :] = other_ref[:, near]
            out_ref[r, ROWS:, :] = own_ref[:, near]

        @pl.when(place_ref[2] != 0)
        def _():
            out_ref[r, :ROWS, :] = own_ref[:, far]
            out_ref[r, ROWS:, :] = other_ref[:, far]


def entered_kernel(place_ref, held_ref, got_ref, out_ref):
    count, _, part = held_ref.shape
    at_start = place_ref[2] == 0
    for r in range(count):
        near, far = [slice(j * part, (j + 1) * part) for j in (r, 2 * count - 1 - r)]

        @pl.when(at_start)
        def _():
            out_ref[:, near] = held_ref[r, :ROWS, :]
            out_ref[:, far] = got_ref[r]

        @pl.when(jnp.logical_not(at_start))
        def _():
            out_ref[:, near] = got_ref[r]
            out_ref[:, far] = held_ref[r, ROWS:, :]


SMEM = pl.BlockSpec(memory_space=pltpu.SMEM)


def params(mib=20):
    return pltpu.CompilerParams(vmem_limit_bytes=mib * 1024 * 1024)


VMEM = pl.BlockSpec(memory_space=pltpu.VMEM)
ANY = pl.BlockSpec(memory_space=pl.ANY)


def shape(rows, columns, dtype=BF):
    return jax.ShapeDtypeStruct((rows, columns), dtype)


def make_send(place, fwd, bwd, gain, ids, gates):
    features = fwd.shape[1]
    return pl.pallas_call(
        send_kernel,
        out_shape=(shape(EXPERTS * BOTH, features + EXTRA), shape(BOTH, EXTRA, F32)),
        in_specs=[SMEM] + [VMEM] * 5,
        out_specs=(VMEM, VMEM),
        compiler_params=params(),
        name="normed",
    )(place, fwd, bwd, gain, ids, gates)


def make_near(place, rows):
    features = rows.shape[1] - EXTRA
    total = EXPERTS * BOTH
    return pl.pallas_call(
        near_kernel,
        out_shape=(shape(COLS * SLOTS, features),) * 2
        + (shape(EXPERTS * LANES, total), shape(8, LANES, jnp.int32)),
        in_specs=[SMEM, VMEM],
        out_specs=(VMEM,) * 4,
        compiler_params=params(),
        name="near",
    )(place, rows)


def pack_kernel(gate_ref, up_ref, down_ref, _, out_ref):
    features, width = gate_ref.shape
    out_ref[:features, :] = gate_ref[...]
    out_ref[features : 2 * features, :] = up_ref[...]
    for i in range(features // width):
        at = 2 * features + i * width
        out_ref[at : at + width, :] = down_ref[:, i * width : (i + 1) * width]


def make_pack(gate, up, down, before):
    features, width = gate.shape
    return pl.pallas_call(
        pack_kernel,
        out_shape=shape(3 * features, width),
        in_specs=[VMEM] * 3 + [ANY],
        out_specs=VMEM,
        compiler_params=params(),
        name="pack",
    )(gate, up, down, before)


def make_rest(place, rows, pick, before):
    features = rows.shape[1] - EXTRA
    return pl.pallas_call(
        rest_kernel,
        out_shape=(
            shape(COLS * SLOTS, features),
            shape(EXPERTS * BOTH, 2 * EXPERTS * LANES),
        ),
        in_specs=[SMEM, VMEM, VMEM, ANY],
        out_specs=(VMEM, VMEM),
        compiler_params=params(),
        name="rest",
    )(place, rows, pick, before)


def make_far(rows, pick, *before):
    return pl.pallas_call(
        far_kernel,
        out_shape=shape(COLS * SLOTS, rows.shape[1] - EXTRA),
        in_specs=[VMEM, VMEM] + [ANY] * len(before),
        out_specs=VMEM,
        compiler_params=params(),
        name="far",
    )(rows, pick, *before)


def run_experts(blocks, own, packed, *before):
    count = len(blocks)

    def body(*refs):
        expert_kernel(count, *refs)

    return pl.pallas_call(
        body,
        out_shape=(shape(*blocks[0].shape),) * count + (shape(8, LANES, jnp.int32),),
        in_specs=[VMEM] * (count + 4) + [ANY] * len(before),
        out_specs=(VMEM,) * (count + 1),
        compiler_params=params(),
        name="experts",
    )(*blocks, *own, packed, *before)


def make_gather(back, blocks, parts, so_far=None, before=()):
    features = blocks[0].shape[1]
    total = back.shape[0]
    last = so_far is not None

    def body(*refs):
        gather_kernel(parts, last, *refs)

    return pl.pallas_call(
        body,
        out_shape=shape(total, features, BF if last else F32),
        in_specs=[VMEM] * (1 + len(blocks) + last) + [ANY] * len(before),
        out_specs=VMEM,
        compiler_params=params(),
        name="gather",
    )(back, *blocks, *([so_far] if last else []), *before)


def make_finish(place, meta, rows, fwd, bwd, before):
    return pl.pallas_call(
        finish_kernel,
        out_shape=(shape(*fwd.shape),) * 2,
        in_specs=[SMEM] + [VMEM] * 4 + [ANY],
        out_specs=(VMEM,) * 2,
        compiler_params=params(),
        name="finish",
    )(place, meta, rows, fwd, bwd, before)


def make_simple(kernel, out, place, *arrays, before=()):
    return pl.pallas_call(
        kernel,
        out_shape=jax.ShapeDtypeStruct(out, BF),
        in_specs=[SMEM] + [VMEM] * len(arrays) + [ANY] * len(before),
        out_specs=VMEM,
        compiler_params=params(),
        name="blocks",
    )(place, *arrays, *before)


def move_pp(block, pairs, sections):
    return lax.ppermute(block, "pp", mirrored(pairs, sections))


def swapped(block, count):
    return lax.ppermute(block, "pp", [(0, count - 1), (count - 1, 0)])


def mirrored(pairs, sections):
    return pairs + [(sections - 1 - i, sections - 1 - j) for i, j in pairs]


def from_other_core(block):
    return lax.ppermute(block, "ep", [(i, i ^ 1) for i in range(lax.axis_size("ep"))])


def inward(held, bit, radix, sections):
    got = []
    for k in range(1, radix):
        pairs = [(i + k * bit, i) for i in range(0, sections // 2, radix * bit)]
        got.append(lax.ppermute(held, "pp", mirrored(pairs, sections)))
    return jnp.concatenate([held] + got, axis=0), got[-1]


def outward(own, place, sections):
    def move(block, *pairs):
        return lax.ppermute(block, "pp", mirrored(list(pairs), sections))

    to4, to6, to2 = [move(own[r : r + 2], (0, r)) for r in (4, 6, 2)]
    pair = jnp.where(place >= 6, to6, jnp.where(place >= 4, to4, to2))
    pair = jnp.where(place < 2, own[:2], pair)
    odd = move(pair[1:], (0, 1), (2, 3), (4, 5), (6, 7))
    return jnp.where((place & 1) == 1, odd[0], pair[0])


def body(
    state_fwd,
    state_bwd,
    enter_fwd,
    enter_bwd,
    norm_gain,
    w_gate,
    w_up,
    w_down,
    route_ids,
    route_gates,
):
    sections = lax.axis_size("pp")
    section = lax.axis_index("pp")
    position = lax.axis_index("ep")
    half = sections // 2
    lower = section < half
    place = jnp.stack([position % 2, position // (2 * COLS), section, lower]).astype(jnp.int32)
    fwd, bwd = state_fwd[0], state_bwd[0]
    features = fwd.shape[1]
    part = features // sections
    ids = route_ids[0, 0].transpose(0, 2, 1)
    gates = route_gates[0, 0].transpose(0, 2, 1)

    sent, meta = make_send(place, fwd, bwd, norm_gain, ids, gates)
    rows = exchange(sent)
    send1, send3, pick, token = make_near(place, rows)
    near, far = hop(send1, 1), hop(send3, 3)
    own = (w_gate[0], w_up[0], w_down[0])
    weights = own, from_other_core(make_pack(*own, pick))
    send0, back = make_rest(place, rows, pick, weights[1])
    done0, token = run_experts([send0], *weights)
    at_start = section == 0
    entering = make_simple(
        enter_kernel, (1, BOTH, part), place, enter_fwd, enter_bwd, before=(weights[1],)
    )
    held, got = inward(entering, 1, 2, sections)
    last = hop(make_far(rows, pick, near, far, got, token), 2)
    done1, done3, token = run_experts([near, far], *weights)
    back1, back3 = hop(done1, -1), hop(done3, -3)
    done2, token = run_experts([last], *weights, token)
    back2 = hop(done2, -2)

    held, _ = inward(held, 2, 2, sections)
    held, got = inward(held, 4, 2, sections)
    begun = make_gather(back, [done0, back1, back3], (0, 1, 3))
    gathered = make_gather(back, [back2], (2,), begun, (got,))
    passed_on = jnp.where(at_start, held[:, ROWS:], held[:, :ROWS])
    got = swapped(passed_on, sections)
    rows = exchange(gathered)
    toward, away = make_finish(place, meta, rows, fwd, bwd, got)
    entered = make_simple(entered_kernel, (ROWS, features), place, held, got)
    inner = move_pp(toward, [(i, i - 1) for i in range(1, half)], sections)
    away_low = lax.ppermute(away, "pp", [(i, i + 1) for i in range(half - 1)])
    other = swapped(toward, sections)
    before = (inner, away_low, entered)
    ends = make_simple(ends_kernel, (half, BOTH, part), place, toward, other, before=before)
    mine = outward(ends, jnp.minimum(section, sections - 1 - section), sections)
    away_up = lax.ppermute(away, "pp", [(i, i - 1) for i in range(half + 1, sections)])
    middle = move_pp(away, [(half - 1, half)], sections)
    inner = jnp.where((section == half - 1) | (section == half), middle, inner)
    outer = jnp.where(lower, away_low, away_up)
    outer = jnp.where(at_start | (section == sections - 1), entered, outer)
    fwd_next = jnp.where(lower, outer, inner)
    bwd_next = jnp.where(lower, inner, outer)
    return (fwd_next[None], bwd_next[None], mine[None, :ROWS], mine[None, ROWS:])


def solution(mesh):
    placed = (
        P("pp", "ep", None),
        P("pp", "ep", None),
        P(None, "ep", "pp"),
        P(None, "ep", "pp"),
        P("pp", None),
        P("pp", None, "ep"),
        P("pp", None, "ep"),
        P("pp", "ep", None),
        P("pp", None, None, "ep", None),
        P("pp", None, None, "ep", None),
    )
    return jax.shard_map(
        body,
        mesh=mesh,
        in_specs=placed,
        out_specs=(
            P("pp", "ep", None),
            P("pp", "ep", None),
            P(None, "ep", "pp"),
            P(None, "ep", "pp"),
        ),
        check_vma=False,
    )
```

```python
import jax
import jax.numpy as jnp
from jax import lax
from jax.experimental import pallas as pl
from jax.experimental.pallas import tpu as pltpu
from jax.sharding import PartitionSpec as P

EPS = 1e-06
BF = jnp.bfloat16
F32 = jnp.float32
EXPERTS = 4
COLS = 4
CAP = 15
ROWS = 24
BOTH = 2 * ROWS
SLOTS = 2 * CAP
EXTRA = 128
WIDE = 1792
CHUNK = 512
PIECE = 896
LANES = 128


def device(y, x, core):
    return (y * COLS + x) * 2 + core


def hop(block, distance):
    route = []
    for y in range(EXPERTS):
        for x in range(COLS):
            for core in range(2):
                along_y = core == 1
                there = ((y + distance) % EXPERTS, x) if along_y else (y, (x + distance) % COLS)
                route.append((device(y, x, core), device(*there, core)))
    return lax.ppermute(block, "ep", route)


def rings(along_y):
    groups = []
    for core in range(2):
        if (core == 0) == along_y:
            groups += [[device(y, x, core) for y in range(EXPERTS)] for x in range(COLS)]
        else:
            groups += [[device(y, x, core) for x in range(COLS)] for y in range(EXPERTS)]
    return groups


def exchange(rows):
    return lax.all_to_all(
        rows, "ep", split_axis=0, concat_axis=0, axis_index_groups=rings(True), tiled=True
    )


def iota(shape, dim):
    return lax.broadcasted_iota(jnp.int32, shape, dim)


def dot(a, b):
    return jnp.dot(a, b, preferred_element_type=F32)


def split_gate(gate):
    high = gate.astype(BF).astype(F32)
    return high, (gate - high).astype(BF).astype(F32)


def send_kernel(place_ref, fwd_ref, bwd_ref, gain_ref, ids_ref, gates_ref, out_ref, meta_ref):
    lanes = iota((BOTH, EXTRA), 1)
    row = iota((BOTH, EXTRA), 0)
    in_fwd = row < ROWS
    own = lanes[:, :ROWS] == row[:, :ROWS] - jnp.where(in_fwd[:, :ROWS], 0, ROWS)

    def column(ref, k):
        both = jnp.where(in_fwd[:, :ROWS], ref[0, k : k + 1, :], ref[1, k : k + 1, :])
        return jnp.sum(jnp.where(own, both, jnp.zeros_like(both)), axis=1, keepdims=True)

    first, second = column(ids_ref, 0), column(ids_ref, 1)
    named = jnp.where((lanes == first) | (lanes == second), 1.0, 0.0)
    r0, r1 = iota((BOTH, BOTH), 0), iota((BOTH, BOTH), 1)
    earlier = jnp.where((r1 < r0) & ((r1 < ROWS) == (r0 < ROWS)), 1.0, 0.0)
    rank = dot(earlier.astype(BF), named.astype(BF))
    offset = jnp.where(in_fwd[:, 0:1], 0, CAP)
    slots = []
    for chosen in (first, second):
        taken = jnp.sum(jnp.where(lanes == chosen, rank, 0.0), axis=1, keepdims=True)
        slots.append(taken.astype(jnp.int32) + offset)
    ahead = [
        jnp.bitwise_and(chosen - place_ref[1] + EXPERTS, EXPERTS - 1) for chosen in (first, second)
    ]
    fields = [ahead[0].astype(F32), slots[0].astype(F32), ahead[1].astype(F32), slots[1].astype(F32)]
    fields += split_gate(column(gates_ref, 0))
    fields += split_gate(column(gates_ref, 1))
    fields += [first.astype(F32), second.astype(F32)]
    meta = jnp.zeros((BOTH, EXTRA), F32)
    for place, field in enumerate(fields):
        meta = jnp.where(lanes == place, field, meta)
    meta_ref[...] = meta

    def as_row(column):
        return jnp.sum(jnp.where(r0 == r1, column, 0), axis=0, keepdims=True)

    target = iota((EXPERTS * BOTH, BOTH), 0)
    source = iota((EXPERTS * BOTH, BOTH), 1)
    routed = (target == as_row(first * BOTH + slots[0])) | (
        target == as_row(second * BOTH + slots[1])
    )
    copied = target == source
    for part in range(1, COLS):
        copied = copied | (target == source + part * BOTH)
    routed_f = jnp.where(routed, 1.0, 0.0)
    copied_f = jnp.where(copied, 1.0, 0.0)
    pick = jnp.where(place_ref[0] == 0, routed_f, copied_f).astype(BF)
    values = jnp.concatenate([fwd_ref[...].astype(F32), bwd_ref[...].astype(F32)], axis=0)
    features = values.shape[1]
    inverse = lax.rsqrt(jnp.mean(values * values, axis=-1, keepdims=True) + EPS)
    normed = (values * inverse * gain_ref[...]).astype(BF)
    for start in range(0, features, CHUNK):
        out_ref[:, start : start + CHUNK] = dot(pick, normed[:, start : start + CHUNK]).astype(BF)
    out_ref[:, features:] = dot(pick, meta.astype(BF)).astype(BF)


def slot_targets(place_ref, rows_ref):
    total = EXPERTS * BOTH
    features = rows_ref.shape[1] - EXTRA
    extra = rows_ref[:, features:].astype(F32)
    row = iota((total, 1), 0)
    part = (
        (row >= BOTH).astype(jnp.int32)
        + (row >= 2 * BOTH).astype(jnp.int32)
        + (row >= 3 * BOTH).astype(jnp.int32)
    )
    place = row - part * BOTH
    on_first = place_ref[0] == 0
    packed = jnp.where(place < SLOTS, part * SLOTS + place, -EXPERTS * LANES)
    found = []
    for k in range(COLS):
        there, high, low = -1, 0.0, 0.0
        if k < 2:
            expert = extra[:, 2 * k : 2 * k + 1].astype(jnp.int32)
            slot = extra[:, 2 * k + 1 : 2 * k + 2].astype(jnp.int32)
            there = expert * LANES + part * SLOTS + slot
            high = extra[:, 4 + 2 * k : 5 + 2 * k]
            low = extra[:, 5 + 2 * k : 6 + 2 * k]
        target = jnp.where(on_first, packed + k * LANES, there)
        found.append((target, jnp.where(on_first, 1.0, high), jnp.where(on_first, 0.0, low)))
    return found


def move(pick_ref, rows_ref, parts, out_refs):
    width = rows_ref.shape[1] - EXTRA
    for start in range(0, width, CHUNK):
        cut = slice(start, start + CHUNK)
        rows = rows_ref[:, cut]
        for part, out_ref in zip(parts, out_refs):
            moved = dot(pick_ref[part * LANES : (part + 1) * LANES, :], rows)
            out_ref[:, cut] = moved[: COLS * SLOTS].astype(BF)


def near_kernel(place_ref, rows_ref, first_ref, third_ref, pick_ref, token_ref):
    token_ref[...] = jnp.zeros_like(token_ref)
    column = iota((EXPERTS * BOTH, EXPERTS * LANES), 1)
    pick = jnp.zeros(column.shape, F32)
    for target, _, _ in slot_targets(place_ref, rows_ref):
        pick = jnp.where(column == target, 1.0, pick)
    pick_ref[...] = pick.T.astype(BF)
    move(pick_ref, rows_ref, (1, 3), (first_ref, third_ref))


def rest_kernel(place_ref, rows_ref, pick_ref, _, own_ref, back_ref):
    column = iota((EXPERTS * BOTH, EXPERTS * LANES), 1)
    high_m = jnp.zeros(column.shape, F32)
    low_m = jnp.zeros(column.shape, F32)
    for target, high, low in slot_targets(place_ref, rows_ref):
        here = column == target
        high_m = jnp.where(here, high, high_m)
        low_m = jnp.where(here, low, low_m)
    back_ref[:, : EXPERTS * LANES] = high_m.astype(BF)
    back_ref[:, EXPERTS * LANES :] = low_m.astype(BF)
    move(pick_ref, rows_ref, (0,), (own_ref,))


def far_kernel(rows_ref, pick_ref, *refs):
    move(pick_ref, rows_ref, (2,), refs[-1:])


def expert_kernel(count, *refs):
    rows_refs = refs[:count]
    gate_ref, up_ref, down_ref, other_ref = refs[count : count + 4]
    out_refs, token_ref = refs[-1 - count : -1], refs[-1]
    token_ref[...] = jnp.zeros_like(token_ref)
    features, width = gate_ref.shape
    hidden = []
    for rows_ref in rows_refs:
        gate, up = 0.0, 0.0
        for start in range(0, features, WIDE):
            cut = slice(start, start + WIDE)
            more = slice(features + start, features + start + WIDE)
            rows = rows_ref[:, cut]
            gate += dot(rows, jnp.concatenate([gate_ref[cut, :], other_ref[cut, :]], axis=1))
            up += dot(rows, jnp.concatenate([up_ref[cut, :], other_ref[more, :]], axis=1))
        hidden.append((gate / (1.0 + jnp.exp(-gate)) * up).astype(BF))
    for start in range(0, features, CHUNK):
        cut = slice(start, start + CHUNK)
        at = [2 * features + start + i * width for i in range(CHUNK // width)]
        other = jnp.concatenate([other_ref[i : i + width, :] for i in at], axis=1)
        down = jnp.concatenate([down_ref[:, cut], other], axis=0)
        for rows, out_ref in zip(hidden, out_refs):
            out_ref[:, cut] = dot(rows, down).astype(BF)


def gather_kernel(parts, last, back_ref, *refs):
    rows_refs, so_far_ref, out_ref = refs[: len(parts)], refs[len(parts)], refs[-1]
    width = rows_refs[0].shape[1]
    used = COLS * SLOTS
    for start in range(0, width, CHUNK):
        cut = slice(start, min(start + CHUNK, width))
        total = so_far_ref[:, cut] if last else 0.0
        for part, ref in zip(parts, rows_refs):
            high = slice(part * LANES, part * LANES + used)
            low = slice((EXPERTS + part) * LANES, (EXPERTS + part) * LANES + used)
            rows = ref[:, cut]
            total += dot(back_ref[:, high], rows) + dot(back_ref[:, low], rows)
        out_ref[:, cut] = total.astype(out_ref.dtype)


def finish_kernel(place_ref, meta_ref, rows_ref, fwd_ref, bwd_ref, _, toward_ref, away_ref, leave_ref):
    meta = meta_ref[...]
    total = EXPERTS * BOTH
    column = iota((BOTH, total), 1)
    row = iota((BOTH, total), 0)
    high = jnp.zeros((BOTH, total), F32)
    low = jnp.zeros((BOTH, total), F32)
    for k in range(2):
        there = (meta[:, 8 + k : 9 + k] * BOTH + meta[:, 2 * k + 1 : 2 * k + 2]).astype(jnp.int32)
        high = jnp.where(column == there, meta[:, 4 + 2 * k : 5 + 2 * k], high)
        low = jnp.where(column == there, meta[:, 5 + 2 * k : 6 + 2 * k], low)
    same = column == row
    for part in range(1, COLS):
        same = same | (column == row + part * BOTH)
    ones = jnp.where(same, 1.0, 0.0)
    on_first = place_ref[0] == 0
    high = jnp.where(on_first, high, ones).astype(BF)
    low = jnp.where(on_first, low, 0.0).astype(BF)
    lower = place_ref[3] == 1
    width = fwd_ref.shape[1]
    half = leave_ref.shape[1]
    for start in range(0, width, PIECE):
        cut = slice(start, start + PIECE)
        rows = rows_ref[:, cut]
        mixture = dot(high, rows) + dot(low, rows)
        forward = (fwd_ref[:, cut].astype(F32) + mixture[:ROWS]).astype(BF)
        backward = (bwd_ref[:, cut].astype(F32) + mixture[ROWS:]).astype(BF)
        toward_ref[:, cut] = jnp.where(lower, backward, forward)
        away_ref[:, cut] = jnp.where(lower, forward, backward)

        @pl.when(lower if start >= half else jnp.logical_not(lower))
        def _():
            at = start % half
            leave_ref[:, at : at + PIECE] = backward if start >= half else forward


def enter_kernel(place_ref, fwd_ref, bwd_ref, _, out_ref):
    out_ref[:, :ROWS, :] = fwd_ref[...]
    out_ref[:, ROWS:, :] = bwd_ref[...]


def ends_kernel(place_ref, own_ref, other_ref, *refs):
    out_ref = refs[-1]
    count, _, part = out_ref.shape
    for r in range(count):
        near, far = [slice(j * part, (j + 1) * part) for j in (r, 2 * count - 1 - r)]
        back = slice((count - 1 - r) * part, (count - r) * part)

        @pl.when(place_ref[2] == 0)
        def _():
            out_ref[r, :ROWS, :] = other_ref[:, near]
            out_ref[r, ROWS:, :] = own_ref[:, near]

        @pl.when(place_ref[2] != 0)
        def _():
            out_ref[r, :ROWS, :] = own_ref[:, far]
            out_ref[r, ROWS:, :] = other_ref[:, back]


def entered_kernel(place_ref, held_ref, got_ref, out_ref):
    count, _, part = held_ref.shape
    at_start = place_ref[2] == 0
    for r in range(count):
        near, far = [slice(j * part, (j + 1) * part) for j in (r, 2 * count - 1 - r)]

        @pl.when(at_start)
        def _():
            out_ref[:, near] = held_ref[r, :ROWS, :]
            out_ref[:, far] = got_ref[r]

        @pl.when(jnp.logical_not(at_start))
        def _():
            out_ref[:, near] = got_ref[r]
            out_ref[:, far] = held_ref[r, ROWS:, :]


SMEM = pl.BlockSpec(memory_space=pltpu.SMEM)


def params(mib=20):
    return pltpu.CompilerParams(vmem_limit_bytes=mib * 1024 * 1024)


VMEM = pl.BlockSpec(memory_space=pltpu.VMEM)
ANY = pl.BlockSpec(memory_space=pl.ANY)


def shape(rows, columns, dtype=BF):
    return jax.ShapeDtypeStruct((rows, columns), dtype)


def make_send(place, fwd, bwd, gain, ids, gates):
    features = fwd.shape[1]
    return pl.pallas_call(
        send_kernel,
        out_shape=(shape(EXPERTS * BOTH, features + EXTRA), shape(BOTH, EXTRA, F32)),
        in_specs=[SMEM] + [VMEM] * 5,
        out_specs=(VMEM, VMEM),
        compiler_params=params(),
        name="normed",
    )(place, fwd, bwd, gain, ids, gates)


def make_near(place, rows):
    features = rows.shape[1] - EXTRA
    total = EXPERTS * BOTH
    return pl.pallas_call(
        near_kernel,
        out_shape=(shape(COLS * SLOTS, features),) * 2
        + (shape(EXPERTS * LANES, total), shape(8, LANES, jnp.int32)),
        in_specs=[SMEM, VMEM],
        out_specs=(VMEM,) * 4,
        compiler_params=params(),
        name="near",
    )(place, rows)


def pack_kernel(gate_ref, up_ref, down_ref, _, out_ref):
    features, width = gate_ref.shape
    out_ref[:features, :] = gate_ref[...]
    out_ref[features : 2 * features, :] = up_ref[...]
    for i in range(features // width):
        at = 2 * features + i * width
        out_ref[at : at + width, :] = down_ref[:, i * width : (i + 1) * width]


def make_pack(gate, up, down, before):
    features, width = gate.shape
    return pl.pallas_call(
        pack_kernel,
        out_shape=shape(3 * features, width),
        in_specs=[VMEM] * 3 + [ANY],
        out_specs=VMEM,
        compiler_params=params(),
        name="pack",
    )(gate, up, down, before)


def make_rest(place, rows, pick, before):
    features = rows.shape[1] - EXTRA
    return pl.pallas_call(
        rest_kernel,
        out_shape=(
            shape(COLS * SLOTS, features),
            shape(EXPERTS * BOTH, 2 * EXPERTS * LANES),
        ),
        in_specs=[SMEM, VMEM, VMEM, ANY],
        out_specs=(VMEM, VMEM),
        compiler_params=params(),
        name="rest",
    )(place, rows, pick, before)


def make_far(rows, pick, *before):
    return pl.pallas_call(
        far_kernel,
        out_shape=shape(COLS * SLOTS, rows.shape[1] - EXTRA),
        in_specs=[VMEM, VMEM] + [ANY] * len(before),
        out_specs=VMEM,
        compiler_params=params(),
        name="far",
    )(rows, pick, *before)


def run_experts(blocks, own, packed, *before):
    count = len(blocks)

    def body(*refs):
        expert_kernel(count, *refs)

    return pl.pallas_call(
        body,
        out_shape=(shape(*blocks[0].shape),) * count + (shape(8, LANES, jnp.int32),),
        in_specs=[VMEM] * (count + 4) + [ANY] * len(before),
        out_specs=(VMEM,) * (count + 1),
        compiler_params=params(),
        name="experts",
    )(*blocks, *own, packed, *before)


def make_gather(back, blocks, parts, so_far=None, before=()):
    features = blocks[0].shape[1]
    total = back.shape[0]
    last = so_far is not None

    def body(*refs):
        gather_kernel(parts, last, *refs)

    return pl.pallas_call(
        body,
        out_shape=shape(total, features, BF if last else F32),
        in_specs=[VMEM] * (1 + len(blocks) + last) + [ANY] * len(before),
        out_specs=VMEM,
        compiler_params=params(),
        name="gather",
    )(back, *blocks, *([so_far] if last else []), *before)


def make_finish(place, meta, rows, fwd, bwd, before):
    return pl.pallas_call(
        finish_kernel,
        out_shape=(shape(*fwd.shape),) * 2 + (shape(fwd.shape[0], fwd.shape[1] // 2),),
        in_specs=[SMEM] + [VMEM] * 4 + [ANY],
        out_specs=(VMEM,) * 3,
        compiler_params=params(),
        name="finish",
    )(place, meta, rows, fwd, bwd, before)


def make_simple(kernel, out, place, *arrays, before=()):
    return pl.pallas_call(
        kernel,
        out_shape=jax.ShapeDtypeStruct(out, BF),
        in_specs=[SMEM] + [VMEM] * len(arrays) + [ANY] * len(before),
        out_specs=VMEM,
        compiler_params=params(),
        name="blocks",
    )(place, *arrays, *before)


def move_pp(block, pairs, sections):
    return lax.ppermute(block, "pp", mirrored(pairs, sections))


def swapped(block, count):
    return lax.ppermute(block, "pp", [(0, count - 1), (count - 1, 0)])


def mirrored(pairs, sections):
    return pairs + [(sections - 1 - i, sections - 1 - j) for i, j in pairs]


def from_other_core(block):
    return lax.ppermute(block, "ep", [(i, i ^ 1) for i in range(lax.axis_size("ep"))])


def inward(held, bit, radix, sections):
    got = []
    for k in range(1, radix):
        pairs = [(i + k * bit, i) for i in range(0, sections // 2, radix * bit)]
        got.append(lax.ppermute(held, "pp", mirrored(pairs, sections)))
    return jnp.concatenate([held] + got, axis=0), got[-1]


def outward(own, place, sections):
    def move(block, *pairs):
        return lax.ppermute(block, "pp", mirrored(list(pairs), sections))

    to4, to6, to2 = [move(own[r : r + 2], (0, r)) for r in (4, 6, 2)]
    pair = jnp.where(place >= 6, to6, jnp.where(place >= 4, to4, to2))
    pair = jnp.where(place < 2, own[:2], pair)
    odd = move(pair[1:], (0, 1), (2, 3), (4, 5), (6, 7))
    return jnp.where((place & 1) == 1, odd[0], pair[0])


def body(
    state_fwd,
    state_bwd,
    enter_fwd,
    enter_bwd,
    norm_gain,
    w_gate,
    w_up,
    w_down,
    route_ids,
    route_gates,
):
    sections = lax.axis_size("pp")
    section = lax.axis_index("pp")
    position = lax.axis_index("ep")
    half = sections // 2
    lower = section < half
    place = jnp.stack([position % 2, position // (2 * COLS), section, lower]).astype(jnp.int32)
    fwd, bwd = state_fwd[0], state_bwd[0]
    features = fwd.shape[1]
    part = features // sections
    ids = route_ids[0, 0].transpose(0, 2, 1)
    gates = route_gates[0, 0].transpose(0, 2, 1)

    sent, meta = make_send(place, fwd, bwd, norm_gain, ids, gates)
    rows = exchange(sent)
    send1, send3, pick, token = make_near(place, rows)
    near, far = hop(send1, 1), hop(send3, 3)
    own = (w_gate[0], w_up[0], w_down[0])
    weights = own, from_other_core(make_pack(*own, pick))
    send0, back = make_rest(place, rows, pick, weights[1])
    done0, token = run_experts([send0], *weights)
    at_start = section == 0
    entering = make_simple(
        enter_kernel, (1, BOTH, part), place, enter_fwd, enter_bwd, before=(weights[1],)
    )
    held, got = inward(entering, 1, 2, sections)
    last = hop(make_far(rows, pick, near, far, got, token), 2)
    done1, done3, token = run_experts([near, far], *weights)
    back1, back3 = hop(done1, -1), hop(done3, -3)
    done2, token = run_experts([last], *weights, token)
    back2 = hop(done2, -2)

    held, _ = inward(held, 2, 2, sections)
    held, got = inward(held, 4, 2, sections)
    begun = make_gather(back, [done0, back1, back3], (0, 1, 3))
    gathered = make_gather(back, [back2], (2,), begun, (got,))
    passed_on = jnp.where(at_start, held[:, ROWS:], held[:, :ROWS])
    got = swapped(passed_on, sections)
    rows = exchange(gathered)
    toward, away, leaving = make_finish(place, meta, rows, fwd, bwd, got)
    entered = make_simple(entered_kernel, (ROWS, features), place, held, got)
    inner = move_pp(toward, [(i, i - 1) for i in range(1, half)], sections)
    other = swapped(leaving, sections)
    ends = make_simple(ends_kernel, (half, BOTH, part), place, toward, other, before=(inner, entered))
    mine = outward(ends, jnp.minimum(section, sections - 1 - section), sections)
    outer = move_pp(away, [(i, i + 1) for i in range(half - 1)], sections)
    middle = move_pp(away, [(half - 1, half)], sections)
    inner = jnp.where((section == half - 1) | (section == half), middle, inner)
    outer = jnp.where(at_start | (section == sections - 1), entered, outer)
    fwd_next = jnp.where(lower, outer, inner)
    bwd_next = jnp.where(lower, inner, outer)
    return (fwd_next[None], bwd_next[None], mine[None, :ROWS], mine[None, ROWS:])


def solution(mesh):
    placed = (
        P("pp", "ep", None),
        P("pp", "ep", None),
        P(None, "ep", "pp"),
        P(None, "ep", "pp"),
        P("pp", None),
        P("pp", None, "ep"),
        P("pp", None, "ep"),
        P("pp", "ep", None),
        P("pp", None, None, "ep", None),
        P("pp", None, None, "ep", None),
    )
    return jax.shard_map(
        body,
        mesh=mesh,
        in_specs=placed,
        out_specs=(
            P("pp", "ep", None),
            P("pp", "ep", None),
            P(None, "ep", "pp"),
            P(None, "ep", "pp"),
        ),
        check_vma=False,
    )
```

```python
import jax
import jax.numpy as jnp
from jax import lax
from jax.experimental import pallas as pl
from jax.experimental.pallas import tpu as pltpu
from jax.sharding import PartitionSpec as P

EPS = 1e-06
BF = jnp.bfloat16
F32 = jnp.float32
EXPERTS = 4
COLS = 4
CAP = 15
ROWS = 24
BOTH = 2 * ROWS
SLOTS = 2 * CAP
EXTRA = 128
WIDE = 1792
CHUNK = 512
PIECE = 896
LANES = 128


def device(y, x, core):
    return (y * COLS + x) * 2 + core


def hop(block, distance):
    route = []
    for y in range(EXPERTS):
        for x in range(COLS):
            for core in range(2):
                along_y = core == 1
                there = ((y + distance) % EXPERTS, x) if along_y else (y, (x + distance) % COLS)
                route.append((device(y, x, core), device(*there, core)))
    return lax.ppermute(block, "ep", route)


def rings(along_y):
    groups = []
    for core in range(2):
        if (core == 0) == along_y:
            groups += [[device(y, x, core) for y in range(EXPERTS)] for x in range(COLS)]
        else:
            groups += [[device(y, x, core) for x in range(COLS)] for y in range(EXPERTS)]
    return groups


def exchange(rows):
    return lax.all_to_all(
        rows, "ep", split_axis=0, concat_axis=0, axis_index_groups=rings(True), tiled=True
    )


def iota(shape, dim):
    return lax.broadcasted_iota(jnp.int32, shape, dim)


def dot(a, b):
    return jnp.dot(a, b, preferred_element_type=F32)


def split_gate(gate):
    high = gate.astype(BF).astype(F32)
    return high, (gate - high).astype(BF).astype(F32)


def send_kernel(place_ref, fwd_ref, bwd_ref, gain_ref, ids_ref, gates_ref, out_ref, meta_ref):
    lanes = iota((BOTH, EXTRA), 1)
    row = iota((BOTH, EXTRA), 0)
    in_fwd = row < ROWS
    own = lanes[:, :ROWS] == row[:, :ROWS] - jnp.where(in_fwd[:, :ROWS], 0, ROWS)

    def column(ref, k):
        both = jnp.where(in_fwd[:, :ROWS], ref[0, k : k + 1, :], ref[1, k : k + 1, :])
        return jnp.sum(jnp.where(own, both, jnp.zeros_like(both)), axis=1, keepdims=True)

    first, second = column(ids_ref, 0), column(ids_ref, 1)
    named = jnp.where((lanes == first) | (lanes == second), 1.0, 0.0)
    r0, r1 = iota((BOTH, BOTH), 0), iota((BOTH, BOTH), 1)
    earlier = jnp.where((r1 < r0) & ((r1 < ROWS) == (r0 < ROWS)), 1.0, 0.0)
    rank = dot(earlier.astype(BF), named.astype(BF))
    offset = jnp.where(in_fwd[:, 0:1], 0, CAP)
    slots = []
    for chosen in (first, second):
        taken = jnp.sum(jnp.where(lanes == chosen, rank, 0.0), axis=1, keepdims=True)
        slots.append(taken.astype(jnp.int32) + offset)
    ahead = [
        jnp.bitwise_and(chosen - place_ref[1] + EXPERTS, EXPERTS - 1) for chosen in (first, second)
    ]
    fields = [ahead[0].astype(F32), slots[0].astype(F32), ahead[1].astype(F32), slots[1].astype(F32)]
    fields += split_gate(column(gates_ref, 0))
    fields += split_gate(column(gates_ref, 1))
    fields += [first.astype(F32), second.astype(F32)]
    meta = jnp.zeros((BOTH, EXTRA), F32)
    for place, field in enumerate(fields):
        meta = jnp.where(lanes == place, field, meta)
    meta_ref[...] = meta

    def as_row(column):
        return jnp.sum(jnp.where(r0 == r1, column, 0), axis=0, keepdims=True)

    target = iota((EXPERTS * BOTH, BOTH), 0)
    source = iota((EXPERTS * BOTH, BOTH), 1)
    routed = (target == as_row(first * BOTH + slots[0])) | (
        target == as_row(second * BOTH + slots[1])
    )
    copied = target == source
    for part in range(1, COLS):
        copied = copied | (target == source + part * BOTH)
    routed_f = jnp.where(routed, 1.0, 0.0)
    copied_f = jnp.where(copied, 1.0, 0.0)
    pick = jnp.where(place_ref[0] == 0, routed_f, copied_f).astype(BF)
    values = jnp.concatenate([fwd_ref[...].astype(F32), bwd_ref[...].astype(F32)], axis=0)
    features = values.shape[1]
    inverse = lax.rsqrt(jnp.mean(values * values, axis=-1, keepdims=True) + EPS)
    normed = (values * inverse * gain_ref[...]).astype(BF)
    for start in range(0, features, CHUNK):
        out_ref[:, start : start + CHUNK] = dot(pick, normed[:, start : start + CHUNK]).astype(BF)
    out_ref[:, features:] = dot(pick, meta.astype(BF)).astype(BF)


def slot_targets(place_ref, rows_ref):
    total = EXPERTS * BOTH
    features = rows_ref.shape[1] - EXTRA
    extra = rows_ref[:, features:].astype(F32)
    row = iota((total, 1), 0)
    part = (
        (row >= BOTH).astype(jnp.int32)
        + (row >= 2 * BOTH).astype(jnp.int32)
        + (row >= 3 * BOTH).astype(jnp.int32)
    )
    place = row - part * BOTH
    on_first = place_ref[0] == 0
    packed = jnp.where(place < SLOTS, part * SLOTS + place, -EXPERTS * LANES)
    found = []
    for k in range(COLS):
        there, high, low = -1, 0.0, 0.0
        if k < 2:
            expert = extra[:, 2 * k : 2 * k + 1].astype(jnp.int32)
            slot = extra[:, 2 * k + 1 : 2 * k + 2].astype(jnp.int32)
            there = expert * LANES + part * SLOTS + slot
            high = extra[:, 4 + 2 * k : 5 + 2 * k]
            low = extra[:, 5 + 2 * k : 6 + 2 * k]
        target = jnp.where(on_first, packed + k * LANES, there)
        found.append((target, jnp.where(on_first, 1.0, high), jnp.where(on_first, 0.0, low)))
    return found


def move(pick_ref, rows_ref, parts, out_refs):
    width = rows_ref.shape[1] - EXTRA
    for start in range(0, width, CHUNK):
        cut = slice(start, start + CHUNK)
        rows = rows_ref[:, cut]
        for part, out_ref in zip(parts, out_refs):
            moved = dot(pick_ref[part * LANES : (part + 1) * LANES, :], rows)
            out_ref[:, cut] = moved[: COLS * SLOTS].astype(BF)


def near_kernel(place_ref, rows_ref, first_ref, third_ref, pick_ref, token_ref):
    token_ref[...] = jnp.zeros_like(token_ref)
    column = iota((EXPERTS * BOTH, EXPERTS * LANES), 1)
    pick = jnp.zeros(column.shape, F32)
    for target, _, _ in slot_targets(place_ref, rows_ref):
        pick = jnp.where(column == target, 1.0, pick)
    pick_ref[...] = pick.T.astype(BF)
    move(pick_ref, rows_ref, (1, 3), (first_ref, third_ref))


def rest_kernel(place_ref, rows_ref, pick_ref, _, own_ref, back_ref):
    column = iota((EXPERTS * BOTH, EXPERTS * LANES), 1)
    high_m = jnp.zeros(column.shape, F32)
    low_m = jnp.zeros(column.shape, F32)
    for target, high, low in slot_targets(place_ref, rows_ref):
        here = column == target
        high_m = jnp.where(here, high, high_m)
        low_m = jnp.where(here, low, low_m)
    back_ref[:, : EXPERTS * LANES] = high_m.astype(BF)
    back_ref[:, EXPERTS * LANES :] = low_m.astype(BF)
    move(pick_ref, rows_ref, (0,), (own_ref,))


def far_kernel(rows_ref, pick_ref, *refs):
    move(pick_ref, rows_ref, (2,), refs[-1:])


def expert_kernel(count, *refs):
    rows_refs = refs[:count]
    gate_ref, up_ref, down_ref, other_ref = refs[count : count + 4]
    out_refs, token_ref = refs[-1 - count : -1], refs[-1]
    token_ref[...] = jnp.zeros_like(token_ref)
    features, width = gate_ref.shape
    hidden = []
    for rows_ref in rows_refs:
        gate, up = 0.0, 0.0
        for start in range(0, features, WIDE):
            cut = slice(start, start + WIDE)
            more = slice(features + start, features + start + WIDE)
            rows = rows_ref[:, cut]
            gate += dot(rows, jnp.concatenate([gate_ref[cut, :], other_ref[cut, :]], axis=1))
            up += dot(rows, jnp.concatenate([up_ref[cut, :], other_ref[more, :]], axis=1))
        hidden.append((gate / (1.0 + jnp.exp(-gate)) * up).astype(BF))
    for start in range(0, features, CHUNK):
        cut = slice(start, start + CHUNK)
        at = [2 * features + start + i * width for i in range(CHUNK // width)]
        other = jnp.concatenate([other_ref[i : i + width, :] for i in at], axis=1)
        down = jnp.concatenate([down_ref[:, cut], other], axis=0)
        for rows, out_ref in zip(hidden, out_refs):
            out_ref[:, cut] = dot(rows, down).astype(BF)


def gather_kernel(parts, last, back_ref, *refs):
    rows_refs, so_far_ref, out_ref = refs[: len(parts)], refs[len(parts)], refs[-1]
    width = rows_refs[0].shape[1]
    used = COLS * SLOTS
    for start in range(0, width, CHUNK):
        cut = slice(start, min(start + CHUNK, width))
        total = so_far_ref[:, cut] if last else 0.0
        for part, ref in zip(parts, rows_refs):
            high = slice(part * LANES, part * LANES + used)
            low = slice((EXPERTS + part) * LANES, (EXPERTS + part) * LANES + used)
            rows = ref[:, cut]
            total += dot(back_ref[:, high], rows) + dot(back_ref[:, low], rows)
        out_ref[:, cut] = total.astype(out_ref.dtype)


def finish_kernel(place_ref, meta_ref, rows_ref, fwd_ref, bwd_ref, _, toward_ref, away_ref, leave_ref):
    meta = meta_ref[...]
    total = EXPERTS * BOTH
    column = iota((BOTH, total), 1)
    row = iota((BOTH, total), 0)
    high = jnp.zeros((BOTH, total), F32)
    low = jnp.zeros((BOTH, total), F32)
    for k in range(2):
        there = (meta[:, 8 + k : 9 + k] * BOTH + meta[:, 2 * k + 1 : 2 * k + 2]).astype(jnp.int32)
        high = jnp.where(column == there, meta[:, 4 + 2 * k : 5 + 2 * k], high)
        low = jnp.where(column == there, meta[:, 5 + 2 * k : 6 + 2 * k], low)
    same = column == row
    for part in range(1, COLS):
        same = same | (column == row + part * BOTH)
    ones = jnp.where(same, 1.0, 0.0)
    on_first = place_ref[0] == 0
    high = jnp.where(on_first, high, ones).astype(BF)
    low = jnp.where(on_first, low, 0.0).astype(BF)
    lower = place_ref[3] == 1
    width = fwd_ref.shape[1]
    half = leave_ref.shape[1]
    for start in range(0, width, PIECE):
        cut = slice(start, start + PIECE)
        rows = rows_ref[:, cut]
        mixture = dot(high, rows) + dot(low, rows)
        forward = (fwd_ref[:, cut].astype(F32) + mixture[:ROWS]).astype(BF)
        backward = (bwd_ref[:, cut].astype(F32) + mixture[ROWS:]).astype(BF)
        toward_ref[:, cut] = jnp.where(lower, backward, forward)
        away_ref[:, cut] = jnp.where(lower, forward, backward)

        @pl.when(lower if start >= half else jnp.logical_not(lower))
        def _():
            at = start % half
            leave_ref[:, at : at + PIECE] = backward if start >= half else forward


def enter_kernel(place_ref, fwd_ref, bwd_ref, _, out_ref):
    out_ref[:, :ROWS, :] = fwd_ref[...]
    out_ref[:, ROWS:, :] = bwd_ref[...]


def ends_kernel(place_ref, own_ref, other_ref, *refs):
    out_ref = refs[-1]
    count, _, part = out_ref.shape
    for r in range(count):
        near, far = [slice(j * part, (j + 1) * part) for j in (r, 2 * count - 1 - r)]
        back = slice((count - 1 - r) * part, (count - r) * part)

        @pl.when(place_ref[2] == 0)
        def _():
            out_ref[r, :ROWS, :] = other_ref[:, near]
            out_ref[r, ROWS:, :] = own_ref[:, near]

        @pl.when(place_ref[2] != 0)
        def _():
            out_ref[r, :ROWS, :] = own_ref[:, far]
            out_ref[r, ROWS:, :] = other_ref[:, back]


def entered_kernel(place_ref, held_ref, got_ref, out_ref):
    count, _, part = held_ref.shape
    at_start = place_ref[2] == 0
    for r in range(count):
        near, far = [slice(j * part, (j + 1) * part) for j in (r, 2 * count - 1 - r)]

        @pl.when(at_start)
        def _():
            out_ref[:, near] = held_ref[r, :ROWS, :]
            out_ref[:, far] = got_ref[r]

        @pl.when(jnp.logical_not(at_start))
        def _():
            out_ref[:, near] = got_ref[r]
            out_ref[:, far] = held_ref[r, ROWS:, :]


SMEM = pl.BlockSpec(memory_space=pltpu.SMEM)


def params(mib=20):
    return pltpu.CompilerParams(vmem_limit_bytes=mib * 1024 * 1024)


VMEM = pl.BlockSpec(memory_space=pltpu.VMEM)
ANY = pl.BlockSpec(memory_space=pl.ANY)


def shape(rows, columns, dtype=BF):
    return jax.ShapeDtypeStruct((rows, columns), dtype)


def make_send(place, fwd, bwd, gain, ids, gates):
    features = fwd.shape[1]
    return pl.pallas_call(
        send_kernel,
        out_shape=(shape(EXPERTS * BOTH, features + EXTRA), shape(BOTH, EXTRA, F32)),
        in_specs=[SMEM] + [VMEM] * 5,
        out_specs=(VMEM, VMEM),
        compiler_params=params(),
        name="normed",
    )(place, fwd, bwd, gain, ids, gates)


def make_near(place, rows):
    features = rows.shape[1] - EXTRA
    total = EXPERTS * BOTH
    return pl.pallas_call(
        near_kernel,
        out_shape=(shape(COLS * SLOTS, features),) * 2
        + (shape(EXPERTS * LANES, total), shape(8, LANES, jnp.int32)),
        in_specs=[SMEM, VMEM],
        out_specs=(VMEM,) * 4,
        compiler_params=params(),
        name="near",
    )(place, rows)


def pack_kernel(gate_ref, up_ref, down_ref, _, out_ref):
    features, width = gate_ref.shape
    out_ref[:features, :] = gate_ref[...]
    out_ref[features : 2 * features, :] = up_ref[...]
    for i in range(features // width):
        at = 2 * features + i * width
        out_ref[at : at + width, :] = down_ref[:, i * width : (i + 1) * width]


def make_pack(gate, up, down, before):
    features, width = gate.shape
    return pl.pallas_call(
        pack_kernel,
        out_shape=shape(3 * features, width),
        in_specs=[VMEM] * 3 + [ANY],
        out_specs=VMEM,
        compiler_params=params(),
        name="pack",
    )(gate, up, down, before)


def make_rest(place, rows, pick, before):
    features = rows.shape[1] - EXTRA
    return pl.pallas_call(
        rest_kernel,
        out_shape=(
            shape(COLS * SLOTS, features),
            shape(EXPERTS * BOTH, 2 * EXPERTS * LANES),
        ),
        in_specs=[SMEM, VMEM, VMEM, ANY],
        out_specs=(VMEM, VMEM),
        compiler_params=params(),
        name="rest",
    )(place, rows, pick, before)


def make_far(rows, pick, *before):
    return pl.pallas_call(
        far_kernel,
        out_shape=shape(COLS * SLOTS, rows.shape[1] - EXTRA),
        in_specs=[VMEM, VMEM] + [ANY] * len(before),
        out_specs=VMEM,
        compiler_params=params(),
        name="far",
    )(rows, pick, *before)


def run_experts(blocks, own, packed, *before):
    count = len(blocks)

    def body(*refs):
        expert_kernel(count, *refs)

    return pl.pallas_call(
        body,
        out_shape=(shape(*blocks[0].shape),) * count + (shape(8, LANES, jnp.int32),),
        in_specs=[VMEM] * (count + 4) + [ANY] * len(before),
        out_specs=(VMEM,) * (count + 1),
        compiler_params=params(),
        name="experts",
    )(*blocks, *own, packed, *before)


def make_gather(back, blocks, parts, so_far=None, before=()):
    features = blocks[0].shape[1]
    total = back.shape[0]
    last = so_far is not None

    def body(*refs):
        gather_kernel(parts, last, *refs)

    return pl.pallas_call(
        body,
        out_shape=shape(total, features, BF if last else F32),
        in_specs=[VMEM] * (1 + len(blocks) + last) + [ANY] * len(before),
        out_specs=VMEM,
        compiler_params=params(),
        name="gather",
    )(back, *blocks, *([so_far] if last else []), *before)


def make_finish(place, meta, rows, fwd, bwd, before):
    return pl.pallas_call(
        finish_kernel,
        out_shape=(shape(*fwd.shape),) * 2 + (shape(fwd.shape[0], fwd.shape[1] // 2),),
        in_specs=[SMEM] + [VMEM] * 4 + [ANY],
        out_specs=(VMEM,) * 3,
        compiler_params=params(),
        name="finish",
    )(place, meta, rows, fwd, bwd, before)


def make_simple(kernel, out, place, *arrays, before=()):
    return pl.pallas_call(
        kernel,
        out_shape=jax.ShapeDtypeStruct(out, BF),
        in_specs=[SMEM] + [VMEM] * len(arrays) + [ANY] * len(before),
        out_specs=VMEM,
        compiler_params=params(),
        name="blocks",
    )(place, *arrays, *before)


def move_pp(block, pairs, sections):
    return lax.ppermute(block, "pp", mirrored(pairs, sections))


def swapped(block, count):
    return lax.ppermute(block, "pp", [(0, count - 1), (count - 1, 0)])


def mirrored(pairs, sections):
    return pairs + [(sections - 1 - i, sections - 1 - j) for i, j in pairs]


def from_other_core(block):
    return lax.ppermute(block, "ep", [(i, i ^ 1) for i in range(lax.axis_size("ep"))])


def inward(held, bit, radix, sections):
    got = []
    for k in range(1, radix):
        pairs = [(i + k * bit, i) for i in range(0, sections // 2, radix * bit)]
        got.append(lax.ppermute(held, "pp", mirrored(pairs, sections)))
    return jnp.concatenate([held] + got, axis=0), got[-1]


def outward(own, place, sections):
    def move(block, *pairs):
        return lax.ppermute(block, "pp", mirrored(list(pairs), sections))

    to4, to6, to2 = [move(own[r : r + 2], (0, r)) for r in (4, 6, 2)]
    pair = jnp.where(place >= 6, to6, jnp.where(place >= 4, to4, to2))
    pair = jnp.where(place < 2, own[:2], pair)
    odd = move(pair[1:], (0, 1), (2, 3), (4, 5), (6, 7))
    return jnp.where((place & 1) == 1, odd[0], pair[0])


def body(
    state_fwd,
    state_bwd,
    enter_fwd,
    enter_bwd,
    norm_gain,
    w_gate,
    w_up,
    w_down,
    route_ids,
    route_gates,
):
    sections = lax.axis_size("pp")
    section = lax.axis_index("pp")
    position = lax.axis_index("ep")
    half = sections // 2
    lower = section < half
    place = jnp.stack([position % 2, position // (2 * COLS), section, lower]).astype(jnp.int32)
    fwd, bwd = state_fwd[0], state_bwd[0]
    features = fwd.shape[1]
    part = features // sections
    ids = route_ids[0, 0].transpose(0, 2, 1)
    gates = route_gates[0, 0].transpose(0, 2, 1)

    sent, meta = make_send(place, fwd, bwd, norm_gain, ids, gates)
    rows = exchange(sent)
    send1, send3, pick, token = make_near(place, rows)
    near, far = hop(send1, 1), hop(send3, 3)
    own = (w_gate[0], w_up[0], w_down[0])
    weights = own, from_other_core(make_pack(*own, pick))
    send0, back = make_rest(place, rows, pick, weights[1])
    done0, token = run_experts([send0], *weights)
    at_start = section == 0
    entering = make_simple(
        enter_kernel, (1, BOTH, part), place, enter_fwd, enter_bwd, before=(weights[1],)
    )
    held, got = inward(entering, 1, 2, sections)
    last = hop(make_far(rows, pick, near, got, token), 2)
    done1, done3, token = run_experts([near, far], *weights)
    back1, back3 = hop(done1, -1), hop(done3, -3)
    done2, token = run_experts([last], *weights, token)
    back2 = hop(done2, -2)

    held, _ = inward(held, 2, 2, sections)
    held, got = inward(held, 4, 2, sections)
    begun = make_gather(back, [done0, back1, back3], (0, 1, 3))
    gathered = make_gather(back, [back2], (2,), begun, (got,))
    passed_on = jnp.where(at_start, held[:, ROWS:], held[:, :ROWS])
    got = swapped(passed_on, sections)
    rows = exchange(gathered)
    toward, away, leaving = make_finish(place, meta, rows, fwd, bwd, got)
    entered = make_simple(entered_kernel, (ROWS, features), place, held, got)
    inner = move_pp(toward, [(i, i - 1) for i in range(1, half)], sections)
    other = swapped(leaving, sections)
    ends = make_simple(ends_kernel, (half, BOTH, part), place, toward, other, before=(inner, entered))
    mine = outward(ends, jnp.minimum(section, sections - 1 - section), sections)
    outer = move_pp(away, [(i, i + 1) for i in range(half - 1)], sections)
    middle = move_pp(away, [(half - 1, half)], sections)
    inner = jnp.where((section == half - 1) | (section == half), middle, inner)
    outer = jnp.where(at_start | (section == sections - 1), entered, outer)
    fwd_next = jnp.where(lower, outer, inner)
    bwd_next = jnp.where(lower, inner, outer)
    return (fwd_next[None], bwd_next[None], mine[None, :ROWS], mine[None, ROWS:])


def solution(mesh):
    placed = (
        P("pp", "ep", None),
        P("pp", "ep", None),
        P(None, "ep", "pp"),
        P(None, "ep", "pp"),
        P("pp", None),
        P("pp", None, "ep"),
        P("pp", None, "ep"),
        P("pp", "ep", None),
        P("pp", None, None, "ep", None),
        P("pp", None, None, "ep", None),
    )
    return jax.shard_map(
        body,
        mesh=mesh,
        in_specs=placed,
        out_specs=(
            P("pp", "ep", None),
            P("pp", "ep", None),
            P(None, "ep", "pp"),
            P(None, "ep", "pp"),
        ),
        check_vma=False,
    )
```
